32 devices in a mesh: seq: 8 (over y, x, core), head: 4 (over z).
Axes of the slice: x: 2, y: 2, z: 4, core: 2. Of those that a mesh axis runs over, the one named last changes fastest.
Arguments:
- inputs: bfloat16 [32768, 512], P(('seq', 'head')), may hold values from -6 to 6
- attn_gain: bfloat16 [512], P(('seq', 'head')), may hold values from 0.099609375 to 1.8984375
- attn_shift: bfloat16 [512], P(('seq', 'head')), may hold values from -3 to 3
- query_weight: bfloat16 [512, 512], P(None, 'head'), may hold values from -1 to 1
- key_weight: bfloat16 [512, 512], P(None, 'head'), may hold values from -0.25 to 0.25
- value_weight: bfloat16 [512, 512], P(None, 'head'), may hold values from -0.25 to 0.25
- control_weight: bfloat16 [512, 512], P(None, 'head'), may hold values from -0.5 to 0.5
- output_weight: bfloat16 [512, 512], P('head'), may hold values from -1 to 1
- ffn_gain: bfloat16 [512], P(('seq', 'head')), may hold values from 0.099609375 to 1.8984375
- ffn_shift: bfloat16 [512], P(('seq', 'head')), may hold values from -3 to 3
- expand_weight: bfloat16 [512, 2048], P(None, ('seq', 'head')), may hold values from -0.25 to 0.25
- expand_bias: bfloat16 [2048], P(('seq', 'head')), may hold values from -3 to 3
- shrink_weight: bfloat16 [2048, 512], P(None, ('seq', 'head')), may hold values from -0.125 to 0.125
- shrink_bias: bfloat16 [512], P(('seq', 'head')), may hold values from -3 to 3
- cotangent: bfloat16 [32768, 512], P(('seq', 'head')), may hold values from -6 to 6
Outputs:
- result: bfloat16 [32768, 512], P(('seq', 'head'))
- grad_inputs: bfloat16 [32768, 512], P(('seq', 'head'))
- grad_attn_gain: float32 [512], P(('seq', 'head'))
- grad_attn_shift: float32 [512], P(('seq', 'head'))
- grad_query_weight: float32 [512, 512], P('seq', 'head')
- grad_key_weight: float32 [512, 512], P('seq', 'head')
- grad_value_weight: float32 [512, 512], P('seq', 'head')
- grad_control_weight: float32 [512, 512], P('seq', 'head')
- grad_output_weight: float32 [512, 512], P('head', 'seq')
- grad_ffn_gain: float32 [512], P(('seq', 'head'))
- grad_ffn_shift: float32 [512], P(('seq', 'head'))
- grad_expand_weight: float32 [512, 2048], P(None, ('seq', 'head'))
- grad_expand_bias: float32 [2048], P(('seq', 'head'))
- grad_shrink_weight: float32 [2048, 512], P(None, ('seq', 'head'))
- grad_shrink_bias: float32 [512], P(('seq', 'head'))
The draws below stay inside these ranges and needn't reach their ends.
All inputs are finite; a program needn't handle non-finite values.
Results may differ from the reference program's by a relative error of at most 0.025.
The reference program's roundings to bfloat16 on the way count: a program that leaves them out, or rounds other values in their place, can miss the bound.
Values may be sent and summed in bfloat16 or wider, within the bound.
No kernel may reach another device: no remote copies, remote signals or barrier semaphores. Data moves between devices by JAX's collectives and lax.ppermute only.
A program may use at most 128 MiB of HBM per device.

```python
import jax
import jax.numpy as jnp
from jax import lax

D = 512
H = 8
SLOTS = 64
FF = 2048
LEN = 1024
NSEQ = 32
TOKENS = 32768


def spiked(array, key, source, target, shards_of, factor):
    owner, partner = [(jnp.arange(array.shape[axis_at]) // (array.shape[axis_at] // shards_of)).reshape([-1 if axis == axis_at else 1 for axis in range(array.ndim)]) for axis_at in (source, target)]
    chosen = jax.random.permutation(key, shards_of)[partner]
    strong = (owner == chosen) | (owner == (partner + shards_of // 2) % shards_of)
    return jnp.where(strong, factor * array, array)


def block_levels(key, extent, cuts, low, high):
    level = 1.0
    for dim, blocks in cuts:
        heights = jax.random.uniform(jax.random.fold_in(jax.random.fold_in(key, 6), dim), (blocks,), jnp.float32, low / len(cuts), high / len(cuts))
        level = level * jnp.repeat(jnp.exp(heights), extent[dim] // blocks).reshape((-1,) + (1,) * (len(extent) - 1 - dim))
    return level


def gaussian(own_key, dims, deviation, limit, pieces=(), dtype=jnp.bfloat16):
    entries = deviation * jax.random.normal(own_key, dims, jnp.float32)
    if pieces:
        entries = entries * block_levels(own_key, dims, pieces, -0.22, 0.18)
    return jnp.clip(entries, -limit, limit).astype(dtype)


def bell_draw_with(stream_key, shape, scale, limit, split, heavy, dtype=jnp.bfloat16):
    values = scale * jax.random.normal(stream_key, shape, jnp.float32)
    if split:
        values = values * block_levels(stream_key, shape, split, -0.22, 0.18)
    return jnp.clip(spiked(values, jax.random.fold_in(stream_key, 3), *heavy), -limit, limit).astype(dtype)


def setup_inputs(seed: int = 0) -> dict:
    keys = jax.random.split(jax.random.key(seed), 16)
    return {
        "inputs": gaussian(keys[0], (TOKENS, D), 1.0, 6.0, ((0, 32),)),
        "attn_gain": jnp.clip(1.0 + 0.18 * jax.random.normal(keys[1], (D,), jnp.float32), 0.099609375, 1.8984375).astype(jnp.bfloat16),
        "attn_shift": gaussian(keys[2], (D,), 0.5, 3.0, ((0, 32),)),
        "query_weight": gaussian(keys[3], (D, D), (D // 16) ** -0.5, 1.0, ((1, 4),)),
        "key_weight": gaussian(keys[4], (D, D), D ** -0.5, 0.25, ((1, 4),)),
        "value_weight": gaussian(keys[5], (D, D), D ** -0.5, 0.25, ((1, 4),)),
        "control_weight": gaussian(keys[6], (D, H * SLOTS), (D // 4) ** -0.5, 0.5, ((1, 4),)),
        "output_weight": gaussian(keys[7], (D, D), (D // 16) ** -0.5, 1.0, ((0, 4),)),
        "ffn_gain": jnp.clip(1.0 + 0.18 * jax.random.normal(keys[8], (D,), jnp.float32), 0.099609375, 1.8984375).astype(jnp.bfloat16),
        "ffn_shift": gaussian(keys[9], (D,), 0.5, 3.0, ((0, 32),)),
        "expand_weight": gaussian(keys[10], (D, FF), D ** -0.5, 0.25, ((1, 32),)),
        "expand_bias": gaussian(keys[11], (FF,), 0.5, 3.0, ((0, 32),)),
        "shrink_weight": gaussian(keys[12], (FF, D), FF ** -0.5, 0.125, ((1, 32),)),
        "shrink_bias": gaussian(keys[13], (D,), 0.5, 3.0, ((0, 32),)),
        "cotangent": bell_draw_with(keys[14], (TOKENS, D), 1.0, 6.0, ((0, 32),), (0, 1, 32, 2.75)),
    }


@jax.custom_vjp
def low(v):
    return lax.optimization_barrier(v.astype(jnp.bfloat16)).astype(jnp.float32)

@jax.custom_vjp
def low_back(v):
    return v

def low_keep(v):
    return (low(v), None)

def low_pass(kept, grad):
    return (grad,)

def back_keep(v):
    return (v, None)

def back_low(kept, grad):
    return (low(grad),)
low.defvjp(low_keep, low_pass)
low_back.defvjp(back_keep, back_low)
EPSILON = 1e-05
precise = lax.Precision.HIGHEST

def layer_norm(tokens, scaling, offset):
    average = lax.optimization_barrier(jnp.mean(tokens, axis=-1, keepdims=True))
    centred = tokens - average
    spread = lax.optimization_barrier(jnp.mean(centred * centred, axis=-1, keepdims=True))
    return centred * lax.rsqrt(spread + EPSILON) * scaling + offset

def attend(queries, key_rows, value_rows, control):
    places = jnp.arange(LEN)
    causal = places[:, None] >= places[None, :]
    powers = jnp.exp(control)
    running = jnp.cumsum(powers, axis=0)
    powers_low = low(powers)
    affinity = jnp.einsum('thd,ihd->hti', queries, key_rows, precision=precise)
    scored = low(low_back(jnp.where(causal, affinity * 0.125, 0.0)))
    summed = low_back(jnp.einsum('hti,ihs->ths', scored, powers_low, precision=precise))
    slot_score = summed / running
    highest = lax.optimization_barrier(jnp.max(slot_score, axis=-1, keepdims=True))
    lifted = jnp.exp(slot_score - highest)
    slot_prob = lifted / lax.optimization_barrier(jnp.sum(lifted, axis=-1, keepdims=True))
    reading = low(slot_prob / running)
    mixing = jnp.einsum('ths,ihs->hti', reading, powers_low, precision=precise)
    mixing = low(low_back(jnp.where(causal, mixing, 0.0)))
    return low(low_back(jnp.einsum('hti,ihd->thd', mixing, value_rows, precision=precise)))

def residual_block(tokens, params):
    attn_gain, attn_shift, query_weight, key_weight, value_weight, control_weight, output_weight, ffn_gain, ffn_shift, expand_weight, expand_bias, shrink_weight, shrink_bias = params
    normed = low(layer_norm(tokens, attn_gain, attn_shift))
    queries = low(low_back(jnp.dot(normed, query_weight, precision=precise))).reshape(LEN, H, D // H)
    key_rows = low(low_back(jnp.dot(normed, key_weight, precision=precise))).reshape(LEN, H, D // H)
    value_rows = low(low_back(jnp.dot(normed, value_weight, precision=precise))).reshape(LEN, H, D // H)
    control = low_back(jnp.dot(normed, control_weight, precision=precise)).reshape(LEN, H, SLOTS)
    heads_out = attend(queries, key_rows, value_rows, control).reshape(LEN, D)
    branch = low_back(jnp.dot(heads_out, output_weight, precision=precise))
    residual = tokens + branch
    second = low(layer_norm(residual, ffn_gain, ffn_shift))
    hidden = low_back(jnp.dot(second, expand_weight, precision=precise) + expand_bias)
    activated = low(jax.nn.gelu(hidden, approximate=True))
    return residual + jnp.dot(activated, shrink_weight, precision=precise) + shrink_bias

def forward(inputs, params):

    def one_block(tokens):
        return residual_block(tokens, params)
    blocks = inputs.reshape(NSEQ, LEN, D)
    return lax.map(jax.checkpoint(one_block), blocks).reshape(TOKENS, D)

def reference(inputs, attn_gain, attn_shift, query_weight, key_weight, value_weight, control_weight, output_weight, ffn_gain, ffn_shift, expand_weight, expand_bias, shrink_weight, shrink_bias, cotangent):
    params = tuple((member.astype(jnp.float32) for member in (attn_gain, attn_shift, query_weight, key_weight, value_weight, control_weight, output_weight, ffn_gain, ffn_shift, expand_weight, expand_bias, shrink_weight, shrink_bias)))
    result, pull = jax.vjp(forward, inputs.astype(jnp.float32), params)
    input_grad, param_grads = pull(cotangent.astype(jnp.float32))
    return (result.astype(jnp.bfloat16), input_grad.astype(jnp.bfloat16), param_grads[0], param_grads[1], param_grads[2], param_grads[3], param_grads[4], param_grads[5], param_grads[6], param_grads[7], param_grads[8], param_grads[9], param_grads[10], param_grads[11], param_grads[12])
```

```python
import functools

import jax
import jax.numpy as jnp
from jax import lax
from jax.experimental import pallas as pl
from jax.experimental.pallas import tpu as pltpu
from jax.sharding import PartitionSpec as P

EPSILON = 1e-5
CHUNK = 128
PAIR = 128
F32 = jnp.float32
BF16 = jnp.bfloat16
LIMIT = 56 * 1024 * 1024


def nn(a, b):
    return lax.dot_general(a, b, (((1,), (0,)), ((), ())), preferred_element_type=F32)


def nt(a, b):
    return lax.dot_general(a, b, (((1,), (1,)), ((), ())), preferred_element_type=F32)


def tn(a, b):
    return lax.dot_general(a, b, (((0,), (0,)), ((), ())), preferred_element_type=F32)


def low(v):
    return v.astype(BF16)


def iota(shape, axis):
    return lax.broadcasted_iota(jnp.int32, shape, axis)


def first_half(shape):
    return iota(shape, 1) < PAIR // 2


def stacked(block):
    left = first_half(block.shape)
    zero = jnp.zeros_like(block)
    return jnp.concatenate([jnp.where(left, block, zero), jnp.where(left, zero, block)], axis=0)


def parts(v):
    high = low(v)
    return jnp.concatenate([high, low(v - high.astype(F32))], axis=1)


def whole(v):
    return v[:, :PAIR] + v[:, PAIR:]


def head_block(shape=(PAIR, PAIR)):
    return (iota(shape, 0) < PAIR // 2) == (iota(shape, 1) < PAIR // 2)


def causal_pair():
    return iota((CHUNK, 2 * CHUNK), 0) >= (iota((CHUNK, 2 * CHUNK), 1) & (CHUNK - 1))


def causal_pair_t():
    return iota((CHUNK, 2 * CHUNK), 0) <= (iota((CHUNK, 2 * CHUNK), 1) & (CHUNK - 1))


def ones_where(mask):
    return low(jnp.where(mask, 1.0, 0.0))


def norm_parts(tokens):
    average = jnp.mean(tokens, axis=-1, keepdims=True)
    centred = tokens - average
    rate = lax.rsqrt(jnp.mean(centred * centred, axis=-1, keepdims=True) + EPSILON)
    return centred * rate, rate


def norm_back(grad, normal, rate, gain):
    w = grad * gain
    return rate * (
        w
        - jnp.mean(w, axis=-1, keepdims=True)
        - normal * jnp.mean(w * normal, axis=-1, keepdims=True)
    )


def chunks(length):
    return [slice(c * CHUNK, (c + 1) * CHUNK) for c in range(length // CHUNK)]


def attend_forward(normed, weight, keep):
    q_ref, k_ref, v_ref, powers_ref, inverse_ref, score_ref, prob_ref, key_state, value_state, heads_ref = keep
    length = normed.shape[0]
    cuts = chunks(length)
    for rows in [slice(r, r + 256) for r in range(0, length, 256)]:
        made = nn(normed[rows, :], weight)
        q_ref[rows, :] = low(low(made[:, :PAIR]).astype(F32) * 0.125)
        k_ref[rows, :] = low(made[:, PAIR : 2 * PAIR])
        v_ref[rows, :] = low(made[:, 2 * PAIR : 3 * PAIR])
        powers_ref[rows, :] = jnp.exp(made[:, 3 * PAIR :])
    tri = ones_where(iota((CHUNK, CHUNK), 0) >= iota((CHUNK, CHUNK), 1))
    same = head_block()
    both = jnp.concatenate([ones_where(same)] * 2, axis=0)
    causal = causal_pair()
    carried = jnp.zeros((1, PAIR), F32)
    local = [whole(nn(tri, parts(powers_ref[rows, :]))) for rows in cuts]
    for rows, sums in zip(cuts, local):
        running = sums + carried
        carried = running[CHUNK - 1 :, :]
        inverse_ref[rows, :] = 1.0 / running
    key_sum = jnp.zeros((PAIR, PAIR), F32)
    value_sum = jnp.zeros((PAIR, PAIR), F32)
    for c, rows in enumerate(cuts):
        key_state[c, :, :] = low(jnp.where(same, key_sum, 0.0))
        value_state[c, :, :] = low(jnp.where(same, value_sum, 0.0))
        if c + 1 < len(cuts):
            powers_low = low(powers_ref[rows, :])
            key_sum = key_sum + tn(k_ref[rows, :], powers_low)
            value_sum = value_sum + tn(powers_low, v_ref[rows, :])
    left = first_half((CHUNK, PAIR))
    scored = [
        low(jnp.where(causal, nt(q_ref[rows, :], stacked(k_ref[rows, :])), 0.0)) for rows in cuts
    ]
    for c, rows in enumerate(cuts):
        summed = nn(scored[c], stacked(low(powers_ref[rows, :]))) + nn(q_ref[rows, :], key_state[c, :, :])
        score_ref[rows, :] = summed * inverse_ref[rows, :]
    for c, rows in enumerate(cuts):
        score = score_ref[rows, :]
        top_a = jnp.max(jnp.where(left, score, -jnp.inf), axis=-1, keepdims=True)
        top_b = jnp.max(jnp.where(left, -jnp.inf, score), axis=-1, keepdims=True)
        lifted = jnp.exp(score - jnp.where(left, top_a, top_b))
        prob_ref[rows, :] = lifted / nn(parts(lifted), both)
    reading = [low(prob_ref[rows, :] * inverse_ref[rows, :]) for rows in cuts]
    mixing = [
        low(jnp.where(causal, nt(reading[c], stacked(low(powers_ref[rows, :]))), 0.0))
        for c, rows in enumerate(cuts)
    ]
    for c, rows in enumerate(cuts):
        heads_ref[rows, :] = low(
            nn(mixing[c], stacked(v_ref[rows, :])) + nn(reading[c], value_state[c, :, :])
        )


def attend_backward(heads_grad, kept, backs):
    q_ref, k_ref, v_ref, powers_ref, inverse_ref, score_ref, prob_ref, key_state, value_state = kept
    cuts = chunks(heads_grad.shape[0])
    same = head_block()
    both = jnp.concatenate([ones_where(same)] * 2, axis=0)
    causal = causal_pair()
    causal_t = causal_pair_t()
    tri_t = ones_where(iota((CHUNK, CHUNK), 0) <= iota((CHUNK, CHUNK), 1))
    after = jnp.zeros((1, PAIR), F32)
    read_sum = jnp.zeros((PAIR, PAIR), F32)
    score_sum = jnp.zeros((PAIR, PAIR), F32)
    for c in reversed(range(len(cuts))):
        rows = cuts[c]
        q, k, v = q_ref[rows, :], k_ref[rows, :], v_ref[rows, :]
        grad = heads_grad[rows, :]
        inverse = inverse_ref[rows, :]
        prob = prob_ref[rows, :]
        powers = powers_ref[rows, :]
        powers_low = low(powers)
        reading = low(prob * inverse)
        powers_two, values_two, keys_two = stacked(powers_low), stacked(v), stacked(k)
        queries_two, grad_two, reading_two = stacked(q), stacked(grad), stacked(reading)
        read_state = low(jnp.where(same, read_sum, 0.0))
        score_state = low(jnp.where(same, score_sum, 0.0))
        mixing_t = low(jnp.where(causal_t, nt(powers_low, reading_two), 0.0))
        mixing_grad = low(jnp.where(causal, nt(grad, values_two), 0.0))
        mixing_grad_t = low(jnp.where(causal_t, nt(v, grad_two), 0.0))
        scored_t = low(jnp.where(causal_t, nt(k, queries_two), 0.0))
        values_grad = nn(mixing_t, grad_two) + nn(powers_low, read_state)
        reading_grad = nn(mixing_grad, powers_two) + nt(grad, value_state[c, :, :])
        powers_grad = nn(mixing_grad_t, reading_two) + nt(v, read_state)
        prob_grad = reading_grad * inverse
        weighed = prob * prob_grad
        slots_grad = weighed - prob * nn(parts(weighed), both)
        running_grad = -inverse * (weighed + slots_grad * score_ref[rows, :])
        summed_grad = low(slots_grad * inverse)
        summed_two = stacked(summed_grad)
        scored_grad = low(jnp.where(causal, nt(summed_grad, powers_two), 0.0))
        scored_grad_t = low(jnp.where(causal_t, nt(powers_low, summed_two), 0.0))
        powers_grad = powers_grad + nn(scored_t, summed_two) + nn(k, score_state)
        backs[rows, :PAIR] = low(
            0.125 * (nn(scored_grad, keys_two) + nt(summed_grad, key_state[c, :, :]))
        )
        backs[rows, PAIR : 2 * PAIR] = low(
            nn(scored_grad_t, queries_two) + nt(powers_low, score_state)
        )
        backs[rows, 2 * PAIR : 3 * PAIR] = low(values_grad)
        later = whole(nn(tri_t, parts(running_grad))) + after
        after = later[:1, :]
        backs[rows, 3 * PAIR :] = low((powers_grad + later) * powers)
        if c:
            read_sum = read_sum + tn(reading, grad)
            score_sum = score_sum + tn(q, summed_grad)


def kept_shapes(length, lead=()):
    n = length // CHUNK
    shape = jax.ShapeDtypeStruct
    return (
        [shape(lead + (length, PAIR), BF16)] * 3
        + [shape(lead + (length, PAIR), F32)] * 4
        + [shape(lead + (n, PAIR, PAIR), BF16)] * 2
        + [shape(lead + (length, PAIR), BF16)]
    )


def vmem(n):
    return [pl.BlockSpec(memory_space=pltpu.VMEM)] * n


def by_slot(shapes):
    return [
        pl.BlockSpec((None,) + s.shape[1:], lambda a, rank=len(s.shape): (a,) + (0,) * (rank - 1))
        for s in shapes
    ]


def fixed(shape):
    return pl.BlockSpec(shape, lambda a: (0,) * len(shape))


def cost(micros):
    return pl.CostEstimate(flops=int(micros * 1e9), bytes_accessed=int(micros * 1e6), transcendentals=0)


def params():
    return pltpu.CompilerParams(vmem_limit_bytes=LIMIT)


def select(width, offset, share, total):
    return ones_where(
        iota((width, total), 0) == offset + (iota((width, total), 1) & (share - 1))
    )


def owned(devices, share, total):
    return iota((devices, total), 0) == lax.shift_right_logical(
        iota((devices, total), 1), share.bit_length() - 1
    )


def spread(rows, offset, share, total):
    each = nn(rows, select(rows.shape[1], offset, share, total))
    return jnp.sum(jnp.where(owned(rows.shape[0], share, total), each, 0.0), axis=0, keepdims=True)


def collect(row, devices, offset, share):
    total = row.shape[1]
    rest = jnp.where(owned(devices, share, total), row, 0.0)
    chosen = select(128, offset, share, total)
    out = jnp.zeros((devices, 128), F32)
    for _ in range(3):
        part = low(rest)
        out = out + nt(part, chosen)
        rest = rest - part.astype(F32)
    return out


def fill(weight, pieces):
    if len(pieces) == 1:
        weight[...] = pieces[0][...]
        return
    mine = lax.axis_index("seq")
    rows = pieces[0].shape[0]
    for r, piece in enumerate(pieces):
        weight[pl.ds(pl.multiple_of((mine ^ r) * rows, rows), rows), :] = piece[...]


def first_kernel(tokens_ref, vectors_ref, weight_ref, normed_ref, residual_ref, *keep):
    tokens = tokens_ref[...].astype(F32)
    normal, _ = norm_parts(tokens)
    width = tokens.shape[1]
    share = width // vectors_ref.shape[0]
    small = vectors_ref[:, :128]
    gain = spread(small, 0, share, width)
    shift = spread(small, share, share, width)
    normed_ref[...] = low(normal * gain + shift)
    attend_forward(normed_ref, weight_ref[:width, :], keep)
    residual_ref[...] = tokens + nn(keep[-1][...], weight_ref[width:, :])


def forward_first(tokens, vectors, weight):
    length, width = tokens.shape
    outs = [jax.ShapeDtypeStruct((length, width), BF16), jax.ShapeDtypeStruct((length, width), F32)]
    outs += kept_shapes(length)
    made = pl.pallas_call(
        first_kernel,
        out_shape=outs,
        in_specs=vmem(3),
        out_specs=vmem(len(outs)),
        compiler_params=params(),
        cost_estimate=cost(6),
        name="attend_first",
    )(tokens, vectors, weight)
    return made[0], made[1], made[2:]


def rest_kernel(count, normed_ref, before_ref, *refs):
    pieces, residual_ref, keep, weight = refs[:count], refs[count], refs[count + 1 : -1], refs[-1]
    width = normed_ref.shape[1]
    fill(weight, pieces)

    @pl.when(pl.program_id(0) == 0)
    def _():
        residual_ref[...] = before_ref[...]

    attend_forward(normed_ref, weight[:width, :], keep)
    residual_ref[...] += nn(keep[-1][...], weight[width:, :])


def forward_rest(normed, residual, pieces):
    length, width = normed.shape
    slots = pieces[0].shape[0]
    keep = kept_shapes(length, (slots,))
    made = pl.pallas_call(
        functools.partial(rest_kernel, len(pieces)),
        grid=(slots,),
        out_shape=[jax.ShapeDtypeStruct((length, width), F32)] + keep,
        in_specs=[fixed((length, width))] * 2 + by_slot(pieces),
        out_specs=[fixed((length, width))] + by_slot(keep),
        scratch_shapes=[pltpu.VMEM((width + PAIR, 4 * PAIR), BF16)],
        compiler_params=params(),
        cost_estimate=cost(17),
        name="attend_rest",
    )(normed, residual, *pieces)
    return made[0], made[1:]


GELU_A = 0.7978845608028654
GELU_B = 0.044715


def gelu_both(u):
    square = u * u
    bend = jnp.tanh(GELU_A * (u + GELU_B * (square * u)))
    half = 0.5 * (1.0 + bend)
    slope = half + 0.5 * u * (1.0 - bend * bend) * (GELU_A * (1.0 + 3.0 * GELU_B * square))
    return u * half, slope


def place(core, chip, turn, slots):
    seq = lax.axis_index("seq") ^ (2 * chip + core)
    return seq * slots + lax.rem(lax.axis_index("head") + turn, slots)


def weight_copies(pieces, expand, shrink, sems):
    if len(pieces) == 2:
        return [
            pltpu.make_async_copy(pieces[0], expand, sems.at[0]),
            pltpu.make_async_copy(pieces[1], shrink, sems.at[1]),
        ]
    copies = []
    for r, piece in enumerate(pieces):
        slots = piece.shape[0]
        for a in range(slots):
            source = place(r % 2, r // 2, slots - a, slots)
            n = len(copies)
            copies.append(
                pltpu.make_async_copy(
                    piece.at[a, pl.ds(0, 4)], expand.at[pl.ds(source * 4, 4)], sems.at[n]
                )
            )
            copies.append(
                pltpu.make_async_copy(
                    piece.at[a, pl.ds(4, 4)], shrink.at[:, source], sems.at[n + 1]
                )
            )
    return copies


def grad_copies(expand, shrink, outs, sems):
    if len(outs) == 2 and outs[0].shape == expand.shape:
        return [
            pltpu.make_async_copy(expand, outs[0], sems.at[0]),
            pltpu.make_async_copy(shrink, outs[1], sems.at[1]),
        ]
    copies = []
    for core, out in enumerate(outs):
        for chip in range(out.shape[0]):
            slots = out.shape[1]
            for a in range(slots):
                target = place(core, chip, a, slots)
                n = len(copies)
                copies.append(
                    pltpu.make_async_copy(
                        expand.at[pl.ds(target * 4, 4)], out.at[chip, a, pl.ds(0, 4)], sems.at[n]
                    )
                )
                copies.append(
                    pltpu.make_async_copy(
                        shrink.at[:, target], out.at[chip, a, pl.ds(4, 4)], sems.at[n + 1]
                    )
                )
    return copies


def ffn_kernel(count, residual_ref, vectors_ref, cotangent_ref, *refs):
    pieces = refs[:count]
    result_ref, grad_ref, branch_ref, sums_ref = refs[count : count + 4]
    grads = refs[count + 4 : count + 6]
    (expand_all, shrink_all, expand_grad, shrink_grad, second, normal_ref, rate_ref, total, back,
     gains, bias_row, bias_grads, sems) = refs[count + 6 :]
    k = pl.program_id(0)
    steps = pl.num_programs(0)
    length, width = residual_ref.shape
    devices = vectors_ref.shape[0]
    share = width // devices
    tiles = [slice(r, r + 256) for r in range(0, length, 256)]
    step = expand_all.shape[0] * 16 // 4
    hidden_share = 4 * step // devices

    @pl.when(k == 0)
    def _():
        copies = weight_copies(pieces, expand_all, shrink_all, sems)
        for copy in copies:
            copy.start()
        small = vectors_ref[:, :128]
        for i in range(3):
            gains[i : i + 1, :] = spread(small, (2 + i) * share, share, width)
        wide = spread(vectors_ref[:, 128:], 0, hidden_share, 4 * step)
        for i in range(4):
            bias_row[i, 0:1, :] = wide[:, i * step : (i + 1) * step]
        for rows in tiles:
            normal, rate = norm_parts(residual_ref[rows, :])
            normal_ref[rows, :] = normal
            rate_ref[rows, :] = rate
            second[rows, :] = low(normal * gains[0:1, :] + gains[1:2, :])
            total[rows, :] = residual_ref[rows, :] + gains[2:3, :]
            back[rows, :] = jnp.zeros((256, width), F32)
        for copy in copies:
            copy.wait()

    blocks = step // 16
    expand = expand_all[pl.ds(k * blocks, blocks)].reshape(step, width)
    shrink = shrink_all[k].reshape(width, step)
    bias = bias_row[k][0:1, :]
    bias_grad = jnp.zeros((1, step), F32)
    acts, hids = [], []
    for rows in tiles:
        hidden = nt(second[rows, :], expand) + bias
        pull = nn(cotangent_ref[rows, :], shrink)
        value, slope = gelu_both(hidden)
        activated = low(value)
        hidden_grad = low(pull * slope)
        bias_grad = bias_grad + jnp.sum(hidden_grad.astype(F32), axis=0, keepdims=True)
        total[rows, :] = total[rows, :] + nt(activated, shrink)
        back[rows, :] = back[rows, :] + nn(hidden_grad, expand)
        acts.append(activated)
        hids.append(hidden_grad)
    bias_grads[k, 0:1, :] = bias_grad
    shrink_grad[k] = low(tn(cotangent_ref[...], jnp.concatenate(acts, axis=0))).reshape(
        width // 16, 16, step
    )
    expand_grad[pl.ds(k * blocks, blocks)] = low(
        tn(jnp.concatenate(hids, axis=0), second[...])
    ).reshape(blocks, 16, width)

    @pl.when(k == steps - 1)
    def _():
        copies = grad_copies(expand_grad, shrink_grad, grads, sems)
        for copy in copies:
            copy.start()
        gain = gains[0:1, :]
        gain_grad = jnp.zeros((1, width), F32)
        shift_grad = jnp.zeros((1, width), F32)
        outer = jnp.zeros((1, width), F32)
        for rows in tiles:
            result_ref[rows, :] = low(total[rows, :])
            grad = back[rows, :]
            normal = normal_ref[rows, :]
            upstream = cotangent_ref[rows, :].astype(F32)
            gain_grad = gain_grad + jnp.sum(grad * normal, axis=0, keepdims=True)
            shift_grad = shift_grad + jnp.sum(grad, axis=0, keepdims=True)
            outer = outer + jnp.sum(upstream, axis=0, keepdims=True)
            full = upstream + norm_back(grad, normal, rate_ref[rows, :], gain)
            grad_ref[rows, :] = full
            branch_ref[rows, :] = low(full)
        sums_ref[:, :128] = (
            collect(gain_grad, devices, 2 * share, share)
            + collect(shift_grad, devices, 3 * share, share)
            + collect(outer, devices, 4 * share, share)
        )
        wide = jnp.concatenate([bias_grads[i][0:1, :] for i in range(4)], axis=1)
        sums_ref[:, 128:] = collect(wide, devices, 0, hidden_share)
        for copy in copies:
            copy.wait()


def feed_forward(residual, vectors, cotangent, pieces, grad_shapes, hidden):
    length, width = residual.shape
    step = hidden // 4
    shape = jax.ShapeDtypeStruct
    anywhere = pl.BlockSpec(memory_space=pl.ANY)
    return pl.pallas_call(
        functools.partial(ffn_kernel, len(pieces)),
        grid=(4,),
        out_shape=[
            shape((length, width), BF16),
            shape((length, width), F32),
            shape((length, width), BF16),
            shape(vectors.shape, F32),
        ]
        + [shape(s, BF16) for s in grad_shapes],
        in_specs=[fixed((length, width)), fixed(vectors.shape), fixed((length, width))]
        + [anywhere] * len(pieces),
        out_specs=[fixed((length, width))] * 3 + [fixed(vectors.shape)] + [anywhere] * len(grad_shapes),
        scratch_shapes=[
            pltpu.VMEM((hidden // 16, 16, width), BF16),
            pltpu.VMEM((4, width // 16, 16, step), BF16),
            pltpu.VMEM((hidden // 16, 16, width), BF16),
            pltpu.VMEM((4, width // 16, 16, step), BF16),
            pltpu.VMEM((length, width), BF16),
            pltpu.VMEM((length, width), F32),
            pltpu.VMEM((length, 1), F32),
            pltpu.VMEM((length, width), F32),
            pltpu.VMEM((length, width), F32),
            pltpu.VMEM((8, width), F32),
            pltpu.VMEM((4, 8, step), F32),
            pltpu.VMEM((4, 8, step), F32),
            pltpu.SemaphoreType.DMA((max(2, 2 * vectors.shape[0]),)),
        ],
        compiler_params=params(),
        cost_estimate=cost(27),
        name="feed_forward",
    )(residual, vectors, cotangent, *pieces)


def pair_grads(branch_ref, normed_ref, weight_in, weight_out, kept, heads_ref, outs, grad, backs, made):
    grad[...] = low(nt(branch_ref[...], weight_out))
    attend_backward(grad, kept, backs)
    made[:, : 4 * PAIR] = low(tn(normed_ref[...], backs[...]))
    made[:, 4 * PAIR :] = low(tn(branch_ref[...], heads_ref[...]))
    if len(outs) == 1:
        outs[0][...] = made[...]
        return
    seq = lax.axis_index("seq")
    for core, out in enumerate(outs):
        rows = out.shape[1]
        for chip in range(out.shape[0]):
            start = pl.multiple_of((seq ^ (2 * chip + core)) * rows, rows)
            out[chip] = made[pl.ds(start, rows), :]


def back_rest_kernel(count, parts_out, branch_ref, normed_ref, *refs):
    pieces, refs = refs[:count], refs[count:]
    kept, heads_ref, refs = refs[:9], refs[9], refs[10:]
    sum_ref, outs = refs[0], refs[1 : 1 + parts_out]
    weight, grad, backs, made = refs[1 + parts_out :]
    width = normed_ref.shape[1]
    fill(weight, pieces)
    pair_grads(
        branch_ref, normed_ref, None, weight[width:, :], kept, heads_ref, outs, grad, backs, made
    )

    @pl.when(pl.program_id(0) == 0)
    def _():
        sum_ref[...] = jnp.zeros_like(sum_ref)

    sum_ref[...] += nt(backs[...], weight[:width, :])


def back_scratch(length, width):
    return [
        pltpu.VMEM((length, PAIR), BF16),
        pltpu.VMEM((length, 4 * PAIR), BF16),
        pltpu.VMEM((width, 5 * PAIR), BF16),
    ]


def backward_rest(branch, normed, pieces, kept, grad_shapes):
    length, width = branch.shape
    slots = pieces[0].shape[0]
    shape = jax.ShapeDtypeStruct
    grads = [shape((slots,) + s, BF16) for s in grad_shapes]
    return pl.pallas_call(
        functools.partial(back_rest_kernel, len(pieces), len(grads)),
        grid=(slots,),
        out_shape=[shape((length, width), F32)] + grads,
        in_specs=[fixed((length, width))] * 2 + by_slot(pieces) + by_slot(kept),
        out_specs=[fixed((length, width))] + by_slot(grads),
        scratch_shapes=[pltpu.VMEM((width + PAIR, 4 * PAIR), BF16)] + back_scratch(length, width),
        compiler_params=params(),
        cost_estimate=cost(36),
        name="attend_back_rest",
    )(branch, normed, *pieces, *kept)


def back_first_kernel(parts_out, branch_ref, normed_ref, weight_ref, *refs):
    kept, heads_ref, refs = refs[:9], refs[9], refs[10:]
    backs, outs = refs[0], refs[1 : 1 + parts_out]
    grad, made = refs[1 + parts_out :]
    width = normed_ref.shape[1]
    pair_grads(
        branch_ref, normed_ref, None, weight_ref[width:, :], kept, heads_ref, outs, grad, backs, made
    )


def backward_first(branch, normed, weight, kept, grad_shapes):
    length, width = branch.shape
    shape = jax.ShapeDtypeStruct
    outs = [shape((length, 4 * PAIR), BF16)] + [shape(s, BF16) for s in grad_shapes]
    scratch = back_scratch(length, width)
    return pl.pallas_call(
        functools.partial(back_first_kernel, len(grad_shapes)),
        out_shape=outs,
        in_specs=vmem(13),
        out_specs=vmem(len(outs)),
        scratch_shapes=[scratch[0], scratch[2]],
        compiler_params=params(),
        cost_estimate=cost(11),
        name="attend_back_first",
    )(branch, normed, weight, *kept)


def last_kernel(tokens_ref, vectors_ref, backs_ref, weight_ref, total_ref, grad_ref, before_ref, out_ref, sums_ref):
    length, width = tokens_ref.shape
    devices = vectors_ref.shape[0]
    share = width // devices
    gain = spread(vectors_ref[:, :128], 0, share, width)
    gain_grad = jnp.zeros((1, width), F32)
    shift_grad = jnp.zeros((1, width), F32)
    for rows in [slice(r, r + 256) for r in range(0, length, 256)]:
        grad = total_ref[rows, :] + nt(backs_ref[rows, :], weight_ref[:width, :])
        normal, rate = norm_parts(tokens_ref[rows, :].astype(F32))
        gain_grad = gain_grad + jnp.sum(grad * normal, axis=0, keepdims=True)
        shift_grad = shift_grad + jnp.sum(grad, axis=0, keepdims=True)
        out_ref[rows, :] = low(grad_ref[rows, :] + norm_back(grad, normal, rate, gain))
    sums_ref[:, :128] = (
        before_ref[:, :128]
        + collect(gain_grad, devices, 0, share)
        + collect(shift_grad, devices, share, share)
    )
    sums_ref[:, 128:] = before_ref[:, 128:]


def finish(tokens, vectors, backs, weight, total, grad, before):
    shape = jax.ShapeDtypeStruct
    return pl.pallas_call(
        last_kernel,
        out_shape=[shape(tokens.shape, BF16), shape(before.shape, F32)],
        in_specs=vmem(7),
        out_specs=vmem(2),
        compiler_params=params(),
        cost_estimate=cost(5),
        name="norm_back",
    )(tokens, vectors, backs, weight, total, grad, before)


def flip(count, bit):
    return [(i, i ^ bit) for i in range(count)]


def turn(count, by):
    return [(i, (i + by) % count) for i in range(count)]


def add(*members):
    return functools.reduce(lambda a, b: a + b, [m.astype(F32) for m in members])


def across(shares, chips, seqs):
    held = [shares] + [lax.ppermute(shares, "seq", flip(seqs, 2 * r)) for r in range(1, chips)]
    mates = [lax.ppermute(h, "seq", flip(seqs, 1)) for h in held]
    return [member for both in zip(held, mates) for member in both]


def back_across(keep, send, chips, seqs):
    other = lax.ppermute(send, "seq", flip(seqs, 1))
    made = [add(keep[r], other[r]) for r in range(chips)]
    came = [lax.ppermute(low(made[r]), "seq", flip(seqs, 2 * r)) for r in range(1, chips)]
    return add(made[0], *came)


def body(
    inputs,
    attn_gain,
    attn_shift,
    query_weight,
    key_weight,
    value_weight,
    control_weight,
    output_weight,
    ffn_gain,
    ffn_shift,
    expand_weight,
    expand_bias,
    shrink_weight,
    shrink_bias,
    cotangent,
):
    seqs, slots = lax.axis_size("seq"), lax.axis_size("head")
    devices = seqs * slots
    chips = seqs // 2
    width = inputs.shape[1]
    share = width // devices
    hidden_share = expand_weight.shape[1]
    hidden = hidden_share * devices
    z = lax.axis_index("head")
    direct = share % 16 == 0 and hidden_share == 4 * share and (width + PAIR) % (16 * seqs) == 0

    own = jnp.concatenate(
        [
            jnp.concatenate([query_weight, key_weight, value_weight, control_weight], axis=1),
            output_weight,
        ],
        axis=0,
    )
    small = jnp.concatenate([attn_gain, attn_shift, ffn_gain, ffn_shift, shrink_bias])
    row = jnp.concatenate(
        [
            small,
            jnp.zeros((128 - small.shape[0],), BF16),
            expand_bias,
            jnp.zeros((128 - expand_bias.shape[0],), BF16),
        ]
    )
    vectors = lax.all_to_all(
        jnp.broadcast_to(row[None, :], (devices, 256)), ("seq", "head"), 0, 0, tiled=True
    )
    expand_t = expand_weight.T
    shrink_t = shrink_weight.T
    if direct:
        rows = own.shape[0] // seqs
        piece = lax.dynamic_slice_in_dim(own, lax.axis_index("seq") * rows, rows, axis=0)
        near = jnp.stack([lax.ppermute(piece, "head", turn(slots, a)) for a in range(1, slots)])
        pieces = across(near, chips, seqs)
        load = jnp.concatenate(
            [expand_t.reshape(4, 16, width)]
            + [shrink_t[None, :, k * width : (k + 1) * width] for k in range(4)],
            axis=0,
        )
        near = jnp.stack([load] + [lax.ppermute(load, "head", turn(slots, a)) for a in range(1, slots)])
        ffn_pieces = across(near, chips, seqs)
        pair_shapes = [(chips, width // seqs, 5 * PAIR)] * 2
        ffn_shapes = [(chips, slots, 8, 16, width)] * 2
    else:
        every = lax.all_gather(own, "head", axis=0, tiled=False)
        pieces = [jnp.stack([every[(z + slots - a) % slots] for a in range(1, slots)])]
        ffn_pieces = [
            lax.all_gather(expand_t, ("seq", "head"), axis=0, tiled=True).reshape(hidden // 16, 16, width),
            lax.all_gather(shrink_t, ("seq", "head"), axis=0, tiled=True)
            .reshape(width // 16, 16, 4, hidden // 4)
            .transpose(2, 0, 1, 3),
        ]
        pair_shapes = [(width, 5 * PAIR)]
        ffn_shapes = [(hidden // 16, 16, width), (4, width // 16, 16, hidden // 4)]

    normed, residual, kept_first = forward_first(inputs, vectors, own)
    residual, kept_rest = forward_rest(normed, residual, pieces)
    result, residual_grad, branch, sums, *ffn_grads = feed_forward(
        residual, vectors, cotangent, ffn_pieces, ffn_shapes, hidden
    )
    total, *rest_grads = backward_rest(branch, normed, pieces, kept_rest, pair_shapes)
    backs, *first_grads = backward_first(branch, normed, own, kept_first, pair_shapes)
    input_grad, sums = finish(inputs, vectors, backs, own, total, residual_grad, sums)

    if direct:
        mine = back_across(*ffn_grads, chips, seqs)
        came = [lax.ppermute(low(mine[a]), "head", turn(slots, a)) for a in range(1, slots)]
        ffn_sum = add(mine[0], *came)
        expand_grad = ffn_sum[:4].reshape(hidden_share, width)
        shrink_grad = jnp.concatenate([ffn_sum[4 + k] for k in range(4)], axis=1)
        keep, send = [jnp.swapaxes(g, 0, 1) for g in rest_grads]
        rest = back_across(keep, send, chips, seqs)
        came = [
            lax.ppermute(low(rest[a - 1]), "head", turn(slots, slots - a)) for a in range(1, slots)
        ]
        pair_sum = add(back_across(*first_grads, chips, seqs), *came)
    else:
        expand_grad = lax.psum_scatter(
            ffn_grads[0].reshape(hidden, width).astype(F32), ("seq", "head"), scatter_dimension=0, tiled=True
        )
        shrink_grad = lax.psum_scatter(
            ffn_grads[1].transpose(1, 2, 0, 3).reshape(width, hidden).astype(F32),
            ("seq", "head"),
            scatter_dimension=0,
            tiled=True,
        )
        every = jnp.concatenate([first_grads[0][None], rest_grads[0]], axis=0).astype(F32)
        every = jnp.stack([every[(z + slots - p) % slots] for p in range(slots)])
        pair_sum = lax.psum_scatter(every, "head", scatter_dimension=0, tiled=False)
        pair_sum = lax.psum_scatter(pair_sum, "seq", scatter_dimension=0, tiled=True)

    sums = jnp.sum(lax.all_to_all(sums, ("seq", "head"), 0, 0, tiled=True), axis=0)
    vector = [sums[i * share : (i + 1) * share] for i in range(5)]
    return (
        result,
        input_grad,
        vector[0],
        vector[1],
        pair_sum[:, :PAIR],
        pair_sum[:, PAIR : 2 * PAIR],
        pair_sum[:, 2 * PAIR : 3 * PAIR],
        pair_sum[:, 3 * PAIR : 4 * PAIR],
        pair_sum[:, 4 * PAIR :].T,
        vector[2],
        vector[3],
        expand_grad.T,
        sums[128 : 128 + hidden_share],
        shrink_grad.T,
        vector[4],
    )


def solution(mesh):
    placed = (
        P(("seq", "head"), None),
        P(("seq", "head")),
        P(("seq", "head")),
        P(None, "head"),
        P(None, "head"),
        P(None, "head"),
        P(None, "head"),
        P("head", None),
        P(("seq", "head")),
        P(("seq", "head")),
        P(None, ("seq", "head")),
        P(("seq", "head")),
        P(None, ("seq", "head")),
        P(("seq", "head")),
        P(("seq", "head"), None),
    )
    return jax.shard_map(
        body,
        mesh=mesh,
        in_specs=placed,
        out_specs=(
            P(("seq", "head"), None),
            P(("seq", "head"), None),
            P(("seq", "head")),
            P(("seq", "head")),
            P("seq", "head"),
            P("seq", "head"),
            P("seq", "head"),
            P("seq", "head"),
            P("head", "seq"),
            P(("seq", "head")),
            P(("seq", "head")),
            P(None, ("seq", "head")),
            P(("seq", "head")),
            P(None, ("seq", "head")),
            P(("seq", "head")),
        ),
        check_vma=False,
    )
```

```python
import functools

import jax
import jax.numpy as jnp
from jax import lax
from jax.experimental import pallas as pl
from jax.experimental.pallas import tpu as pltpu
from jax.sharding import PartitionSpec as P

EPSILON = 1e-5
CHUNK = 128
PAIR = 128
F32 = jnp.float32
BF16 = jnp.bfloat16
LIMIT = 56 * 1024 * 1024


def nn(a, b):
    return lax.dot_general(a, b, (((1,), (0,)), ((), ())), preferred_element_type=F32)


def nt(a, b):
    return lax.dot_general(a, b, (((1,), (1,)), ((), ())), preferred_element_type=F32)


def tn(a, b):
    return lax.dot_general(a, b, (((0,), (0,)), ((), ())), preferred_element_type=F32)


def low(v):
    return v.astype(BF16)


def iota(shape, axis):
    return lax.broadcasted_iota(jnp.int32, shape, axis)


def first_half(shape):
    return iota(shape, 1) < PAIR // 2


def stacked(block):
    left = first_half(block.shape)
    zero = jnp.zeros_like(block)
    return jnp.concatenate([jnp.where(left, block, zero), jnp.where(left, zero, block)], axis=0)


def parts(v):
    high = low(v)
    return jnp.concatenate([high, low(v - high.astype(F32))], axis=1)


def whole(v):
    return v[:, :PAIR] + v[:, PAIR:]


def head_block(shape=(PAIR, PAIR)):
    return (iota(shape, 0) < PAIR // 2) == (iota(shape, 1) < PAIR // 2)


def causal_pair():
    return iota((CHUNK, 2 * CHUNK), 0) >= (iota((CHUNK, 2 * CHUNK), 1) & (CHUNK - 1))


def causal_pair_t():
    return iota((CHUNK, 2 * CHUNK), 0) <= (iota((CHUNK, 2 * CHUNK), 1) & (CHUNK - 1))


def ones_where(mask):
    return low(jnp.where(mask, 1.0, 0.0))


def norm_parts(tokens):
    average = jnp.mean(tokens, axis=-1, keepdims=True)
    centred = tokens - average
    rate = lax.rsqrt(jnp.mean(centred * centred, axis=-1, keepdims=True) + EPSILON)
    return centred * rate, rate


def norm_back(grad, normal, rate, gain):
    w = grad * gain
    return rate * (
        w
        - jnp.mean(w, axis=-1, keepdims=True)
        - normal * jnp.mean(w * normal, axis=-1, keepdims=True)
    )


def chunks(length):
    return [slice(c * CHUNK, (c + 1) * CHUNK) for c in range(length // CHUNK)]


def attend_forward(normed, weight, keep):
    q_ref, k_ref, v_ref, powers_ref, inverse_ref, score_ref, prob_ref, key_state, value_state, heads_ref = keep
    length = normed.shape[0]
    cuts = chunks(length)
    for rows in [slice(r, r + 256) for r in range(0, length, 256)]:
        made = nn(normed[rows, :], weight)
        q_ref[rows, :] = low(low(made[:, :PAIR]).astype(F32) * 0.125)
        k_ref[rows, :] = low(made[:, PAIR : 2 * PAIR])
        v_ref[rows, :] = low(made[:, 2 * PAIR : 3 * PAIR])
        powers_ref[rows, :] = jnp.exp(made[:, 3 * PAIR :])
    tri = ones_where(iota((CHUNK, CHUNK), 0) >= iota((CHUNK, CHUNK), 1))
    same = head_block()
    both = jnp.concatenate([ones_where(same)] * 2, axis=0)
    causal = causal_pair()
    carried = jnp.zeros((1, PAIR), F32)
    local = [whole(nn(tri, parts(powers_ref[rows, :]))) for rows in cuts]
    for rows, sums in zip(cuts, local):
        running = sums + carried
        carried = running[CHUNK - 1 :, :]
        inverse_ref[rows, :] = 1.0 / running
    key_sum = jnp.zeros((PAIR, PAIR), F32)
    value_sum = jnp.zeros((PAIR, PAIR), F32)
    for c, rows in enumerate(cuts):
        key_state[c, :, :] = low(jnp.where(same, key_sum, 0.0))
        value_state[c, :, :] = low(jnp.where(same, value_sum, 0.0))
        if c + 1 < len(cuts):
            powers_low = low(powers_ref[rows, :])
            key_sum = key_sum + tn(k_ref[rows, :], powers_low)
            value_sum = value_sum + tn(powers_low, v_ref[rows, :])
    left = first_half((CHUNK, PAIR))
    scored = [
        low(jnp.where(causal, nt(q_ref[rows, :], stacked(k_ref[rows, :])), 0.0)) for rows in cuts
    ]
    for c, rows in enumerate(cuts):
        summed = nn(scored[c], stacked(low(powers_ref[rows, :]))) + nn(q_ref[rows, :], key_state[c, :, :])
        score_ref[rows, :] = summed * inverse_ref[rows, :]
    for c, rows in enumerate(cuts):
        score = score_ref[rows, :]
        top_a = jnp.max(jnp.where(left, score, -jnp.inf), axis=-1, keepdims=True)
        top_b = jnp.max(jnp.where(left, -jnp.inf, score), axis=-1, keepdims=True)
        lifted = jnp.exp(score - jnp.where(left, top_a, top_b))
        prob_ref[rows, :] = lifted / nn(parts(lifted), both)
    reading = [low(prob_ref[rows, :] * inverse_ref[rows, :]) for rows in cuts]
    mixing = [
        low(jnp.where(causal, nt(reading[c], stacked(low(powers_ref[rows, :]))), 0.0))
        for c, rows in enumerate(cuts)
    ]
    for c, rows in enumerate(cuts):
        heads_ref[rows, :] = low(
            nn(mixing[c], stacked(v_ref[rows, :])) + nn(reading[c], value_state[c, :, :])
        )


def attend_backward(heads_grad, kept, backs):
    q_ref, k_ref, v_ref, powers_ref, inverse_ref, score_ref, prob_ref, key_state, value_state = kept
    cuts = chunks(heads_grad.shape[0])
    same = head_block()
    both = jnp.concatenate([ones_where(same)] * 2, axis=0)
    causal = causal_pair()
    causal_t = causal_pair_t()
    tri_t = ones_where(iota((CHUNK, CHUNK), 0) <= iota((CHUNK, CHUNK), 1))
    after = jnp.zeros((1, PAIR), F32)
    read_sum = jnp.zeros((PAIR, PAIR), F32)
    score_sum = jnp.zeros((PAIR, PAIR), F32)
    for c in reversed(range(len(cuts))):
        rows = cuts[c]
        q, k, v = q_ref[rows, :], k_ref[rows, :], v_ref[rows, :]
        grad = heads_grad[rows, :]
        inverse = inverse_ref[rows, :]
        prob = prob_ref[rows, :]
        powers = powers_ref[rows, :]
        powers_low = low(powers)
        reading = low(prob * inverse)
        powers_two, values_two, keys_two = stacked(powers_low), stacked(v), stacked(k)
        queries_two, grad_two, reading_two = stacked(q), stacked(grad), stacked(reading)
        read_state = low(jnp.where(same, read_sum, 0.0))
        score_state = low(jnp.where(same, score_sum, 0.0))
        mixing_t = low(jnp.where(causal_t, nt(powers_low, reading_two), 0.0))
        mixing_grad = low(jnp.where(causal, nt(grad, values_two), 0.0))
        mixing_grad_t = low(jnp.where(causal_t, nt(v, grad_two), 0.0))
        scored_t = low(jnp.where(causal_t, nt(k, queries_two), 0.0))
        values_grad = nn(mixing_t, grad_two) + nn(powers_low, read_state)
        reading_grad = nn(mixing_grad, powers_two) + nt(grad, value_state[c, :, :])
        powers_grad = nn(mixing_grad_t, reading_two) + nt(v, read_state)
        prob_grad = reading_grad * inverse
        weighed = prob * prob_grad
        slots_grad = weighed - prob * nn(parts(weighed), both)
        running_grad = -inverse * (weighed + slots_grad * score_ref[rows, :])
        summed_grad = low(slots_grad * inverse)
        summed_two = stacked(summed_grad)
        scored_grad = low(jnp.where(causal, nt(summed_grad, powers_two), 0.0))
        scored_grad_t = low(jnp.where(causal_t, nt(powers_low, summed_two), 0.0))
        powers_grad = powers_grad + nn(scored_t, summed_two) + nn(k, score_state)
        backs[rows, :PAIR] = low(
            0.125 * (nn(scored_grad, keys_two) + nt(summed_grad, key_state[c, :, :]))
        )
        backs[rows, PAIR : 2 * PAIR] = low(
            nn(scored_grad_t, queries_two) + nt(powers_low, score_state)
        )
        backs[rows, 2 * PAIR : 3 * PAIR] = low(values_grad)
        later = whole(nn(tri_t, parts(running_grad))) + after
        after = later[:1, :]
        backs[rows, 3 * PAIR :] = low((powers_grad + later) * powers)
        if c:
            read_sum = read_sum + tn(reading, grad)
            score_sum = score_sum + tn(q, summed_grad)


def kept_shapes(length, lead=()):
    n = length // CHUNK
    shape = jax.ShapeDtypeStruct
    return (
        [shape(lead + (length, PAIR), BF16)] * 3
        + [shape(lead + (length, PAIR), F32)] * 4
        + [shape(lead + (n, PAIR, PAIR), BF16)] * 2
        + [shape(lead + (length, PAIR), BF16)]
    )


def vmem(n):
    return [pl.BlockSpec(memory_space=pltpu.VMEM)] * n


def by_slot(shapes):
    return [
        pl.BlockSpec((None,) + s.shape[1:], lambda a, rank=len(s.shape): (a,) + (0,) * (rank - 1))
        for s in shapes
    ]


def fixed(shape):
    return pl.BlockSpec(shape, lambda a: (0,) * len(shape))


def cost(micros):
    return pl.CostEstimate(flops=int(micros * 1e9), bytes_accessed=int(micros * 1e6), transcendentals=0)


def params():
    return pltpu.CompilerParams(vmem_limit_bytes=LIMIT)


def select(width, offset, share, total):
    return ones_where(
        iota((width, total), 0) == offset + (iota((width, total), 1) & (share - 1))
    )


def owned(devices, share, total):
    return iota((devices, total), 0) == lax.shift_right_logical(
        iota((devices, total), 1), share.bit_length() - 1
    )


def spread(rows, offset, share, total):
    each = nn(rows, select(rows.shape[1], offset, share, total))
    return jnp.sum(jnp.where(owned(rows.shape[0], share, total), each, 0.0), axis=0, keepdims=True)


def collect(row, devices, offset, share):
    total = row.shape[1]
    rest = jnp.where(owned(devices, share, total), row, 0.0)
    chosen = select(128, offset, share, total)
    out = jnp.zeros((devices, 128), F32)
    for _ in range(3):
        part = low(rest)
        out = out + nt(part, chosen)
        rest = rest - part.astype(F32)
    return out


def fill(weight, own_ref, pieces, slot):
    rows = weight.shape[0] // len(pieces)
    stride = rows + 16 if len(pieces) > 1 else rows

    @pl.when(slot == 0)
    def _():
        weight[...] = own_ref[...]

    @pl.when(slot > 0)
    def _():
        first = pl.multiple_of((slot - 1) * stride, 16)
        mine = lax.axis_index("seq") if len(pieces) > 1 else 0
        for r, piece in enumerate(pieces):
            weight[pl.ds(pl.multiple_of((mine ^ r) * rows, 16), rows), :] = piece[pl.ds(first, rows), :]


def gather_vectors(pieces, rows, slots, vectors, staged):
    for r, piece in enumerate(pieces):
        for a in range(slots):
            first = a * (rows + 16) - 16 if a else (slots - 1) * (rows + 16)
            source = place(r % 2, r // 2, slots - a, slots)
            staged[pl.ds(source, 1), :] = piece[first : first + 16, :256].astype(F32)[0:1, :]
    vectors[...] = low(staged[...])


def forward_kernel(count, slots, tokens_ref, own_ref, *refs):
    pieces, refs = refs[:count], refs[count:]
    if count == 1:
        given, refs = refs[0], refs[1:]
    normed_ref, residual_ref, vectors_ref, keep = refs[0], refs[1], refs[2], refs[3:-2]
    weight, staged = refs[-2:]
    slot = pl.program_id(0)
    length, width = tokens_ref.shape
    share = width // vectors_ref.shape[0]

    @pl.when(slot == 0)
    def _():
        if count == 1:
            vectors_ref[...] = given[...]
        else:
            gather_vectors(pieces, weight.shape[0] // count, slots, vectors_ref, staged)
        small = vectors_ref[:, :128]
        gain = spread(small, 0, share, width)
        shift = spread(small, share, share, width)
        for rows in [slice(r, r + 256) for r in range(0, length, 256)]:
            tokens = tokens_ref[rows, :].astype(F32)
            normal, _ = norm_parts(tokens)
            normed_ref[rows, :] = low(normal * gain + shift)
            residual_ref[rows, :] = tokens

    fill(weight, own_ref, pieces, slot)
    attend_forward(normed_ref, weight[:width, :], keep)
    residual_ref[...] += nn(keep[-1][...], weight[width:, :])


def forward(tokens, own, pieces, vectors, devices, slots):
    length, width = tokens.shape
    shape = jax.ShapeDtypeStruct
    keep = kept_shapes(length, (slots,))
    given = [] if vectors is None else [vectors]
    operands = [tokens, own, *pieces, *given]
    outs = [shape((length, width), BF16), shape((length, width), F32), shape((devices, 256), BF16)]
    made = pl.pallas_call(
        functools.partial(forward_kernel, len(pieces), slots),
        grid=(slots,),
        out_shape=outs + keep,
        in_specs=[fixed(o.shape) for o in operands],
        out_specs=[fixed(o.shape) for o in outs] + by_slot(keep),
        scratch_shapes=[pltpu.VMEM(own.shape, BF16), pltpu.VMEM((devices, 256), F32)],
        compiler_params=params(),
        cost_estimate=cost(18),
        name="attend_forward",
    )(*operands)
    return made[0], made[1], made[2], made[3:]


GELU_A = 0.7978845608028654
GELU_B = 0.044715


def gelu_both(u):
    square = u * u
    bend = jnp.tanh(GELU_A * (u + GELU_B * (square * u)))
    half = 0.5 * (1.0 + bend)
    slope = half + 0.5 * u * (1.0 - bend * bend) * (GELU_A * (1.0 + 3.0 * GELU_B * square))
    return u * half, slope


def place(core, chip, turn, slots):
    seq = lax.axis_index("seq") ^ (2 * chip + core)
    return seq * slots + lax.rem(lax.axis_index("head") + turn, slots)


def weight_copies(pieces, expand, shrink, sems):
    if len(pieces) == 2:
        return [
            pltpu.make_async_copy(pieces[0], expand, sems.at[0]),
            pltpu.make_async_copy(pieces[1], shrink, sems.at[1]),
        ]
    copies = []
    for r, piece in enumerate(pieces):
        slots = piece.shape[0]
        for a in range(slots):
            source = place(r % 2, r // 2, slots - a, slots)
            n = len(copies)
            copies.append(
                pltpu.make_async_copy(
                    piece.at[a, pl.ds(0, 4)], expand.at[pl.ds(source * 4, 4)], sems.at[n]
                )
            )
            copies.append(
                pltpu.make_async_copy(
                    piece.at[a, pl.ds(4, 4)], shrink.at[:, source], sems.at[n + 1]
                )
            )
    return copies


def grad_copies(expand, shrink, outs, sems):
    if len(outs) == 2 and outs[0].shape == expand.shape:
        return [
            pltpu.make_async_copy(expand, outs[0], sems.at[0]),
            pltpu.make_async_copy(shrink, outs[1], sems.at[1]),
        ]
    copies = []
    for core, out in enumerate(outs):
        for chip in range(out.shape[0]):
            slots = out.shape[1]
            for a in range(slots):
                target = place(core, chip, a, slots)
                n = len(copies)
                copies.append(
                    pltpu.make_async_copy(
                        expand.at[pl.ds(target * 4, 4)], out.at[chip, a, pl.ds(0, 4)], sems.at[n]
                    )
                )
                copies.append(
                    pltpu.make_async_copy(
                        shrink.at[:, target], out.at[chip, a, pl.ds(4, 4)], sems.at[n + 1]
                    )
                )
    return copies


def ffn_kernel(count, residual_ref, vectors_ref, cotangent_ref, *refs):
    pieces = refs[:count]
    result_ref, grad_ref, branch_ref, sums_ref = refs[count : count + 4]
    grads = refs[count + 4 : count + 6]
    (expand_all, shrink_all, expand_grad, shrink_grad, second, normal_ref, rate_ref, total, back,
     gains, bias_row, bias_grads, sems) = refs[count + 6 :]
    k = pl.program_id(0)
    steps = pl.num_programs(0)
    length, width = residual_ref.shape
    devices = vectors_ref.shape[0]
    share = width // devices
    tiles = [slice(r, r + 256) for r in range(0, length, 256)]
    step = expand_all.shape[0] * 16 // 4
    hidden_share = 4 * step // devices

    @pl.when(k == 0)
    def _():
        copies = weight_copies(pieces, expand_all, shrink_all, sems)
        for copy in copies:
            copy.start()
        small = vectors_ref[:, :128]
        for i in range(3):
            gains[i : i + 1, :] = spread(small, (2 + i) * share, share, width)
        wide = spread(vectors_ref[:, 128:], 0, hidden_share, 4 * step)
        for i in range(4):
            bias_row[i, 0:1, :] = wide[:, i * step : (i + 1) * step]
        for rows in tiles:
            normal, rate = norm_parts(residual_ref[rows, :])
            normal_ref[rows, :] = normal
            rate_ref[rows, :] = rate
            second[rows, :] = low(normal * gains[0:1, :] + gains[1:2, :])
            total[rows, :] = residual_ref[rows, :] + gains[2:3, :]
            back[rows, :] = jnp.zeros((256, width), F32)
        for copy in copies:
            copy.wait()

    blocks = step // 16
    expand = expand_all[pl.ds(k * blocks, blocks)].reshape(step, width)
    shrink = shrink_all[k].reshape(width, step)
    bias = bias_row[k][0:1, :]
    bias_grad = jnp.zeros((1, step), F32)
    acts, hids = [], []
    for rows in tiles:
        hidden = nt(second[rows, :], expand) + bias
        pull = nn(cotangent_ref[rows, :], shrink)
        value, slope = gelu_both(hidden)
        activated = low(value)
        hidden_grad = low(pull * slope)
        bias_grad = bias_grad + jnp.sum(hidden_grad.astype(F32), axis=0, keepdims=True)
        total[rows, :] = total[rows, :] + nt(activated, shrink)
        back[rows, :] = back[rows, :] + nn(hidden_grad, expand)
        acts.append(activated)
        hids.append(hidden_grad)
    bias_grads[k, 0:1, :] = bias_grad
    shrink_grad[k] = low(tn(cotangent_ref[...], jnp.concatenate(acts, axis=0))).reshape(
        width // 16, 16, step
    )
    expand_grad[pl.ds(k * blocks, blocks)] = low(
        tn(jnp.concatenate(hids, axis=0), second[...])
    ).reshape(blocks, 16, width)

    @pl.when(k == steps - 1)
    def _():
        copies = grad_copies(expand_grad, shrink_grad, grads, sems)
        for copy in copies:
            copy.start()
        gain = gains[0:1, :]
        gain_grad = jnp.zeros((1, width), F32)
        shift_grad = jnp.zeros((1, width), F32)
        outer = jnp.zeros((1, width), F32)
        for rows in tiles:
            result_ref[rows, :] = low(total[rows, :])
            grad = back[rows, :]
            normal = normal_ref[rows, :]
            upstream = cotangent_ref[rows, :].astype(F32)
            gain_grad = gain_grad + jnp.sum(grad * normal, axis=0, keepdims=True)
            shift_grad = shift_grad + jnp.sum(grad, axis=0, keepdims=True)
            outer = outer + jnp.sum(upstream, axis=0, keepdims=True)
            full = upstream + norm_back(grad, normal, rate_ref[rows, :], gain)
            grad_ref[rows, :] = full
            branch_ref[rows, :] = low(full)
        sums_ref[:, :128] = (
            collect(gain_grad, devices, 2 * share, share)
            + collect(shift_grad, devices, 3 * share, share)
            + collect(outer, devices, 4 * share, share)
        )
        wide = jnp.concatenate([bias_grads[i][0:1, :] for i in range(4)], axis=1)
        sums_ref[:, 128:] = collect(wide, devices, 0, hidden_share)
        for copy in copies:
            copy.wait()


def feed_forward(residual, vectors, cotangent, pieces, grad_shapes, hidden):
    length, width = residual.shape
    step = hidden // 4
    shape = jax.ShapeDtypeStruct
    return pl.pallas_call(
        functools.partial(ffn_kernel, len(pieces)),
        grid=(4,),
        out_shape=[
            shape((length, width), BF16),
            shape((length, width), F32),
            shape((length, width), BF16),
            shape(vectors.shape, F32),
        ]
        + [shape(s, BF16) for s in grad_shapes],
        in_specs=[fixed((length, width)), fixed(vectors.shape), fixed((length, width))]
        + anywhere(pieces),
        out_specs=[fixed((length, width))] * 3 + [fixed(vectors.shape)] + anywhere(grad_shapes),
        scratch_shapes=[
            pltpu.VMEM((hidden // 16, 16, width), BF16),
            pltpu.VMEM((4, width // 16, 16, step), BF16),
            pltpu.VMEM((hidden // 16, 16, width), BF16),
            pltpu.VMEM((4, width // 16, 16, step), BF16),
            pltpu.VMEM((length, width), BF16),
            pltpu.VMEM((length, width), F32),
            pltpu.VMEM((length, 1), F32),
            pltpu.VMEM((length, width), F32),
            pltpu.VMEM((length, width), F32),
            pltpu.VMEM((8, width), F32),
            pltpu.VMEM((4, 8, step), F32),
            pltpu.VMEM((4, 8, step), F32),
            pltpu.SemaphoreType.DMA((max(2, 2 * vectors.shape[0]),)),
        ],
        compiler_params=params(),
        cost_estimate=cost(27),
        name="feed_forward",
    )(residual, vectors, cotangent, *pieces)


def pair_grads(branch_ref, normed_ref, weight_in, weight_out, kept, heads_ref, outs, grad, backs, made):
    grad[...] = low(nt(branch_ref[...], weight_out))
    attend_backward(grad, kept, backs)
    made[:, : 4 * PAIR] = low(tn(normed_ref[...], backs[...]))
    made[:, 4 * PAIR :] = low(tn(branch_ref[...], heads_ref[...]))
    if len(outs) == 1:
        outs[0][...] = made[...]
        return
    seq = lax.axis_index("seq")
    for core, out in enumerate(outs):
        rows = out.shape[1]
        for chip in range(out.shape[0]):
            start = pl.multiple_of((seq ^ (2 * chip + core)) * rows, rows)
            out[chip] = made[pl.ds(start, rows), :]


def back_rest_kernel(count, waits, parts_out, branch_ref, normed_ref, own_ref, *refs):
    pieces, refs = refs[:count], refs[count + waits :]
    kept, heads_ref, refs = refs[:9], refs[9], refs[10:]
    sum_ref, outs = refs[0], refs[1 : 1 + parts_out]
    weight, grad, backs, made = refs[1 + parts_out :]
    width = normed_ref.shape[1]
    fill(weight, own_ref, pieces, pl.program_id(0) + 1)
    pair_grads(
        branch_ref, normed_ref, None, weight[width:, :], kept, heads_ref, outs, grad, backs, made
    )

    @pl.when(pl.program_id(0) == 0)
    def _():
        sum_ref[...] = jnp.zeros_like(sum_ref)

    sum_ref[...] += nt(backs[...], weight[:width, :])


def back_scratch(length, width):
    return [
        pltpu.VMEM((length, PAIR), BF16),
        pltpu.VMEM((length, 4 * PAIR), BF16),
        pltpu.VMEM((width, 5 * PAIR), BF16),
    ]


def later_slots(shapes, first):
    return [
        pl.BlockSpec((None,) + s.shape[1:], lambda a, rank=len(s.shape): (a + first,) + (0,) * (rank - 1))
        for s in shapes
    ]


def anywhere(members):
    return [pl.BlockSpec(memory_space=pl.ANY)] * len(members)


def backward_rest(branch, normed, own, pieces, waits, kept, grad_shapes):
    length, width = branch.shape
    slots = kept[0].shape[0] - 1
    shape = jax.ShapeDtypeStruct
    grads = [shape((slots,) + s, BF16) for s in grad_shapes]
    return pl.pallas_call(
        functools.partial(back_rest_kernel, len(pieces), len(waits), len(grads)),
        grid=(slots,),
        out_shape=[shape((length, width), F32)] + grads,
        in_specs=[fixed(o.shape) for o in (branch, normed, own, *pieces)]
        + anywhere(waits)
        + later_slots(kept, 1),
        out_specs=[fixed((length, width))] + by_slot(grads),
        scratch_shapes=[pltpu.VMEM(own.shape, BF16)] + back_scratch(length, width),
        compiler_params=params(),
        cost_estimate=cost(30),
        name="attend_back_rest",
    )(branch, normed, own, *pieces, *waits, *kept)


def back_first_kernel(waits, parts_out, branch_ref, normed_ref, weight_ref, *refs):
    refs = refs[waits:]
    kept, heads_ref, refs = refs[:9], refs[9], refs[10:]
    backs, outs = refs[0], refs[1 : 1 + parts_out]
    grad, made = refs[1 + parts_out :]
    width = normed_ref.shape[1]
    pair_grads(
        branch_ref, normed_ref, None, weight_ref[width:, :], kept, heads_ref, outs, grad, backs, made
    )


def backward_first(branch, normed, weight, waits, kept):
    length, width = branch.shape
    shape = jax.ShapeDtypeStruct
    outs = [shape((length, 4 * PAIR), BF16), shape((width, 5 * PAIR), BF16)]
    scratch = back_scratch(length, width)
    return pl.pallas_call(
        functools.partial(back_first_kernel, len(waits), 1),
        grid=(1,),
        out_shape=outs,
        in_specs=[fixed(o.shape) for o in (branch, normed, weight)]
        + anywhere(waits)
        + later_slots(kept, 0),
        out_specs=[fixed(o.shape) for o in outs],
        scratch_shapes=[scratch[0], scratch[2]],
        compiler_params=params(),
        cost_estimate=cost(11),
        name="attend_back_first",
    )(branch, normed, weight, *waits, *kept)


def last_kernel(tokens_ref, vectors_ref, backs_ref, weight_ref, total_ref, grad_ref, before_ref, out_ref, sums_ref):
    length, width = tokens_ref.shape
    devices = vectors_ref.shape[0]
    share = width // devices
    gain = spread(vectors_ref[:, :128], 0, share, width)
    gain_grad = jnp.zeros((1, width), F32)
    shift_grad = jnp.zeros((1, width), F32)
    for rows in [slice(r, r + 256) for r in range(0, length, 256)]:
        grad = total_ref[rows, :] + nt(backs_ref[rows, :], weight_ref[:width, :])
        normal, rate = norm_parts(tokens_ref[rows, :].astype(F32))
        gain_grad = gain_grad + jnp.sum(grad * normal, axis=0, keepdims=True)
        shift_grad = shift_grad + jnp.sum(grad, axis=0, keepdims=True)
        out_ref[rows, :] = low(grad_ref[rows, :] + norm_back(grad, normal, rate, gain))
    sums_ref[:, :128] = (
        before_ref[:, :128]
        + collect(gain_grad, devices, 0, share)
        + collect(shift_grad, devices, share, share)
    )
    sums_ref[:, 128:] = before_ref[:, 128:]


def finish(tokens, vectors, backs, weight, total, grad, before):
    shape = jax.ShapeDtypeStruct
    return pl.pallas_call(
        last_kernel,
        out_shape=[shape(tokens.shape, BF16), shape(before.shape, F32)],
        in_specs=vmem(7),
        out_specs=vmem(2),
        compiler_params=params(),
        cost_estimate=cost(5),
        name="norm_back",
    )(tokens, vectors, backs, weight, total, grad, before)


def flip(count, bit):
    return [(i, i ^ bit) for i in range(count)]


def turn(count, by):
    return [(i, (i + by) % count) for i in range(count)]


def add(*members):
    return functools.reduce(lambda a, b: a + b, [m.astype(F32) for m in members])


def across(shares, chips, seqs):
    held = [shares] + [lax.ppermute(shares, "seq", flip(seqs, 2 * r)) for r in range(1, chips)]
    mates = [lax.ppermute(h, "seq", flip(seqs, 1)) for h in held]
    return [member for both in zip(held, mates) for member in both]


def join_cores(keep, send, chips, seqs):
    other = lax.ppermute(send, "seq", flip(seqs, 1))
    made = [add(keep[r], other[r]) for r in range(chips)]
    return made[0], [low(m) for m in made[1:]]


def join_chips(held, sends, seqs):
    came = [lax.ppermute(m, "seq", flip(seqs, 2 * r + 2)) for r, m in enumerate(sends)]
    return add(held, *came)


def body(
    inputs,
    attn_gain,
    attn_shift,
    query_weight,
    key_weight,
    value_weight,
    control_weight,
    output_weight,
    ffn_gain,
    ffn_shift,
    expand_weight,
    expand_bias,
    shrink_weight,
    shrink_bias,
    cotangent,
):
    seqs, slots = lax.axis_size("seq"), lax.axis_size("head")
    devices = seqs * slots
    chips = seqs // 2
    width = inputs.shape[1]
    share = width // devices
    hidden_share = expand_weight.shape[1]
    hidden = hidden_share * devices
    z = lax.axis_index("head")
    direct = share % 16 == 0 and hidden_share == 4 * share and (width + PAIR) % (16 * seqs) == 0

    own = jnp.concatenate(
        [
            jnp.concatenate([query_weight, key_weight, value_weight, control_weight], axis=1),
            output_weight,
        ],
        axis=0,
    )
    small = jnp.concatenate([attn_gain, attn_shift, ffn_gain, ffn_shift, shrink_bias])
    row = jnp.concatenate(
        [
            small,
            jnp.zeros((128 - small.shape[0],), BF16),
            expand_bias,
            jnp.zeros((128 - expand_bias.shape[0],), BF16),
        ]
    )
    expand_t = expand_weight.T
    shrink_t = shrink_weight.T
    vectors = None
    if direct:
        rows = own.shape[0] // seqs
        piece = lax.dynamic_slice_in_dim(own, lax.axis_index("seq") * rows, rows, axis=0)
        block = jnp.pad(row[None, :], ((0, 15), (0, width - 256)))
        piece = jnp.concatenate([piece, block], axis=0)
        came = [lax.ppermute(piece, "head", turn(slots, a)) for a in range(1, slots)]
        pieces = across(jnp.concatenate(came + [block], axis=0), chips, seqs)
        load = jnp.concatenate(
            [expand_t.reshape(4, 16, width)]
            + [shrink_t[None, :, k * width : (k + 1) * width] for k in range(4)],
            axis=0,
        )
        near = jnp.stack([load] + [lax.ppermute(load, "head", turn(slots, a)) for a in range(1, slots)])
        ffn_pieces = across(near, chips, seqs)
        pair_shapes = [(chips, width // seqs, 5 * PAIR)] * 2
        ffn_shapes = [(chips, slots, 8, 16, width)] * 2
    else:
        every = lax.all_gather(own, "head", axis=0, tiled=False)
        pieces = [jnp.concatenate([every[(z + slots - a) % slots] for a in range(1, slots)], axis=0)]
        vectors = lax.all_to_all(
            jnp.broadcast_to(row[None, :], (devices, 256)), ("seq", "head"), 0, 0, tiled=True
        )
        ffn_pieces = [
            lax.all_gather(expand_t, ("seq", "head"), axis=0, tiled=True).reshape(hidden // 16, 16, width),
            lax.all_gather(shrink_t, ("seq", "head"), axis=0, tiled=True)
            .reshape(width // 16, 16, 4, hidden // 4)
            .transpose(2, 0, 1, 3),
        ]
        pair_shapes = [(width, 5 * PAIR)]
        ffn_shapes = [(hidden // 16, 16, width), (4, width // 16, 16, hidden // 4)]

    normed, residual, vectors, kept = forward(inputs, own, pieces, vectors, devices, slots)
    result, residual_grad, branch, sums, *ffn_grads = feed_forward(
        residual, vectors, cotangent, ffn_pieces, ffn_shapes, hidden
    )
    waits, later = [], []
    if direct:
        ffn_held, waits = join_cores(*ffn_grads, chips, seqs)
    total, *rest_grads = backward_rest(branch, normed, own, pieces, waits, kept, pair_shapes)
    if direct:
        ffn_mine = join_chips(ffn_held, waits, seqs)
        ffn_sends = [low(ffn_mine[a]) for a in range(1, slots)]
        rest_held, rest_sends = join_cores(*[jnp.swapaxes(g, 0, 1) for g in rest_grads], chips, seqs)
        later = ffn_sends + rest_sends
    backs, first_grad = backward_first(branch, normed, own, later, kept)
    input_grad, sums = finish(inputs, vectors, backs, own, total, residual_grad, sums)

    if direct:
        first_all = lax.all_to_all(first_grad, "seq", 0, 0, tiled=True)
        ffn_came = [lax.ppermute(m, "head", turn(slots, a + 1)) for a, m in enumerate(ffn_sends)]
        ffn_sum = add(ffn_mine[0], *ffn_came)
        expand_grad = ffn_sum[:4].reshape(hidden_share, width)
        shrink_grad = jnp.concatenate([ffn_sum[4 + k] for k in range(4)], axis=1)
        rest = join_chips(rest_held, rest_sends, seqs)
        rest_came = [
            lax.ppermute(low(rest[a - 1]), "head", turn(slots, slots - a)) for a in range(1, slots)
        ]
        first_all = first_all.reshape((seqs,) + rest.shape[1:])
        pair_sum = add(*[first_all[i] for i in range(seqs)], *rest_came)
    else:
        expand_grad = lax.psum_scatter(
            ffn_grads[0].reshape(hidden, width).astype(F32), ("seq", "head"), scatter_dimension=0, tiled=True
        )
        shrink_grad = lax.psum_scatter(
            ffn_grads[1].transpose(1, 2, 0, 3).reshape(width, hidden).astype(F32),
            ("seq", "head"),
            scatter_dimension=0,
            tiled=True,
        )
        every = jnp.concatenate([first_grad[None], rest_grads[0]], axis=0).astype(F32)
        every = jnp.stack([every[(z + slots - p) % slots] for p in range(slots)])
        pair_sum = lax.psum_scatter(every, "head", scatter_dimension=0, tiled=False)
        pair_sum = lax.psum_scatter(pair_sum, "seq", scatter_dimension=0, tiled=True)

    sums = jnp.sum(lax.all_to_all(sums, ("seq", "head"), 0, 0, tiled=True), axis=0)
    vector = [sums[i * share : (i + 1) * share] for i in range(5)]
    return (
        result,
        input_grad,
        vector[0],
        vector[1],
        pair_sum[:, :PAIR],
        pair_sum[:, PAIR : 2 * PAIR],
        pair_sum[:, 2 * PAIR : 3 * PAIR],
        pair_sum[:, 3 * PAIR : 4 * PAIR],
        pair_sum[:, 4 * PAIR :].T,
        vector[2],
        vector[3],
        expand_grad.T,
        sums[128 : 128 + hidden_share],
        shrink_grad.T,
        vector[4],
    )


def solution(mesh):
    placed = (
        P(("seq", "head"), None),
        P(("seq", "head")),
        P(("seq", "head")),
        P(None, "head"),
        P(None, "head"),
        P(None, "head"),
        P(None, "head"),
        P("head", None),
        P(("seq", "head")),
        P(("seq", "head")),
        P(None, ("seq", "head")),
        P(("seq", "head")),
        P(None, ("seq", "head")),
        P(("seq", "head")),
        P(("seq", "head"), None),
    )
    return jax.shard_map(
        body,
        mesh=mesh,
        in_specs=placed,
        out_specs=(
            P(("seq", "head"), None),
            P(("seq", "head"), None),
            P(("seq", "head")),
            P(("seq", "head")),
            P("seq", "head"),
            P("seq", "head"),
            P("seq", "head"),
            P("seq", "head"),
            P("head", "seq"),
            P(("seq", "head")),
            P(("seq", "head")),
            P(None, ("seq", "head")),
            P(("seq", "head")),
            P(None, ("seq", "head")),
            P(("seq", "head")),
        ),
        check_vma=False,
    )
```

```python
import functools

import jax
import jax.numpy as jnp
from jax import lax
from jax.experimental import pallas as pl
from jax.experimental.pallas import tpu as pltpu
from jax.sharding import PartitionSpec as P

EPSILON = 1e-5
CHUNK = 128
PAIR = 128
F32 = jnp.float32
BF16 = jnp.bfloat16
LIMIT = 56 * 1024 * 1024


def nn(a, b):
    return lax.dot_general(a, b, (((1,), (0,)), ((), ())), preferred_element_type=F32)


def nt(a, b):
    return lax.dot_general(a, b, (((1,), (1,)), ((), ())), preferred_element_type=F32)


def tn(a, b):
    return lax.dot_general(a, b, (((0,), (0,)), ((), ())), preferred_element_type=F32)


def low(v):
    return v.astype(BF16)


def iota(shape, axis):
    return lax.broadcasted_iota(jnp.int32, shape, axis)


def first_half(shape):
    return iota(shape, 1) < PAIR // 2


def stacked(block):
    left = first_half(block.shape)
    zero = jnp.zeros_like(block)
    return jnp.concatenate([jnp.where(left, block, zero), jnp.where(left, zero, block)], axis=0)


def parts(v):
    high = low(v)
    return jnp.concatenate([high, low(v - high.astype(F32))], axis=1)


def whole(v):
    return v[:, :PAIR] + v[:, PAIR:]


def head_block(shape=(PAIR, PAIR)):
    return (iota(shape, 0) < PAIR // 2) == (iota(shape, 1) < PAIR // 2)


def causal_pair():
    return iota((CHUNK, 2 * CHUNK), 0) >= (iota((CHUNK, 2 * CHUNK), 1) & (CHUNK - 1))


def causal_pair_t():
    return iota((CHUNK, 2 * CHUNK), 0) <= (iota((CHUNK, 2 * CHUNK), 1) & (CHUNK - 1))


def ones_where(mask):
    return low(jnp.where(mask, 1.0, 0.0))


def norm_parts(tokens):
    average = jnp.mean(tokens, axis=-1, keepdims=True)
    centred = tokens - average
    rate = lax.rsqrt(jnp.mean(centred * centred, axis=-1, keepdims=True) + EPSILON)
    return centred * rate, rate


def norm_back(grad, normal, rate, gain):
    w = grad * gain
    return rate * (
        w
        - jnp.mean(w, axis=-1, keepdims=True)
        - normal * jnp.mean(w * normal, axis=-1, keepdims=True)
    )


def chunks(length):
    return [slice(c * CHUNK, (c + 1) * CHUNK) for c in range(length // CHUNK)]


def attend_forward(normed, weight, keep):
    q_ref, k_ref, v_ref, powers_ref, inverse_ref, score_ref, prob_ref, key_state, value_state, heads_ref = keep
    length = normed.shape[0]
    cuts = chunks(length)
    for rows in [slice(r, r + 256) for r in range(0, length, 256)]:
        made = nn(normed[rows, :], weight)
        q_ref[rows, :] = low(low(made[:, :PAIR]).astype(F32) * 0.125)
        k_ref[rows, :] = low(made[:, PAIR : 2 * PAIR])
        v_ref[rows, :] = low(made[:, 2 * PAIR : 3 * PAIR])
        powers_ref[rows, :] = jnp.exp(made[:, 3 * PAIR :])
    tri = ones_where(iota((CHUNK, CHUNK), 0) >= iota((CHUNK, CHUNK), 1))
    same = head_block()
    both = jnp.concatenate([ones_where(same)] * 2, axis=0)
    causal = causal_pair()
    carried = jnp.zeros((1, PAIR), F32)
    local = [whole(nn(tri, parts(powers_ref[rows, :]))) for rows in cuts]
    for rows, sums in zip(cuts, local):
        running = sums + carried
        carried = running[CHUNK - 1 :, :]
        inverse_ref[rows, :] = 1.0 / running
    key_sum = jnp.zeros((PAIR, PAIR), F32)
    value_sum = jnp.zeros((PAIR, PAIR), F32)
    for c, rows in enumerate(cuts):
        key_state[c, :, :] = low(jnp.where(same, key_sum, 0.0))
        value_state[c, :, :] = low(jnp.where(same, value_sum, 0.0))
        if c + 1 < len(cuts):
            powers_low = low(powers_ref[rows, :])
            key_sum = key_sum + tn(k_ref[rows, :], powers_low)
            value_sum = value_sum + tn(powers_low, v_ref[rows, :])
    left = first_half((CHUNK, PAIR))
    scored = [
        low(jnp.where(causal, nt(q_ref[rows, :], stacked(k_ref[rows, :])), 0.0)) for rows in cuts
    ]
    for c, rows in enumerate(cuts):
        summed = nn(scored[c], stacked(low(powers_ref[rows, :]))) + nn(q_ref[rows, :], key_state[c, :, :])
        score_ref[rows, :] = summed * inverse_ref[rows, :]
    for c, rows in enumerate(cuts):
        score = score_ref[rows, :]
        top_a = jnp.max(jnp.where(left, score, -jnp.inf), axis=-1, keepdims=True)
        top_b = jnp.max(jnp.where(left, -jnp.inf, score), axis=-1, keepdims=True)
        lifted = jnp.exp(score - jnp.where(left, top_a, top_b))
        prob_ref[rows, :] = lifted / nn(parts(lifted), both)
    reading = [low(prob_ref[rows, :] * inverse_ref[rows, :]) for rows in cuts]
    mixing = [
        low(jnp.where(causal, nt(reading[c], stacked(low(powers_ref[rows, :]))), 0.0))
        for c, rows in enumerate(cuts)
    ]
    for c, rows in enumerate(cuts):
        heads_ref[rows, :] = low(
            nn(mixing[c], stacked(v_ref[rows, :])) + nn(reading[c], value_state[c, :, :])
        )


def attend_backward(heads_grad, kept, backs):
    q_ref, k_ref, v_ref, powers_ref, inverse_ref, score_ref, prob_ref, key_state, value_state = kept
    cuts = chunks(heads_grad.shape[0])
    same = head_block()
    both = jnp.concatenate([ones_where(same)] * 2, axis=0)
    causal = causal_pair()
    causal_t = causal_pair_t()
    tri_t = ones_where(iota((CHUNK, CHUNK), 0) <= iota((CHUNK, CHUNK), 1))
    after = jnp.zeros((1, PAIR), F32)
    read_sum = jnp.zeros((PAIR, PAIR), F32)
    score_sum = jnp.zeros((PAIR, PAIR), F32)
    for c in reversed(range(len(cuts))):
        rows = cuts[c]
        q, k, v = q_ref[rows, :], k_ref[rows, :], v_ref[rows, :]
        grad = heads_grad[rows, :]
        inverse = inverse_ref[rows, :]
        prob = prob_ref[rows, :]
        powers = powers_ref[rows, :]
        powers_low = low(powers)
        reading = low(prob * inverse)
        powers_two, values_two, keys_two = stacked(powers_low), stacked(v), stacked(k)
        queries_two, grad_two, reading_two = stacked(q), stacked(grad), stacked(reading)
        read_state = low(jnp.where(same, read_sum, 0.0))
        score_state = low(jnp.where(same, score_sum, 0.0))
        mixing_t = low(jnp.where(causal_t, nt(powers_low, reading_two), 0.0))
        mixing_grad = low(jnp.where(causal, nt(grad, values_two), 0.0))
        mixing_grad_t = low(jnp.where(causal_t, nt(v, grad_two), 0.0))
        scored_t = low(jnp.where(causal_t, nt(k, queries_two), 0.0))
        values_grad = nn(mixing_t, grad_two) + nn(powers_low, read_state)
        reading_grad = nn(mixing_grad, powers_two) + nt(grad, value_state[c, :, :])
        powers_grad = nn(mixing_grad_t, reading_two) + nt(v, read_state)
        prob_grad = reading_grad * inverse
        weighed = prob * prob_grad
        slots_grad = weighed - prob * nn(parts(weighed), both)
        running_grad = -inverse * (weighed + slots_grad * score_ref[rows, :])
        summed_grad = low(slots_grad * inverse)
        summed_two = stacked(summed_grad)
        scored_grad = low(jnp.where(causal, nt(summed_grad, powers_two), 0.0))
        scored_grad_t = low(jnp.where(causal_t, nt(powers_low, summed_two), 0.0))
        powers_grad = powers_grad + nn(scored_t, summed_two) + nn(k, score_state)
        backs[rows, :PAIR] = low(
            0.125 * (nn(scored_grad, keys_two) + nt(summed_grad, key_state[c, :, :]))
        )
        backs[rows, PAIR : 2 * PAIR] = low(
            nn(scored_grad_t, queries_two) + nt(powers_low, score_state)
        )
        backs[rows, 2 * PAIR : 3 * PAIR] = low(values_grad)
        later = whole(nn(tri_t, parts(running_grad))) + after
        after = later[:1, :]
        backs[rows, 3 * PAIR :] = low((powers_grad + later) * powers)
        if c:
            read_sum = read_sum + tn(reading, grad)
            score_sum = score_sum + tn(q, summed_grad)


def kept_shapes(length, lead=()):
    n = length // CHUNK
    shape = jax.ShapeDtypeStruct
    return (
        [shape(lead + (length, PAIR), BF16)] * 3
        + [shape(lead + (length, PAIR), F32)] * 4
        + [shape(lead + (n, PAIR, PAIR), BF16)] * 2
        + [shape(lead + (length, PAIR), BF16)]
    )


def by_slot(shapes):
    return [
        pl.BlockSpec((None,) + s.shape[1:], lambda a, rank=len(s.shape): (a,) + (0,) * (rank - 1))
        for s in shapes
    ]


def fixed(shape):
    return pl.BlockSpec(shape, lambda a: (0,) * len(shape))


def cost(micros):
    return pl.CostEstimate(flops=int(micros * 1e9), bytes_accessed=int(micros * 1e6), transcendentals=0)


def params():
    return pltpu.CompilerParams(vmem_limit_bytes=LIMIT)


def select(width, offset, share, total):
    return ones_where(
        iota((width, total), 0) == offset + (iota((width, total), 1) & (share - 1))
    )


def owned(devices, share, total):
    return iota((devices, total), 0) == lax.shift_right_logical(
        iota((devices, total), 1), share.bit_length() - 1
    )


def spread(rows, offset, share, total):
    each = nn(rows, select(rows.shape[1], offset, share, total))
    return jnp.sum(jnp.where(owned(rows.shape[0], share, total), each, 0.0), axis=0, keepdims=True)


def collect(row, devices, offset, share):
    total = row.shape[1]
    rest = jnp.where(owned(devices, share, total), row, 0.0)
    chosen = select(128, offset, share, total)
    out = jnp.zeros((devices, 128), F32)
    for _ in range(3):
        part = low(rest)
        out = out + nt(part, chosen)
        rest = rest - part.astype(F32)
    return out


def own_device(core, chip, z, slots):
    return (lax.axis_index("seq") ^ (2 * chip + core)) * slots + z


def turned(by, slots):
    return lax.rem(lax.axis_index("head") + by, slots)


def fill(weight, own_ref, pieces, slot):
    @pl.when(slot == 0)
    def _():
        weight[...] = own_ref[...]

    if len(pieces) == 1:
        rows = weight.shape[0]

        @pl.when(slot > 0)
        def _():
            weight[...] = pieces[0][pl.ds(pl.multiple_of((slot - 1) * rows, 16), rows), :]

        return
    rows = weight.shape[0] // 8
    mine = lax.axis_index("seq")
    for a in range(1, 4):

        @pl.when(slot == a)
        def _(a=a):
            for core in range(2):
                low_a, low_b, a_x, b_y, a_y, b_x = pieces[6 * core : 6 * core + 6]
                if a < 3:
                    n, start = 2 * rows, (a - 1) * rows
                    parts = [(low_a, 0), (a_x, 0), (a_y, 0), (a_y, n)]
                else:
                    n, start = low_b.shape[0], 0
                    parts = [(low_b, 0), (b_x, 0), (b_y, 0), (b_x, n)]
                for chip, (piece, offset) in enumerate(parts):
                    source = pl.multiple_of((mine ^ (2 * chip + core)) * rows, 16)
                    first = offset + start
                    weight[pl.ds(source, rows), :] = piece[first : first + rows, :]


def gather_vectors(pieces, rows, slots, vectors, staged):
    for core in range(2):
        _, low_b, _, b_y, _, b_x = pieces[6 * core : 6 * core + 6]
        n = low_b.shape[0]
        for chip, (piece, offset) in enumerate([(low_b, 0), (b_x, 0), (b_y, 0), (b_x, n)]):
            for a in range(slots):
                first = offset + rows + 16 * ((a + slots - 1) % slots)
                source = own_device(core, chip, turned(slots - a, slots), slots)
                staged[pl.ds(source, 1), :] = piece[first : first + 16, :256].astype(F32)[0:1, :]
    vectors[...] = low(staged[...])


def forward_kernel(count, slots, tokens_ref, own_ref, *refs):
    pieces, refs = refs[:count], refs[count:]
    if count == 1:
        given, refs = refs[0], refs[1:]
    normed_ref, residual_ref, vectors_ref, weight, keep = refs[0], refs[1], refs[2], refs[3], refs[4:-1]
    staged = refs[-1]
    slot = pl.program_id(0)
    length, width = tokens_ref.shape
    share = width // vectors_ref.shape[0]

    @pl.when(slot == 0)
    def _():
        if count == 1:
            vectors_ref[...] = given[...]
        else:
            gather_vectors(pieces, own_ref.shape[0] // 8, slots, vectors_ref, staged)
        small = vectors_ref[:, :128]
        gain = spread(small, 0, share, width)
        shift = spread(small, share, share, width)
        for rows in [slice(r, r + 256) for r in range(0, length, 256)]:
            tokens = tokens_ref[rows, :].astype(F32)
            normal, _ = norm_parts(tokens)
            normed_ref[rows, :] = low(normal * gain + shift)
            residual_ref[rows, :] = tokens

    fill(weight, own_ref, pieces, slot)
    attend_forward(normed_ref, weight[:width, :], keep)
    residual_ref[...] += nn(keep[-1][...], weight[width:, :])


def forward(tokens, own, pieces, vectors, devices, slots):
    length, width = tokens.shape
    shape = jax.ShapeDtypeStruct
    stacked_outs = [shape((slots,) + own.shape, BF16)] + kept_shapes(length, (slots,))
    given = [] if vectors is None else [vectors]
    operands = [tokens, own, *pieces, *given]
    outs = [shape((length, width), BF16), shape((length, width), F32), shape((devices, 256), BF16)]
    made = pl.pallas_call(
        functools.partial(forward_kernel, len(pieces), slots),
        grid=(slots,),
        out_shape=outs + stacked_outs,
        in_specs=[fixed(o.shape) for o in operands],
        out_specs=[fixed(o.shape) for o in outs] + by_slot(stacked_outs),
        scratch_shapes=[pltpu.VMEM((devices, 256), F32)],
        compiler_params=params(),
        cost_estimate=cost(16),
        name="attend_forward",
    )(*operands)
    return made[0], made[1], made[2], made[3], made[4:]


GELU_A = 0.7978845608028654
GELU_B = 0.044715


def gelu_both(u):
    square = u * u
    bend = jnp.tanh(GELU_A * (u + GELU_B * (square * u)))
    half = 0.5 * (1.0 + bend)
    slope = half + 0.5 * u * (1.0 - bend * bend) * (GELU_A * (1.0 + 3.0 * GELU_B * square))
    return u * half, slope


def weight_copies(pieces, weights, sems):
    if len(pieces) == 1:
        return [pltpu.make_async_copy(pieces[0], weights, sems.at[0])]
    copies = []
    for core in range(2):
        low_a, low_b, a_x, b_y, a_y, b_x = pieces[6 * core : 6 * core + 6]
        slots = low_a.shape[0]
        halves = [
            [low_a, a_x, a_y.at[0], a_y.at[1]],
            [low_b, b_x.at[0], b_y, b_x.at[1]],
        ]
        for half in range(2):
            for chip in range(4):
                for a in range(slots):
                    source = own_device(core, chip, turned(slots - a, slots), slots)
                    copies.append(
                        pltpu.make_async_copy(
                            halves[half][chip].at[a],
                            weights.at[pl.ds(2 * half, 2), :, source],
                            sems.at[len(copies)],
                        )
                    )
    return copies


def grad_copies(grads, outs, sems):
    if len(outs) == 1:
        return [pltpu.make_async_copy(grads, outs[0], sems.at[0])]
    copies = []
    for core, out in enumerate(outs):
        chips, slots = out.shape[:2]
        for chip in range(chips):
            for z in range(slots):
                target = own_device(core, chip, z, slots)
                copies.append(
                    pltpu.make_async_copy(
                        grads.at[:, :, target], out.at[chip, z], sems.at[len(copies)]
                    )
                )
    return copies


def ffn_kernel(count, residual_ref, vectors_ref, cotangent_ref, *refs):
    pieces = refs[:count]
    result_ref, grad_ref, branch_ref, sums_ref = refs[count : count + 4]
    outs = refs[count + 4 : -11]
    (weights, grads, second, normal_ref, rate_ref, total, back, gains, bias_row, bias_grads, sems) = refs[-11:]
    k = pl.program_id(0)
    length, width = residual_ref.shape
    devices = vectors_ref.shape[0]
    share = width // devices
    tiles = [slice(r, r + 256) for r in range(0, length, 256)]

    @pl.when(k == 0)
    def _():
        copies = weight_copies(pieces, weights, sems)
        for copy in copies:
            copy.start()
        small, wide = vectors_ref[:, :128], vectors_ref[:, 128:]
        for i in range(3):
            gains[i : i + 1, :] = spread(small, (2 + i) * share, share, width)
        for i in range(4):
            bias_row[i, 0:1, :] = spread(wide, i * share, share, width)
        for rows in tiles:
            normal, rate = norm_parts(residual_ref[rows, :])
            normal_ref[rows, :] = normal
            rate_ref[rows, :] = rate
            second[rows, :] = low(normal * gains[0:1, :] + gains[1:2, :])
            total[rows, :] = residual_ref[rows, :] + gains[2:3, :]
            back[rows, :] = jnp.zeros((256, width), F32)
        for copy in copies:
            copy.wait()

    expand = weights[k, 0].reshape(width, width)
    shrink = weights[k, 1].reshape(width, width)
    bias = bias_row[k][0:1, :]
    bias_grad = jnp.zeros((1, width), F32)
    acts, hids = [], []
    for rows in tiles:
        hidden = nt(second[rows, :], expand) + bias
        pull = nn(cotangent_ref[rows, :], shrink)
        value, slope = gelu_both(hidden)
        activated = low(value)
        hidden_grad = low(pull * slope)
        bias_grad = bias_grad + jnp.sum(hidden_grad.astype(F32), axis=0, keepdims=True)
        total[rows, :] = total[rows, :] + nt(activated, shrink)
        back[rows, :] = back[rows, :] + nn(hidden_grad, expand)
        acts.append(activated)
        hids.append(hidden_grad)
    bias_grads[k, 0:1, :] = bias_grad
    grads[k, 1] = low(tn(cotangent_ref[...], jnp.concatenate(acts, axis=0))).reshape(
        width // 16, 16, width
    )
    grads[k, 0] = low(tn(jnp.concatenate(hids, axis=0), second[...])).reshape(width // 16, 16, width)

    @pl.when(k == 3)
    def _():
        copies = grad_copies(grads, outs, sems)
        for copy in copies:
            copy.start()
        gain = gains[0:1, :]
        gain_grad = jnp.zeros((1, width), F32)
        shift_grad = jnp.zeros((1, width), F32)
        outer = jnp.zeros((1, width), F32)
        for rows in tiles:
            result_ref[rows, :] = low(total[rows, :])
            grad = back[rows, :]
            normal = normal_ref[rows, :]
            upstream = cotangent_ref[rows, :].astype(F32)
            gain_grad = gain_grad + jnp.sum(grad * normal, axis=0, keepdims=True)
            shift_grad = shift_grad + jnp.sum(grad, axis=0, keepdims=True)
            outer = outer + jnp.sum(upstream, axis=0, keepdims=True)
            full = upstream + norm_back(grad, normal, rate_ref[rows, :], gain)
            grad_ref[rows, :] = full
            branch_ref[rows, :] = low(full)
        sums_ref[:, :128] = (
            collect(gain_grad, devices, 2 * share, share)
            + collect(shift_grad, devices, 3 * share, share)
            + collect(outer, devices, 4 * share, share)
        )
        sums_ref[:, 128:] = functools.reduce(
            lambda a, b: a + b,
            [collect(bias_grads[i][0:1, :], devices, i * share, share) for i in range(4)],
        )
        for copy in copies:
            copy.wait()


def feed_forward(residual, vectors, cotangent, pieces, grad_shapes):
    length, width = residual.shape
    shape = jax.ShapeDtypeStruct
    weights = (4, 2, width // 16, 16, width)
    return pl.pallas_call(
        functools.partial(ffn_kernel, len(pieces)),
        grid=(4,),
        out_shape=[
            shape((length, width), BF16),
            shape((length, width), F32),
            shape((length, width), BF16),
            shape(vectors.shape, F32),
        ]
        + [shape(s, BF16) for s in grad_shapes],
        in_specs=[fixed((length, width)), fixed(vectors.shape), fixed((length, width))] + anywhere(pieces),
        out_specs=[fixed((length, width))] * 3 + [fixed(vectors.shape)] + anywhere(grad_shapes),
        scratch_shapes=[
            pltpu.VMEM(weights, BF16),
            pltpu.VMEM(weights, BF16),
            pltpu.VMEM((length, width), BF16),
            pltpu.VMEM((length, width), F32),
            pltpu.VMEM((length, 1), F32),
            pltpu.VMEM((length, width), F32),
            pltpu.VMEM((length, width), F32),
            pltpu.VMEM((8, width), F32),
            pltpu.VMEM((4, 8, width), F32),
            pltpu.VMEM((4, 8, width), F32),
            pltpu.SemaphoreType.DMA((64,)),
        ],
        compiler_params=params(),
        cost_estimate=cost(26),
        name="feed_forward",
    )(residual, vectors, cotangent, *pieces)


def heads_kernel(branch_ref, weight_ref, heads_ref, grad_ref, output_grad_ref):
    grad_ref[...] = low(nt(branch_ref[...], weight_ref[...]))
    output_grad_ref[...] = low(tn(branch_ref[...], heads_ref[...]))


def heads_back(branch, weights, heads):
    slots, length, pair = heads.shape
    width = branch.shape[1]
    shape = jax.ShapeDtypeStruct
    outs = [shape((slots, length, pair), BF16), shape((slots, width, pair), BF16)]
    last = width // pair
    return pl.pallas_call(
        heads_kernel,
        grid=(slots,),
        out_shape=outs,
        in_specs=[
            fixed((length, width)),
            pl.BlockSpec((None, pair, width), lambda a: (a, last, 0)),
        ]
        + by_slot([heads]),
        out_specs=by_slot(outs),
        compiler_params=params(),
        cost_estimate=cost(4),
        name="heads_back",
    )(branch, weights, heads)


def later_slots(shapes, first):
    return [
        pl.BlockSpec((None,) + s.shape[1:], lambda a, rank=len(s.shape): (a + first,) + (0,) * (rank - 1))
        for s in shapes
    ]


def anywhere(members):
    return [pl.BlockSpec(memory_space=pl.ANY)] * len(members)


def pair_grads(grad_ref, output_grad_ref, normed_ref, kept, outs, backs, made):
    attend_backward(grad_ref, kept, backs)
    made[:, : 4 * PAIR] = low(tn(normed_ref[...], backs[...]))
    made[:, 4 * PAIR :] = output_grad_ref[...]
    if len(outs) == 1:
        outs[0][...] = made[...]
        return
    seq = lax.axis_index("seq")
    for core, out in enumerate(outs):
        rows = out.shape[1]
        for chip in range(out.shape[0]):
            start = pl.multiple_of((seq ^ (2 * chip + core)) * rows, rows)
            out[chip] = made[pl.ds(start, rows), :]


def back_rest_kernel(waits, parts_out, normed_ref, *refs):
    refs = refs[waits:]
    weight, grad_ref, output_grad_ref, kept, refs = refs[0], refs[1], refs[2], refs[3:12], refs[12:]
    sum_ref, outs = refs[0], refs[1 : 1 + parts_out]
    backs, made = refs[1 + parts_out :]
    width = normed_ref.shape[1]
    pair_grads(grad_ref, output_grad_ref, normed_ref, kept, outs, backs, made)

    @pl.when(pl.program_id(0) == 0)
    def _():
        sum_ref[...] = jnp.zeros_like(sum_ref)

    sum_ref[...] += nt(backs[...], weight[:width, :])


def backward_rest(normed, waits, members, grad_shapes):
    length, width = normed.shape
    slots = members[0].shape[0] - 1
    shape = jax.ShapeDtypeStruct
    grads = [shape(s[:-2] + (slots,) + s[-2:], BF16) for s in grad_shapes]
    if len(grads) == 2:
        grad_specs = [
            pl.BlockSpec((g.shape[0], None) + g.shape[2:], lambda a: (0, a, 0, 0)) for g in grads
        ]
    else:
        grad_specs = by_slot(grads)
    return pl.pallas_call(
        functools.partial(back_rest_kernel, len(waits), len(grads)),
        grid=(slots,),
        out_shape=[shape((length, width), F32)] + grads,
        in_specs=[fixed(normed.shape)] + anywhere(waits) + later_slots(members, 1),
        out_specs=[fixed((length, width))] + grad_specs,
        scratch_shapes=[pltpu.VMEM((length, 4 * PAIR), BF16), pltpu.VMEM((width, 5 * PAIR), BF16)],
        compiler_params=params(),
        cost_estimate=cost(28),
        name="attend_back_rest",
    )(normed, *waits, *members)


def back_first_kernel(waits, parts_out, normed_ref, tokens_ref, vectors_ref, total_ref, residual_grad_ref, before_ref, *refs):
    refs = refs[waits:]
    weight, grad_ref, output_grad_ref, kept, refs = refs[0], refs[1], refs[2], refs[3:12], refs[12:]
    input_grad_ref, sums_ref, outs = refs[0], refs[1], refs[2 : 2 + parts_out]
    backs, made = refs[2 + parts_out :]
    length, width = normed_ref.shape
    devices = vectors_ref.shape[0]
    share = width // devices
    pair_grads(grad_ref, output_grad_ref, normed_ref, kept, outs, backs, made)
    gain = spread(vectors_ref[:, :128], 0, share, width)
    gain_grad = jnp.zeros((1, width), F32)
    shift_grad = jnp.zeros((1, width), F32)
    for rows in [slice(r, r + 256) for r in range(0, length, 256)]:
        grad = total_ref[rows, :] + nt(backs[rows, :], weight[:width, :])
        normal, rate = norm_parts(tokens_ref[rows, :].astype(F32))
        gain_grad = gain_grad + jnp.sum(grad * normal, axis=0, keepdims=True)
        shift_grad = shift_grad + jnp.sum(grad, axis=0, keepdims=True)
        input_grad_ref[rows, :] = low(residual_grad_ref[rows, :] + norm_back(grad, normal, rate, gain))
    sums_ref[...] = jnp.zeros_like(sums_ref)
    sums_ref[:, 0, :] = (
        before_ref[:, :128]
        + collect(gain_grad, devices, 0, share)
        + collect(shift_grad, devices, share, share)
    )
    sums_ref[:, 1, :] = before_ref[:, 128:]


def backward_first(normed, tokens, vectors, total, residual_grad, before, waits, members, grad_shapes):
    length, width = normed.shape
    shape = jax.ShapeDtypeStruct
    operands = (normed, tokens, vectors, total, residual_grad, before)
    outs = [shape((length, width), BF16), shape((before.shape[0], 8, 128), F32)]
    outs += [shape(s, BF16) for s in grad_shapes]
    return pl.pallas_call(
        functools.partial(back_first_kernel, len(waits), len(grad_shapes)),
        grid=(1,),
        out_shape=outs,
        in_specs=[fixed(o.shape) for o in operands] + anywhere(waits) + later_slots(members, 0),
        out_specs=[fixed(o.shape) for o in outs],
        scratch_shapes=[pltpu.VMEM((length, 4 * PAIR), BF16), pltpu.VMEM((width, 5 * PAIR), BF16)],
        compiler_params=params(),
        cost_estimate=cost(14),
        name="attend_back_first",
    )(*operands, *waits, *members)


def flip(count, bit):
    return [(i, i ^ bit) for i in range(count)]


def turn(count, by):
    return [(i, (i + by) % count) for i in range(count)]


def add(*members):
    return functools.reduce(lambda a, b: a + b, [m.astype(F32) for m in members])


def across(part_a, part_b, join, seqs):
    def send(v, bit):
        return lax.ppermute(v, "seq", flip(seqs, bit))

    a_x, b_y = send(part_a, 2), send(part_b, 4)
    held = [part_a, part_b, a_x, b_y, send(join(part_a, a_x), 4), send(join(part_b, b_y), 2)]
    return held + [send(h, 1) for h in held]


def join_cores(keep, send, chips, seqs):
    other = lax.ppermute(send, "seq", flip(seqs, 1))
    made = [add(keep[r], other[r]) for r in range(chips)]
    return made[0], [low(m) for m in made[1:]]


def join_chips(held, sends, seqs):
    came = [lax.ppermute(m, "seq", flip(seqs, 2 * r + 2)) for r, m in enumerate(sends)]
    return add(held, *came)


def body(
    inputs,
    attn_gain,
    attn_shift,
    query_weight,
    key_weight,
    value_weight,
    control_weight,
    output_weight,
    ffn_gain,
    ffn_shift,
    expand_weight,
    expand_bias,
    shrink_weight,
    shrink_bias,
    cotangent,
):
    seqs, slots = lax.axis_size("seq"), lax.axis_size("head")
    devices = seqs * slots
    chips = seqs // 2
    width = inputs.shape[1]
    share = width // devices
    hidden_share = expand_weight.shape[1]
    z = lax.axis_index("head")
    direct = seqs == 8 and slots == 4 and share == 16 and hidden_share == 4 * share

    own = jnp.concatenate(
        [
            jnp.concatenate([query_weight, key_weight, value_weight, control_weight], axis=1),
            output_weight,
        ],
        axis=0,
    )
    places = [(attn_gain, 0), (attn_shift, 1), (ffn_gain, 2), (ffn_shift, 3), (shrink_bias, 4)]
    row = jnp.pad(expand_bias, (128, 128 - hidden_share))
    for member, i in places:
        row = row + jnp.pad(member, (i * share, 256 - (i + 1) * share))
    vectors = None
    expand_t = expand_weight.T.reshape(4, share, width)
    shrink_t = shrink_weight.reshape(devices, 4, share, share).transpose(1, 3, 0, 2).reshape(4, share, width)
    if direct:
        rows = own.shape[0] // seqs
        piece = lax.dynamic_slice_in_dim(own, lax.axis_index("seq") * rows, rows, axis=0)
        block = jnp.pad(row[None, :], ((0, 15), (0, width - 256)))
        piece = jnp.concatenate([piece, block], axis=0)
        came = [lax.ppermute(piece, "head", turn(slots, a)) for a in range(1, slots)]
        part_a = jnp.concatenate([came[0][:rows], came[1][:rows]], axis=0)
        part_b = jnp.concatenate([came[2][:rows]] + [c[rows:] for c in came] + [block], axis=0)
        pieces = across(part_a, part_b, lambda *m: jnp.concatenate(m, axis=0), seqs)
        load = jnp.stack([expand_t, shrink_t], axis=1)
        came = [load] + [lax.ppermute(load, "head", turn(slots, a)) for a in range(1, slots)]
        ffn_pieces = across(
            jnp.stack([c[:2] for c in came]), jnp.stack([c[2:] for c in came]), lambda *m: jnp.stack(m), seqs
        )
        pair_shapes = [(chips, width // seqs, 5 * PAIR)] * 2
        ffn_shapes = [(chips, slots, 4, 2, 16, width)] * 2
    else:
        every = lax.all_gather(own, "head", axis=0, tiled=False)
        pieces = [jnp.concatenate([every[(z + slots - a) % slots] for a in range(1, slots)], axis=0)]
        vectors = lax.all_to_all(
            jnp.broadcast_to(row[None, :], (devices, 256)), ("seq", "head"), 0, 0, tiled=True
        )
        both = lax.all_gather(jnp.stack([expand_t, shrink_t], axis=1), ("seq", "head"), axis=2, tiled=True)
        ffn_pieces = [both.reshape(4, 2, width // 16, 16, width)]
        pair_shapes = [(width, 5 * PAIR)]
        ffn_shapes = [ffn_pieces[0].shape]

    normed, residual, vectors, weights, kept = forward(inputs, own, pieces, vectors, devices, slots)
    kept, heads = kept[:-1], kept[-1]
    result, residual_grad, branch, sums, *ffn_grads = feed_forward(
        residual, vectors, cotangent, ffn_pieces, ffn_shapes
    )
    heads_grad, output_grad = heads_back(branch, weights, heads)
    members = [weights, heads_grad, output_grad, *kept]
    waits, later = [], []
    if direct:
        ffn_held, waits = join_cores(*ffn_grads, chips, seqs)
    total, *rest_grads = backward_rest(normed, waits, members, pair_shapes)
    if direct:
        ffn_mine = low(join_chips(ffn_held, waits, seqs))
        rest_held, rest_sends = join_cores(*rest_grads, chips, seqs)
        later = [ffn_mine] + rest_sends
    input_grad, sums, *first_grads = backward_first(
        normed, inputs, vectors, total, residual_grad, sums, later, members, pair_shapes
    )

    if direct:
        ffn_sum = add(*lax.all_to_all(ffn_mine, "head", 0, 0, tiled=True))
        rest = join_chips(rest_held, rest_sends, seqs)
        rest_came = [
            lax.ppermute(low(rest[a - 1]), "head", turn(slots, slots - a)) for a in range(1, slots)
        ]
        pair_sum = add(join_chips(*join_cores(*first_grads, chips, seqs), seqs), *rest_came)
    else:
        ffn_sum = lax.psum_scatter(
            ffn_grads[0].astype(F32).reshape(4, 2, width, width), ("seq", "head"), scatter_dimension=2, tiled=True
        )
        every = jnp.concatenate([first_grads[0][None], rest_grads[0]], axis=0).astype(F32)
        every = jnp.stack([every[(z + slots - p) % slots] for p in range(slots)])
        pair_sum = lax.psum_scatter(every, "head", scatter_dimension=0, tiled=False)
        pair_sum = lax.psum_scatter(pair_sum, "seq", scatter_dimension=0, tiled=True)

    sums = jnp.sum(lax.all_to_all(sums, ("seq", "head"), 0, 0, tiled=True), axis=0)
    vector = [sums[0, i * share : (i + 1) * share] for i in range(5)]
    shrink_grad = ffn_sum[:, 1].reshape(4, share, devices, share).transpose(2, 0, 3, 1)
    return (
        result,
        input_grad,
        vector[0],
        vector[1],
        pair_sum[:, :PAIR],
        pair_sum[:, PAIR : 2 * PAIR],
        pair_sum[:, 2 * PAIR : 3 * PAIR],
        pair_sum[:, 3 * PAIR : 4 * PAIR],
        pair_sum[:, 4 * PAIR :].T,
        vector[2],
        vector[3],
        ffn_sum[:, 0].reshape(hidden_share, width).T,
        sums[1, :hidden_share],
        shrink_grad.reshape(devices * hidden_share, share),
        vector[4],
    )


def solution(mesh):
    placed = (
        P(("seq", "head"), None),
        P(("seq", "head")),
        P(("seq", "head")),
        P(None, "head"),
        P(None, "head"),
        P(None, "head"),
        P(None, "head"),
        P("head", None),
        P(("seq", "head")),
        P(("seq", "head")),
        P(None, ("seq", "head")),
        P(("seq", "head")),
        P(None, ("seq", "head")),
        P(("seq", "head")),
        P(("seq", "head"), None),
    )
    return jax.shard_map(
        body,
        mesh=mesh,
        in_specs=placed,
        out_specs=(
            P(("seq", "head"), None),
            P(("seq", "head"), None),
            P(("seq", "head")),
            P(("seq", "head")),
            P("seq", "head"),
            P("seq", "head"),
            P("seq", "head"),
            P("seq", "head"),
            P("head", "seq"),
            P(("seq", "head")),
            P(("seq", "head")),
            P(None, ("seq", "head")),
            P(("seq", "head")),
            P(None, ("seq", "head")),
            P(("seq", "head")),
        ),
        check_vma=False,
    )
```

```python
import functools

import jax
import jax.numpy as jnp
from jax import lax
from jax.experimental import pallas as pl
from jax.experimental.pallas import tpu as pltpu
from jax.sharding import PartitionSpec as P

EPSILON = 1e-5
CHUNK = 128
PAIR = 128
F32 = jnp.float32
BF16 = jnp.bfloat16
LIMIT = 56 * 1024 * 1024


def nn(a, b):
    return lax.dot_general(a, b, (((1,), (0,)), ((), ())), preferred_element_type=F32)


def nt(a, b):
    return lax.dot_general(a, b, (((1,), (1,)), ((), ())), preferred_element_type=F32)


def tn(a, b):
    return lax.dot_general(a, b, (((0,), (0,)), ((), ())), preferred_element_type=F32)


def low(v):
    return v.astype(BF16)


def iota(shape, axis):
    return lax.broadcasted_iota(jnp.int32, shape, axis)


def first_half(shape):
    return iota(shape, 1) < PAIR // 2


def stacked(block):
    left = first_half(block.shape)
    zero = jnp.zeros_like(block)
    return jnp.concatenate([jnp.where(left, block, zero), jnp.where(left, zero, block)], axis=0)


def parts(v):
    high = low(v)
    return jnp.concatenate([high, low(v - high.astype(F32))], axis=1)


def whole(v):
    return v[:, :PAIR] + v[:, PAIR:]


def head_block(shape=(PAIR, PAIR)):
    return (iota(shape, 0) < PAIR // 2) == (iota(shape, 1) < PAIR // 2)


def causal_pair():
    return iota((CHUNK, 2 * CHUNK), 0) >= (iota((CHUNK, 2 * CHUNK), 1) & (CHUNK - 1))


def causal_pair_t():
    return iota((CHUNK, 2 * CHUNK), 0) <= (iota((CHUNK, 2 * CHUNK), 1) & (CHUNK - 1))


def ones_where(mask):
    return low(jnp.where(mask, 1.0, 0.0))


def norm_parts(tokens):
    average = jnp.mean(tokens, axis=-1, keepdims=True)
    centred = tokens - average
    rate = lax.rsqrt(jnp.mean(centred * centred, axis=-1, keepdims=True) + EPSILON)
    return centred * rate, rate


def norm_back(grad, normal, rate, gain):
    w = grad * gain
    return rate * (
        w
        - jnp.mean(w, axis=-1, keepdims=True)
        - normal * jnp.mean(w * normal, axis=-1, keepdims=True)
    )


def chunks(length):
    return [slice(c * CHUNK, (c + 1) * CHUNK) for c in range(length // CHUNK)]


def attend_forward(normed, weight, keep):
    q_ref, k_ref, v_ref, powers_ref, inverse_ref, score_ref, prob_ref, key_state, value_state, heads_ref = keep
    cuts = chunks(normed.shape[0])
    tri = ones_where(iota((CHUNK, CHUNK), 0) >= iota((CHUNK, CHUNK), 1))
    same = head_block()
    both = jnp.concatenate([ones_where(same)] * 2, axis=0)
    causal = causal_pair()
    left = first_half((CHUNK, PAIR))
    carried = jnp.zeros((1, PAIR), F32)
    key_sum = jnp.zeros((PAIR, PAIR), F32)
    value_sum = jnp.zeros((PAIR, PAIR), F32)

    def masked(product):
        return low(jnp.where(causal, product, 0.0))

    def lift(score):
        top_a = jnp.max(jnp.where(left, score, -jnp.inf), axis=-1, keepdims=True)
        top_b = jnp.max(jnp.where(left, -jnp.inf, score), axis=-1, keepdims=True)
        return jnp.exp(score - jnp.where(left, top_a, top_b))

    for first in range(0, len(cuts), 8):
        group = list(range(first, min(first + 8, len(cuts))))
        each = range(len(group))
        rows = slice(group[0] * CHUNK, (group[-1] + 1) * CHUNK)
        made = nn(normed[rows, :], weight)
        cut = [made[i * CHUNK : (i + 1) * CHUNK, :] for i in each]
        q = [low(low(m[:, :PAIR]).astype(F32) * 0.125) for m in cut]
        k = [low(m[:, PAIR : 2 * PAIR]) for m in cut]
        v = [low(m[:, 2 * PAIR : 3 * PAIR]) for m in cut]
        powers = [jnp.exp(m[:, 3 * PAIR :]) for m in cut]
        powers_low = [low(p) for p in powers]
        local = [whole(nn(tri, parts(p))) for p in powers]
        scored = [masked(nt(q[i], stacked(k[i]))) for i in each]
        inverse = []
        for i in each:
            running = local[i] + carried
            carried = running[CHUNK - 1 :, :]
            inverse.append(1.0 / running)
        powers_two = [stacked(m) for m in powers_low]
        for i, c in enumerate(group):
            key_state[c, :, :] = low(jnp.where(same, key_sum, 0.0))
            value_state[c, :, :] = low(jnp.where(same, value_sum, 0.0))
            if c + 1 < len(cuts):
                key_sum = key_sum + tn(k[i], powers_low[i])
                value_sum = value_sum + tn(powers_low[i], v[i])
        score = [
            (nn(scored[i], powers_two[i]) + nn(q[i], key_state[c, :, :])) * inverse[i]
            for i, c in enumerate(group)
        ]
        lifted = [lift(m) for m in score]
        prob = [lifted[i] / nn(parts(lifted[i]), both) for i in each]
        reading = [low(prob[i] * inverse[i]) for i in each]
        mixing = [masked(nt(reading[i], powers_two[i])) for i in each]
        for i, c in enumerate(group):
            q_ref[cuts[c], :] = q[i]
            k_ref[cuts[c], :] = k[i]
            v_ref[cuts[c], :] = v[i]
            powers_ref[cuts[c], :] = powers[i]
            inverse_ref[cuts[c], :] = inverse[i]
            score_ref[cuts[c], :] = score[i]
            prob_ref[cuts[c], :] = prob[i]
        for i, c in enumerate(group):
            heads_ref[cuts[c], :] = low(
                nn(mixing[i], stacked(v[i])) + nn(reading[i], value_state[c, :, :])
            )


def attend_backward(heads_grad, kept, backs):
    q_ref, k_ref, v_ref, powers_ref, inverse_ref, score_ref, prob_ref, key_state, value_state = kept
    cuts = chunks(heads_grad.shape[0])
    same = head_block()
    both = jnp.concatenate([ones_where(same)] * 2, axis=0)
    causal = causal_pair()
    causal_t = causal_pair_t()
    tri_t = ones_where(iota((CHUNK, CHUNK), 0) <= iota((CHUNK, CHUNK), 1))
    after_sum = jnp.zeros((1, PAIR), F32)
    read_sum = jnp.zeros((PAIR, PAIR), F32)
    score_sum = jnp.zeros((PAIR, PAIR), F32)

    def masked(product, mask):
        return low(jnp.where(mask, product, 0.0))

    for first in reversed(range(0, len(cuts), 4)):
        group = list(reversed(range(first, min(first + 4, len(cuts)))))
        load = lambda ref: [ref[cuts[c], :] for c in group]
        q, k, v, grad = load(q_ref), load(k_ref), load(v_ref), load(heads_grad)
        inverse, prob, powers = load(inverse_ref), load(prob_ref), load(powers_ref)
        each = range(len(group))
        powers_low = [low(p) for p in powers]
        reading = [low(prob[i] * inverse[i]) for i in each]
        powers_two, values_two = [stacked(m) for m in powers_low], [stacked(m) for m in v]
        grad_two, reading_two = [stacked(m) for m in grad], [stacked(m) for m in reading]
        mixing_grad = [masked(nt(grad[i], values_two[i]), causal) for i in each]
        reading_grad = [
            nn(mixing_grad[i], powers_two[i]) + nt(grad[i], value_state[group[i], :, :]) for i in each
        ]
        mixing_grad_t = [masked(nt(v[i], grad_two[i]), causal_t) for i in each]
        mixing_t = [masked(nt(powers_low[i], reading_two[i]), causal_t) for i in each]
        read_states = []
        for i in each:
            read_states.append(low(jnp.where(same, read_sum, 0.0)))
            if group[i]:
                read_sum = read_sum + tn(reading[i], grad[i])
        prob_grad = [reading_grad[i] * inverse[i] for i in each]
        weighed = [prob[i] * prob_grad[i] for i in each]
        slots_grad = [weighed[i] - prob[i] * nn(parts(weighed[i]), both) for i in each]
        summed_grad = [low(slots_grad[i] * inverse[i]) for i in each]
        running_grad = [
            -inverse[i] * (weighed[i] + slots_grad[i] * score_ref[cuts[group[i]], :]) for i in each
        ]
        powers_grad = [
            nn(mixing_grad_t[i], reading_two[i]) + nt(v[i], read_states[i]) for i in each
        ]
        for i in each:
            backs[cuts[group[i]], 2 * PAIR : 3 * PAIR] = low(
                nn(mixing_t[i], grad_two[i]) + nn(powers_low[i], read_states[i])
            )
        queries_two, keys_two = [stacked(m) for m in q], [stacked(m) for m in k]
        scored_t = [masked(nt(k[i], queries_two[i]), causal_t) for i in each]
        summed_two = [stacked(m) for m in summed_grad]
        score_states = []
        for i in each:
            score_states.append(low(jnp.where(same, score_sum, 0.0)))
            if group[i]:
                score_sum = score_sum + tn(q[i], summed_grad[i])
        scored_grad = [masked(nt(summed_grad[i], powers_two[i]), causal) for i in each]
        scored_grad_t = [masked(nt(powers_low[i], summed_two[i]), causal_t) for i in each]
        later = [whole(nn(tri_t, parts(running_grad[i]))) for i in each]
        powers_grad = [
            powers_grad[i] + nn(scored_t[i], summed_two[i]) + nn(k[i], score_states[i]) for i in each
        ]
        for i in each:
            rows = cuts[group[i]]
            backs[rows, :PAIR] = low(
                0.125 * (nn(scored_grad[i], keys_two[i]) + nt(summed_grad[i], key_state[group[i], :, :]))
            )
            backs[rows, PAIR : 2 * PAIR] = low(
                nn(scored_grad_t[i], queries_two[i]) + nt(powers_low[i], score_states[i])
            )
            total = later[i] + after_sum
            after_sum = total[:1, :]
            backs[rows, 3 * PAIR :] = low((powers_grad[i] + total) * powers[i])


def kept_shapes(length, lead=()):
    n = length // CHUNK
    shape = jax.ShapeDtypeStruct
    return (
        [shape(lead + (length, PAIR), BF16)] * 3
        + [shape(lead + (length, PAIR), F32)] * 4
        + [shape(lead + (n, PAIR, PAIR), BF16)] * 2
    )


def fixed(shape):
    return pl.BlockSpec(shape, lambda a: (0,) * len(shape))


def one_slot(members, slot):
    return [
        pl.BlockSpec((None,) + s.shape[1:], lambda a, rank=len(s.shape): (slot,) + (0,) * (rank - 1))
        for s in members
    ]


def by_step(members, first=0):
    return [
        pl.BlockSpec((None,) + s.shape[1:], lambda a, rank=len(s.shape): (a + first,) + (0,) * (rank - 1))
        for s in members
    ]


def anywhere(members):
    return [pl.BlockSpec(memory_space=pl.ANY)] * len(members)


def mark_spec():
    return pl.BlockSpec(memory_space=pltpu.SMEM)


MARK = jax.ShapeDtypeStruct((1,), F32)


def cost(micros):
    return pl.CostEstimate(flops=int(micros * 1e9), bytes_accessed=int(micros * 1e6), transcendentals=0)


def params():
    return pltpu.CompilerParams(vmem_limit_bytes=LIMIT)


def select(width, offset, share, total):
    return ones_where(
        iota((width, total), 0) == offset + (iota((width, total), 1) & (share - 1))
    )


def owned(devices, share, total):
    return iota((devices, total), 0) == lax.shift_right_logical(
        iota((devices, total), 1), share.bit_length() - 1
    )


def spread(rows, offset, share, total):
    each = nn(rows, select(rows.shape[1], offset, share, total))
    return jnp.sum(jnp.where(owned(rows.shape[0], share, total), each, 0.0), axis=0, keepdims=True)


def collect(rows, devices, share):
    total = rows[0].shape[1]
    mine = owned(devices, share, total)
    out = jnp.zeros((devices, 128), F32)
    for i, row in enumerate(rows):
        rest = jnp.where(mine, row, 0.0)
        high = low(rest)
        pair = jnp.concatenate([high, low(rest - high.astype(F32))], axis=0)
        made = nt(pair, select(128, i * share, share, total))
        out = out + made[:devices] + made[devices:]
    return out


def own_device(core, chip, slots):
    return (lax.axis_index("seq") ^ (2 * chip + core)) * slots


def fill(weight, own_ref, pieces, slot):
    @pl.when(slot == 0)
    def _():
        weight[...] = own_ref[...]

    @pl.when(slot > 0)
    def _():
        rows = weight.shape[0] // len(pieces)
        mine = lax.axis_index("seq") if len(pieces) > 1 else 0
        start = pl.multiple_of((slot - 1) * rows, 16)
        for r, piece in enumerate(pieces):
            weight[pl.ds(pl.multiple_of((mine ^ r) * rows, rows), rows), :] = piece[pl.ds(start, rows), :]


def gather_vectors(pieces, rows, slots, vectors):
    for r, piece in enumerate(pieces):
        block = piece[(slots - 1) * rows :, :256].astype(F32)
        for a in range(slots):
            z = lax.rem(lax.axis_index("head") + slots - a, slots)
            source = own_device(r % 2, r // 2, slots) + z
            for i in range(2):
                part = block[a : a + 1, 128 * i : 128 * (i + 1)]
                vectors[pl.ds(source, 1), i : i + 1, :] = part[None]


def forward_kernel(count, slots, tokens_ref, own_ref, *refs):
    pieces, refs = refs[:count], refs[count:]
    if count == 1:
        given, refs = refs[0], refs[1:]
    normed_ref, rows_ref, residual_ref, second_ref, mark, heads_ref, weight = refs[:7]
    keep, staged, vectors = refs[7:-2], refs[-2], refs[-1]
    slot = pl.program_id(0)
    length, width = tokens_ref.shape
    share = width // vectors.shape[0]
    tiles = [slice(r, r + 256) for r in range(0, length, 256)]

    @pl.when(slot == 0)
    def _():
        if count == 1:
            vectors[...] = given[:, :8, :].astype(F32)
        else:
            gather_vectors(pieces, weight.shape[0] // count, slots, vectors)
        for i in range(9):
            part = low(vectors[:, 0 if i < 5 else 1, :])
            rows_ref[i : i + 1, :] = spread(part, (i if i < 5 else i - 5) * share, share, width)
        gain, shift = rows_ref[0:1, :], rows_ref[1:2, :]
        for rows in tiles:
            tokens = tokens_ref[rows, :].astype(F32)
            normal, _ = norm_parts(tokens)
            normed_ref[rows, :] = low(normal * gain + shift)
            residual_ref[rows, :] = tokens
        mark[0] = 1.0

    fill(weight, own_ref, pieces, slot)
    attend_forward(normed_ref, weight[:width, :], list(keep) + [staged])
    heads_ref[...] = staged[...]
    residual_ref[...] += nn(staged[...], weight[width:, :])

    @pl.when(slot == slots - 1)
    def _():
        gain, shift = rows_ref[2:3, :], rows_ref[3:4, :]
        for rows in tiles:
            normal, _ = norm_parts(residual_ref[rows, :])
            second_ref[rows, :] = low(normal * gain + shift)


def forward(tokens, own, pieces, vectors, devices, slots):
    length, width = tokens.shape
    shape = jax.ShapeDtypeStruct
    operands = [tokens, own, *pieces, *vectors]
    outs = [
        shape((length, width), BF16),
        shape((16, width), F32),
        shape((length, width), F32),
        shape((length, width), BF16),
    ]
    stacked_outs = [shape((slots, length, PAIR), BF16), shape((slots, width + PAIR, 4 * PAIR), BF16)]
    stacked_outs += kept_shapes(length, (slots,))
    made = pl.pallas_call(
        functools.partial(forward_kernel, len(pieces), slots),
        grid=(slots,),
        out_shape=outs + [MARK] + stacked_outs,
        in_specs=[fixed(o.shape) for o in operands],
        out_specs=[fixed(o.shape) for o in outs] + [mark_spec()] + by_step(stacked_outs),
        scratch_shapes=[pltpu.VMEM((length, PAIR), BF16), pltpu.VMEM((devices, 8, 128), F32)],
        compiler_params=params(),
        cost_estimate=cost(17),
        name="attend_forward",
    )(*operands)
    return made[:5], made[5:]


GELU_A = 0.7978845608028654
GELU_B = 0.044715


def gelu_both(u):
    square = u * u
    bend = jnp.tanh(GELU_A * (u + GELU_B * (square * u)))
    half = 0.5 * (1.0 + bend)
    slope = half + 0.5 * u * (1.0 - bend * bend) * (GELU_A * (1.0 + 3.0 * GELU_B * square))
    return u * half, slope


def weight_copies(block, pieces, weights, sems):
    if len(pieces) == 1:
        return [pltpu.make_async_copy(pieces[0].at[block], weights.at[block], sems.at[block, 0])]
    copies = []
    for r, piece in enumerate(pieces):
        slots = piece.shape[0]
        copies.append(
            pltpu.make_async_copy(
                piece.at[:, pl.ds(2 * block, 2)],
                weights.at[block, pl.ds(own_device(r % 2, r // 2, slots), slots)],
                sems.at[block, len(copies)],
            )
        )
    return copies


def grad_copies(block, grads, outs, sems):
    if len(outs) == 1:
        return [pltpu.make_async_copy(grads.at[block], outs[0].at[block], sems.at[block, 0])]
    copies = []
    for core, out in enumerate(outs):
        chips, slots = out.shape[:2]
        for chip in range(chips):
            target = (2 * chip + ((lax.axis_index("seq") & 1) ^ core)) * slots
            copies.append(
                pltpu.make_async_copy(
                    grads.at[block, pl.ds(target, slots)],
                    out.at[chip, :, block],
                    sems.at[block, len(copies)],
                )
            )
    return copies


def ffn_kernel(count, second_ref, rows_ref, cotangent_ref, residual_hbm, *refs):
    pieces = refs[:count]
    result_ref, grad_ref, branch_ref, sums_ref = refs[count : count + 4]
    outs = refs[count + 4 : -8]
    weights, grads, residual, total, back, in_sems, out_sems, residual_sem = refs[-8:]
    k = pl.program_id(0)
    length, width = second_ref.shape
    tiles = [slice(r, r + 256) for r in range(0, length, 256)]
    fetch = pltpu.make_async_copy(residual_hbm, residual, residual_sem)

    @pl.when(k == 0)
    def _():
        for block in range(4):
            for copy in weight_copies(block, pieces, weights, in_sems):
                copy.start()
        fetch.start()
        total[...] = jnp.zeros_like(total)
        back[...] = jnp.zeros_like(back)

    for block in range(4):

        @pl.when(k == block)
        def _(block=block):
            for copy in weight_copies(block, pieces, weights, in_sems):
                copy.wait()

    expand = weights[k, :, 0].reshape(width, width)
    shrink = weights[k, :, 1].reshape(width, width)
    bias = rows_ref[pl.ds(5 + k, 1), :]
    bias_grad = jnp.zeros((1, width), F32)
    acts, hids = [], []
    for rows in tiles:
        hidden = nt(second_ref[rows, :], expand) + bias
        pull = nn(cotangent_ref[rows, :], shrink)
        value, slope = gelu_both(hidden)
        activated = low(value)
        hidden_grad = low(pull * slope)
        bias_grad = bias_grad + jnp.sum(hidden_grad.astype(F32), axis=0, keepdims=True)
        total[rows, :] += nt(activated, shrink)
        back[rows, :] += nn(hidden_grad, expand)
        acts.append(activated)
        hids.append(hidden_grad)
    sums_ref[pl.ds(5 + k, 1), :] = bias_grad
    grads[k, :, 1] = low(tn(cotangent_ref[...], jnp.concatenate(acts, axis=0))).reshape(
        width // 16, 16, width
    )
    grads[k, :, 0] = low(tn(jnp.concatenate(hids, axis=0), second_ref[...])).reshape(width // 16, 16, width)
    for block in range(4):

        @pl.when(k == block)
        def _(block=block):
            for copy in grad_copies(block, grads, outs, out_sems):
                copy.start()

    @pl.when(k == 3)
    def _():
        fetch.wait()
        gain, bias = rows_ref[2:3, :], rows_ref[4:5, :]
        gain_grad = jnp.zeros((1, width), F32)
        shift_grad = jnp.zeros((1, width), F32)
        outer = jnp.zeros((1, width), F32)
        for rows in tiles:
            base = residual[rows, :]
            result_ref[rows, :] = low(base + total[rows, :] + bias)
            grad = back[rows, :]
            normal, rate = norm_parts(base)
            upstream = cotangent_ref[rows, :].astype(F32)
            gain_grad = gain_grad + jnp.sum(grad * normal, axis=0, keepdims=True)
            shift_grad = shift_grad + jnp.sum(grad, axis=0, keepdims=True)
            outer = outer + jnp.sum(upstream, axis=0, keepdims=True)
            full = upstream + norm_back(grad, normal, rate, gain)
            grad_ref[rows, :] = full
            branch_ref[rows, :] = low(full)
        sums_ref[0:2, :] = jnp.zeros((2, width), F32)
        sums_ref[2:3, :] = gain_grad
        sums_ref[3:4, :] = shift_grad
        sums_ref[4:5, :] = outer
        for block in range(4):
            for copy in grad_copies(block, grads, outs, out_sems):
                copy.wait()


def feed_forward(second, rows, cotangent, residual, pieces, grad_shapes):
    length, width = second.shape
    shape = jax.ShapeDtypeStruct
    weights = (4, width // 16, 2, 16, width)
    outs = [
        shape((length, width), BF16),
        shape((length, width), F32),
        shape((length, width), BF16),
        shape((16, width), F32),
    ]
    return pl.pallas_call(
        functools.partial(ffn_kernel, len(pieces)),
        grid=(4,),
        out_shape=outs + [shape(s, BF16) for s in grad_shapes],
        in_specs=[fixed(o.shape) for o in (second, rows, cotangent)] + anywhere([residual, *pieces]),
        out_specs=[fixed(o.shape) for o in outs] + anywhere(grad_shapes),
        scratch_shapes=[
            pltpu.VMEM(weights, BF16),
            pltpu.VMEM(weights, BF16),
            pltpu.VMEM((length, width), F32),
            pltpu.VMEM((length, width), F32),
            pltpu.VMEM((length, width), F32),
            pltpu.SemaphoreType.DMA((4, 8)),
            pltpu.SemaphoreType.DMA((4, 8)),
            pltpu.SemaphoreType.DMA,
        ],
        compiler_params=params(),
        cost_estimate=cost(22),
        name="feed_forward",
    )(second, rows, cotangent, residual, *pieces)


def heads_kernel(branch_ref, weight_ref, heads_ref, grad_ref, output_grad_ref, mark):
    slots = heads_ref.shape[0]
    weight = weight_ref[...].reshape(slots * PAIR, weight_ref.shape[2])
    grad = low(nt(branch_ref[...], weight))
    output_grad = low(tn(branch_ref[...], jnp.concatenate([heads_ref[a] for a in range(slots)], axis=1)))
    for a in range(slots):
        grad_ref[a] = grad[:, a * PAIR : (a + 1) * PAIR]
        output_grad_ref[a] = output_grad[:, a * PAIR : (a + 1) * PAIR]
    mark[0] = 1.0


def heads_back(branch, weights, heads):
    slots = heads.shape[0]
    length, width = branch.shape
    shape = jax.ShapeDtypeStruct
    outs = [shape((slots, length, PAIR), BF16), shape((slots, width, PAIR), BF16)]
    return pl.pallas_call(
        heads_kernel,
        grid=(1,),
        out_shape=outs + [MARK],
        in_specs=[
            fixed((length, width)),
            pl.BlockSpec((slots, PAIR, width), lambda a: (0, width // PAIR, 0)),
        ]
        + [fixed(heads.shape)],
        out_specs=[fixed(o.shape) for o in outs] + [mark_spec()],
        compiler_params=params(),
        cost_estimate=cost(4),
        name="heads_back",
    )(branch, weights, heads)


def pair_grads(grad_ref, output_grad_ref, normed_ref, kept, outs, backs, made):
    attend_backward(grad_ref, kept, backs)
    made[:, : 4 * PAIR] = low(tn(normed_ref[...], backs[...]))
    made[:, 4 * PAIR :] = output_grad_ref[...]
    if len(outs) == 1:
        outs[0][...] = made[...]
        return
    seq = lax.axis_index("seq")
    rows = outs[1].shape[0]
    for chip in range(outs[0].shape[0]):
        for core, out in enumerate((outs[0].at[chip], outs[1 + chip])):
            start = pl.multiple_of((seq ^ (2 * chip + core)) * rows, rows)
            out[...] = made[pl.ds(start, rows), :]


def back_kernel(waits, parts_out, normed_ref, rows_ref, before_ref, tokens_hbm, residual_grad_hbm, *refs):
    refs = refs[waits:]
    weight, grad_ref, output_grad_ref, kept, refs = refs[0], refs[1], refs[2], refs[3:12], refs[12:]
    input_grad_ref, sums_ref, outs, mark = refs[0], refs[1], refs[2 : 2 + parts_out], refs[2 + parts_out]
    backs, made, total, tokens, residual_grad, sems = refs[3 + parts_out :]
    length, width = normed_ref.shape
    devices = sums_ref.shape[0]
    share = width // devices
    step, steps = pl.program_id(0), pl.num_programs(0)
    copies = [
        pltpu.make_async_copy(tokens_hbm, tokens, sems.at[0]),
        pltpu.make_async_copy(residual_grad_hbm, residual_grad, sems.at[1]),
    ]

    @pl.when(step == 0)
    def _():
        for copy in copies:
            copy.start()
        total[...] = jnp.zeros_like(total)
        mark[0] = 1.0

    pair_grads(grad_ref, output_grad_ref, normed_ref, kept, outs, backs, made)
    total[...] += nt(backs[...], weight[:width, :])

    @pl.when(step == steps - 1)
    def _():
        for copy in copies:
            copy.wait()
        gain = rows_ref[0:1, :]
        gain_grad = jnp.zeros((1, width), F32)
        shift_grad = jnp.zeros((1, width), F32)
        for rows in [slice(r, r + 256) for r in range(0, length, 256)]:
            grad = total[rows, :]
            normal, rate = norm_parts(tokens[rows, :].astype(F32))
            gain_grad = gain_grad + jnp.sum(grad * normal, axis=0, keepdims=True)
            shift_grad = shift_grad + jnp.sum(grad, axis=0, keepdims=True)
            input_grad_ref[rows, :] = low(residual_grad[rows, :] + norm_back(grad, normal, rate, gain))
        sums_ref[...] = jnp.zeros_like(sums_ref)
        small = [gain_grad, shift_grad] + [before_ref[i : i + 1, :] for i in range(2, 5)]
        sums_ref[:, 0, :] = collect(small, devices, share)
        sums_ref[:, 1, :] = collect([before_ref[i : i + 1, :] for i in range(5, 9)], devices, share)


def backward(normed, rows, before, tokens, residual_grad, devices, waits, members, grad_shapes):
    length, width = normed.shape
    slots = members[0].shape[0]
    shape = jax.ShapeDtypeStruct
    outs = [shape((length, width), BF16), shape((devices, 8, 128), F32)]
    grads = [shape(s[:-2] + (slots,) + s[-2:], BF16) for s in grad_shapes]
    grad_specs = [
        by_step([g])[0]
        if len(g.shape) == 3
        else pl.BlockSpec((g.shape[0], None) + g.shape[2:], lambda a: (0, a, 0, 0))
        for g in grads
    ]
    large = [tokens, residual_grad]
    return pl.pallas_call(
        functools.partial(back_kernel, len(waits), len(grad_shapes)),
        grid=(slots,),
        out_shape=outs + grads + [MARK],
        in_specs=[fixed(o.shape) for o in (normed, rows, before)] + anywhere(large + waits) + by_step(members),
        out_specs=[fixed(o.shape) for o in outs] + grad_specs + [mark_spec()],
        scratch_shapes=[
            pltpu.VMEM((length, 4 * PAIR), BF16),
            pltpu.VMEM((width, 5 * PAIR), BF16),
            pltpu.VMEM((length, width), F32),
        ]
        + [pltpu.VMEM((length, width), m.dtype) for m in large]
        + [pltpu.SemaphoreType.DMA((2,))],
        compiler_params=params(),
        cost_estimate=cost(27),
        name="attend_back",
    )(normed, rows, before, *large, *waits, *members)


def after(value, *others):
    return pl.pallas_call(
        lambda *refs: None,
        out_shape=jax.ShapeDtypeStruct(value.shape, value.dtype),
        in_specs=anywhere((value,) + others),
        out_specs=anywhere([value])[0],
        input_output_aliases={0: 0},
        name="after",
    )(value, *others)


def join_kernel(chips, slots, ffn_ref, *refs):
    keep_ref, others, sums_ref, refs = refs[0], refs[1 : 1 + chips], refs[1 + chips], refs[2 + chips :]
    ffn_outs, outs, sums_out = refs[:slots], refs[slots : slots + chips], refs[slots + chips]
    z = lax.axis_index("head")
    for a, out in enumerate(ffn_outs):
        place = lax.rem(z + a, slots)
        out[...] = low(functools.reduce(lambda x, y: x + y, [ffn_ref[c, pl.ds(place, 1)][0].astype(F32) for c in range(chips)]))
    for chip, out in enumerate(outs):
        out[...] = low(keep_ref[chip].astype(F32) + others[chip][...].astype(F32))
    sums_out[...] = sums_ref[...]


def join(ffn, keep, others, sums):
    shape = jax.ShapeDtypeStruct
    chips, slots = ffn.shape[:2]
    operands = [ffn, keep, *others, sums]
    outs = [shape(ffn.shape[2:], BF16)] * slots + [shape(keep.shape[1:], BF16)] * chips
    outs += [shape(sums.shape, F32)]
    made = pl.pallas_call(
        functools.partial(join_kernel, chips, slots),
        grid=(1,),
        out_shape=outs,
        in_specs=[fixed(o.shape) for o in operands],
        out_specs=[fixed(o.shape) for o in outs],
        compiler_params=params(),
        cost_estimate=cost(3),
        name="join",
    )(*operands)
    return made[:slots], made[slots : slots + chips], made[-1]


def sum_plane_kernel(slots, *refs):
    pairs, mine_ref, sends = refs[: -slots - 1], refs[-slots - 1], refs[-slots:-1]
    for a in range(slots):
        mine = functools.reduce(lambda x, y: x + y, [p[a].astype(F32) for p in pairs])
        if a == 0:
            mine_ref[...] = mine
        else:
            sends[a - 1][...] = low(mine)
    refs[-1][0] = 1.0


def sum_plane(pairs, waits):
    shape = jax.ShapeDtypeStruct
    slots = pairs[0].shape[0]
    outs = [shape(pairs[0].shape[1:], F32)] + [shape(pairs[0].shape[1:], BF16)] * (slots - 1)

    def kernel(*refs):
        sum_plane_kernel(slots, *refs[: len(pairs)], *refs[len(pairs) + len(waits) :])

    return pl.pallas_call(
        kernel,
        grid=(1,),
        out_shape=outs + [MARK],
        in_specs=[fixed(p.shape) for p in pairs] + anywhere(waits),
        out_specs=[fixed(o.shape) for o in outs] + [mark_spec()],
        compiler_params=params(),
        cost_estimate=cost(2),
        name="sum_plane",
    )(*pairs, *waits)


def settle_kernel(slots, *refs):
    ffn, sums_ref, expand_ref, shrink_ref, vector_ref = refs[:slots], *refs[slots + 1 :]
    blocks, _, share, width = ffn[0].shape
    total = functools.reduce(lambda x, y: x + y, [f[...].astype(F32) for f in ffn])
    expand_ref[...] = total[:, 0].reshape(blocks * share, width).T
    for i in range(blocks):
        shrink_ref[:, i] = total[i, 1].T.reshape(width // share, share, share)
    vector_ref[...] = jnp.sum(sums_ref[...], axis=0)


def settle(ffn, sums, wait):
    shape = jax.ShapeDtypeStruct
    slots = len(ffn)
    blocks, _, share, width = ffn[0].shape
    outs = [
        shape((width, blocks * share), F32),
        shape((width // share, blocks, share, share), F32),
        shape(sums.shape[1:], F32),
    ]

    def kernel(*refs):
        settle_kernel(slots, *refs[:slots], None, *refs[slots : slots + 1], *refs[slots + 2 :])

    return pl.pallas_call(
        kernel,
        grid=(1,),
        out_shape=outs,
        in_specs=[fixed(o.shape) for o in (*ffn, sums)] + anywhere([wait]),
        out_specs=[fixed(o.shape) for o in outs],
        compiler_params=params(),
        cost_estimate=cost(3),
        name="settle",
    )(*ffn, sums, wait)


def flip(count, bit):
    return [(i, i ^ bit) for i in range(count)]


def turn(count, by):
    return [(i, (i + by) % count) for i in range(count)]


def add(*members):
    return functools.reduce(lambda a, b: a + b, [m.astype(F32) for m in members])


def to_mate(shares, seqs):
    return lax.ppermute(shares, "seq", flip(seqs, 1))


def over_chips(shares, chips, seqs):
    return [shares] + [lax.ppermute(shares, "seq", flip(seqs, 2 * r)) for r in range(1, chips)]


def over_cores(held, seqs):
    return [member for h in held for member in (h, to_mate(h, seqs))]


def to_chips(shares, seqs):
    plane = [list(range(core, seqs, 2)) for core in range(2)]
    return lax.all_to_all(shares, "seq", 0, 0, axis_index_groups=plane, tiled=True)


def from_chips(sends, seqs):
    return [lax.ppermute(m, "seq", flip(seqs, 2 * r + 2)) for r, m in enumerate(sends)]


def body(
    inputs,
    attn_gain,
    attn_shift,
    query_weight,
    key_weight,
    value_weight,
    control_weight,
    output_weight,
    ffn_gain,
    ffn_shift,
    expand_weight,
    expand_bias,
    shrink_weight,
    shrink_bias,
    cotangent,
):
    seqs, slots = lax.axis_size("seq"), lax.axis_size("head")
    devices = seqs * slots
    chips = seqs // 2
    width = inputs.shape[1]
    share = width // devices
    hidden_share = expand_weight.shape[1]
    z = lax.axis_index("head")
    direct = seqs == 8 and slots == 4 and share == 16 and hidden_share == 4 * share

    own = jnp.concatenate(
        [
            jnp.concatenate([query_weight, key_weight, value_weight, control_weight], axis=1),
            output_weight,
        ],
        axis=0,
    )
    places = [(attn_gain, 0), (attn_shift, 1), (ffn_gain, 2), (ffn_shift, 3), (shrink_bias, 4)]
    row = functools.reduce(
        lambda a, b: a + b,
        [jnp.pad(m, (i * share, width - (i + 1) * share)) for m, i in places]
        + [jnp.pad(expand_bias, (128, width - 128 - hidden_share))],
    )
    block = jnp.pad(row[None, :], ((0, 15), (0, 0)))
    expand_t = expand_weight.T.reshape(4, share, width)
    shrink_t = shrink_weight.reshape(devices, 4, share, share).transpose(1, 3, 0, 2).reshape(4, share, width)
    load = jnp.stack([expand_t, shrink_t], axis=1)
    if direct:
        rows = own.shape[0] // seqs
        piece = lax.dynamic_slice_in_dim(own, lax.axis_index("seq") * rows, rows, axis=0)
        piece = jnp.concatenate([piece, block], axis=0)
        came = [lax.ppermute(piece, "head", turn(slots, a)) for a in range(1, slots)]
        for a in range(1, slots):
            block = block + jnp.pad(came[a - 1][rows : rows + 1], ((a, 15 - a), (0, 0)))
        near = jnp.concatenate([c[:rows] for c in came] + [block], axis=0)
        pieces, vectors = over_cores(over_chips(near, chips, seqs), seqs), []
        load = jnp.broadcast_to(load.reshape(1, 8, share, width), (slots, 8, share, width))
        load = lax.all_to_all(after(load, near), "head", 0, 0, tiled=True)
        held = over_chips(load, chips, seqs)
        pair_shapes = [(chips, width // seqs, 5 * PAIR)] + [(width // seqs, 5 * PAIR)] * chips
        ffn_shapes = [(chips, slots, 4, 2, 16, width)] * 2
    else:
        every = lax.all_gather(own, "head", axis=0, tiled=False)
        pieces = [jnp.concatenate([every[(z + slots - a) % slots] for a in range(1, slots)], axis=0)]
        block = jnp.concatenate([block[:1, :128], block[:1, 128:256], block[2:, :128]], axis=0)
        vectors = [lax.all_gather(block, ("seq", "head"), axis=0, tiled=False)]
        both = lax.all_gather(load, ("seq", "head"), axis=2, tiled=True)
        ffn_pieces = [both.reshape(4, 2, width // 16, 16, width).transpose(0, 2, 1, 3, 4)]
        pair_shapes = [(width, 5 * PAIR)]
        ffn_shapes = [ffn_pieces[0].shape]

    (normed, rows, residual, second, _), (heads, weights, *members) = forward(
        inputs, own, pieces, vectors, devices, slots
    )
    if direct:
        ffn_pieces = over_cores(held[:-1] + [after(held[-1], second)], seqs)
    result, residual_grad, branch, sums, *ffn_grads = feed_forward(
        second, rows, cotangent, residual, ffn_pieces, ffn_shapes
    )
    heads_grad, output_grad, mark = heads_back(branch, weights, heads)
    members = [weights, heads_grad, output_grad, *members]
    waits = []
    if direct:
        ffn_mine = low(add(ffn_grads[0], to_mate(ffn_grads[1], seqs)) * mark[0])
        waits = [ffn_mine]
    input_grad, sums, *pair_grads, _ = backward(
        normed, rows, sums, inputs, residual_grad, devices, waits, members, pair_shapes
    )

    if direct:
        keep, *sends = pair_grads
        ffn, pairs, sums = join(
            to_chips(ffn_mine, seqs), keep, [to_mate(s, seqs) for s in sends], sums
        )
        ffn = [ffn[0]] + [lax.ppermute(ffn[a], "head", turn(slots, a)) for a in range(1, slots)]
        pairs = [pairs[0]] + from_chips(pairs[1:], seqs)
        sums = lax.all_to_all(sums, ("seq", "head"), 0, 0, tiled=True)
        mine, *sends, wait = sum_plane(pairs, ffn[1:] + [sums])
        expand_grad, shrink_grad, sums = settle(ffn, sums, wait)
        came = [lax.ppermute(m, "head", turn(slots, slots - 1 - a)) for a, m in enumerate(sends)]
        pair_sum = add(mine, *came)
    else:
        ffn_sum = lax.psum_scatter(
            ffn_grads[0].astype(F32).transpose(0, 2, 1, 3, 4).reshape(4, 2, width, width), ("seq", "head"), scatter_dimension=2, tiled=True
        )
        every = pair_grads[0].astype(F32)
        every = jnp.stack([every[(z + slots - p) % slots] for p in range(slots)])
        pair_sum = lax.psum_scatter(every, "head", scatter_dimension=0, tiled=False)
        pair_sum = lax.psum_scatter(pair_sum, "seq", scatter_dimension=0, tiled=True)

        sums = jnp.sum(lax.all_to_all(sums, ("seq", "head"), 0, 0, tiled=True), axis=0)
        expand_grad = ffn_sum[:, 0].reshape(hidden_share, width).T
        shrink_grad = ffn_sum[:, 1].reshape(4, share, devices, share).transpose(2, 0, 3, 1)

    vector = [sums[0, i * share : (i + 1) * share] for i in range(5)]
    return (
        result,
        input_grad,
        vector[0],
        vector[1],
        pair_sum[:, :PAIR],
        pair_sum[:, PAIR : 2 * PAIR],
        pair_sum[:, 2 * PAIR : 3 * PAIR],
        pair_sum[:, 3 * PAIR : 4 * PAIR],
        pair_sum[:, 4 * PAIR :].T,
        vector[2],
        vector[3],
        expand_grad,
        sums[1, :hidden_share],
        shrink_grad.reshape(devices * hidden_share, share),
        vector[4],
    )


def solution(mesh):
    placed = (
        P(("seq", "head"), None),
        P(("seq", "head")),
        P(("seq", "head")),
        P(None, "head"),
        P(None, "head"),
        P(None, "head"),
        P(None, "head"),
        P("head", None),
        P(("seq", "head")),
        P(("seq", "head")),
        P(None, ("seq", "head")),
        P(("seq", "head")),
        P(None, ("seq", "head")),
        P(("seq", "head")),
        P(("seq", "head"), None),
    )
    return jax.shard_map(
        body,
        mesh=mesh,
        in_specs=placed,
        out_specs=(
            P(("seq", "head"), None),
            P(("seq", "head"), None),
            P(("seq", "head")),
            P(("seq", "head")),
            P("seq", "head"),
            P("seq", "head"),
            P("seq", "head"),
            P("seq", "head"),
            P("head", "seq"),
            P(("seq", "head")),
            P(("seq", "head")),
            P(None, ("seq", "head")),
            P(("seq", "head")),
            P(None, ("seq", "head")),
            P(("seq", "head")),
        ),
        check_vma=False,
    )
```

```python
import functools

import jax
import jax.numpy as jnp
from jax import lax
from jax.experimental import pallas as pl
from jax.experimental.pallas import tpu as pltpu
from jax.sharding import PartitionSpec as P

EPSILON = 1e-5
CHUNK = 128
PAIR = 128
F32 = jnp.float32
BF16 = jnp.bfloat16


def nn(a, b):
    return lax.dot_general(a, b, (((1,), (0,)), ((), ())), preferred_element_type=F32)


def nt(a, b):
    return lax.dot_general(a, b, (((1,), (1,)), ((), ())), preferred_element_type=F32)


def tn(a, b):
    return lax.dot_general(a, b, (((0,), (0,)), ((), ())), preferred_element_type=F32)


def low(v):
    return v.astype(BF16)


def iota(shape, axis):
    return lax.broadcasted_iota(jnp.int32, shape, axis)


def first_half(shape):
    return iota(shape, 1) < PAIR // 2


def stacked(block):
    left = first_half(block.shape)
    zero = jnp.zeros_like(block)
    return jnp.concatenate([jnp.where(left, block, zero), jnp.where(left, zero, block)], axis=0)


def parts(v):
    high = low(v)
    return jnp.concatenate([high, low(v - high.astype(F32))], axis=1)


def whole(v):
    return v[:, :PAIR] + v[:, PAIR:]


def head_block(shape=(PAIR, PAIR)):
    return (iota(shape, 0) < PAIR // 2) == (iota(shape, 1) < PAIR // 2)


def causal_pair():
    return iota((CHUNK, 2 * CHUNK), 0) >= (iota((CHUNK, 2 * CHUNK), 1) & (CHUNK - 1))


def causal_pair_t():
    return iota((CHUNK, 2 * CHUNK), 0) <= (iota((CHUNK, 2 * CHUNK), 1) & (CHUNK - 1))


def ones_where(mask):
    return low(jnp.where(mask, 1.0, 0.0))


def norm_parts(tokens):
    average = jnp.mean(tokens, axis=-1, keepdims=True)
    centred = tokens - average
    rate = lax.rsqrt(jnp.mean(centred * centred, axis=-1, keepdims=True) + EPSILON)
    return centred * rate, rate


def norm_back(grad, normal, rate, gain):
    w = grad * gain
    return rate * (
        w
        - jnp.mean(w, axis=-1, keepdims=True)
        - normal * jnp.mean(w * normal, axis=-1, keepdims=True)
    )


def chunks(length):
    return [slice(c * CHUNK, (c + 1) * CHUNK) for c in range(length // CHUNK)]


def attend_forward(normed, weight, keep):
    q_ref, k_ref, v_ref, powers_ref, inverse_ref, score_ref, prob_ref, key_state, value_state, heads_ref = keep
    cuts = chunks(normed.shape[0])
    tri = ones_where(iota((CHUNK, CHUNK), 0) >= iota((CHUNK, CHUNK), 1))
    same = head_block()
    both = jnp.concatenate([ones_where(same)] * 2, axis=0)
    causal = causal_pair()
    left = first_half((CHUNK, PAIR))
    carried = jnp.zeros((1, PAIR), F32)
    key_sum = jnp.zeros((PAIR, PAIR), F32)
    value_sum = jnp.zeros((PAIR, PAIR), F32)

    def masked(product):
        return low(jnp.where(causal, product, 0.0))

    def lift(score):
        top_a = jnp.max(jnp.where(left, score, -jnp.inf), axis=-1, keepdims=True)
        top_b = jnp.max(jnp.where(left, -jnp.inf, score), axis=-1, keepdims=True)
        return jnp.exp(score - jnp.where(left, top_a, top_b))

    for first in range(0, len(cuts), 8):
        group = list(range(first, min(first + 8, len(cuts))))
        each = range(len(group))
        rows = slice(group[0] * CHUNK, (group[-1] + 1) * CHUNK)
        made = nn(normed[rows, :], weight)
        cut = [made[i * CHUNK : (i + 1) * CHUNK, :] for i in each]
        q = [low(low(m[:, :PAIR]).astype(F32) * 0.125) for m in cut]
        k = [low(m[:, PAIR : 2 * PAIR]) for m in cut]
        v = [low(m[:, 2 * PAIR : 3 * PAIR]) for m in cut]
        powers = [jnp.exp(m[:, 3 * PAIR :]) for m in cut]
        powers_low = [low(p) for p in powers]
        local = [whole(nn(tri, parts(p))) for p in powers]
        scored = [masked(nt(q[i], stacked(k[i]))) for i in each]
        inverse = []
        for i in each:
            running = local[i] + carried
            carried = running[CHUNK - 1 :, :]
            inverse.append(1.0 / running)
        powers_two = [stacked(m) for m in powers_low]
        for i, c in enumerate(group):
            key_state[c, :, :] = low(jnp.where(same, key_sum, 0.0))
            value_state[c, :, :] = low(jnp.where(same, value_sum, 0.0))
            if c + 1 < len(cuts):
                key_sum = key_sum + tn(k[i], powers_low[i])
                value_sum = value_sum + tn(powers_low[i], v[i])
        score = [
            (nn(scored[i], powers_two[i]) + nn(q[i], key_state[c, :, :])) * inverse[i]
            for i, c in enumerate(group)
        ]
        lifted = [lift(m) for m in score]
        prob = [lifted[i] / nn(parts(lifted[i]), both) for i in each]
        reading = [low(prob[i] * inverse[i]) for i in each]
        mixing = [masked(nt(reading[i], powers_two[i])) for i in each]
        for i, c in enumerate(group):
            q_ref[cuts[c], :] = q[i]
            k_ref[cuts[c], :] = k[i]
            v_ref[cuts[c], :] = v[i]
            powers_ref[cuts[c], :] = powers[i]
            inverse_ref[cuts[c], :] = inverse[i]
            score_ref[cuts[c], :] = score[i]
            prob_ref[cuts[c], :] = prob[i]
        for i, c in enumerate(group):
            heads_ref[cuts[c], :] = low(
                nn(mixing[i], stacked(v[i])) + nn(reading[i], value_state[c, :, :])
            )


def attend_backward(heads_grad, kept, backs):
    q_ref, k_ref, v_ref, powers_ref, inverse_ref, score_ref, prob_ref, key_state, value_state = kept
    cuts = chunks(heads_grad.shape[0])
    same = head_block()
    both = jnp.concatenate([ones_where(same)] * 2, axis=0)
    causal = causal_pair()
    causal_t = causal_pair_t()
    tri_t = ones_where(iota((CHUNK, CHUNK), 0) <= iota((CHUNK, CHUNK), 1))
    after_sum = jnp.zeros((1, PAIR), F32)
    read_sum = jnp.zeros((PAIR, PAIR), F32)
    score_sum = jnp.zeros((PAIR, PAIR), F32)

    def masked(product, mask):
        return low(jnp.where(mask, product, 0.0))

    for first in reversed(range(0, len(cuts), 4)):
        group = list(reversed(range(first, min(first + 4, len(cuts)))))
        load = lambda ref: [ref[cuts[c], :] for c in group]
        q, k, v, grad = load(q_ref), load(k_ref), load(v_ref), load(heads_grad)
        inverse, prob, powers = load(inverse_ref), load(prob_ref), load(powers_ref)
        each = range(len(group))
        powers_low = [low(p) for p in powers]
        reading = [low(prob[i] * inverse[i]) for i in each]
        powers_two, values_two = [stacked(m) for m in powers_low], [stacked(m) for m in v]
        grad_two, reading_two = [stacked(m) for m in grad], [stacked(m) for m in reading]
        mixing_grad = [masked(nt(grad[i], values_two[i]), causal) for i in each]
        reading_grad = [
            nn(mixing_grad[i], powers_two[i]) + nt(grad[i], value_state[group[i], :, :]) for i in each
        ]
        mixing_grad_t = [masked(nt(v[i], grad_two[i]), causal_t) for i in each]
        mixing_t = [masked(nt(powers_low[i], reading_two[i]), causal_t) for i in each]
        read_states = []
        for i in each:
            read_states.append(low(jnp.where(same, read_sum, 0.0)))
            if group[i]:
                read_sum = read_sum + tn(reading[i], grad[i])
        prob_grad = [reading_grad[i] * inverse[i] for i in each]
        weighed = [prob[i] * prob_grad[i] for i in each]
        slots_grad = [weighed[i] - prob[i] * nn(parts(weighed[i]), both) for i in each]
        summed_grad = [low(slots_grad[i] * inverse[i]) for i in each]
        running_grad = [
            -inverse[i] * (weighed[i] + slots_grad[i] * score_ref[cuts[group[i]], :]) for i in each
        ]
        powers_grad = [
            nn(mixing_grad_t[i], reading_two[i]) + nt(v[i], read_states[i]) for i in each
        ]
        for i in each:
            backs[cuts[group[i]], 2 * PAIR : 3 * PAIR] = low(
                nn(mixing_t[i], grad_two[i]) + nn(powers_low[i], read_states[i])
            )
        queries_two, keys_two = [stacked(m) for m in q], [stacked(m) for m in k]
        scored_t = [masked(nt(k[i], queries_two[i]), causal_t) for i in each]
        summed_two = [stacked(m) for m in summed_grad]
        score_states = []
        for i in each:
            score_states.append(low(jnp.where(same, score_sum, 0.0)))
            if group[i]:
                score_sum = score_sum + tn(q[i], summed_grad[i])
        scored_grad = [masked(nt(summed_grad[i], powers_two[i]), causal) for i in each]
        scored_grad_t = [masked(nt(powers_low[i], summed_two[i]), causal_t) for i in each]
        later = [whole(nn(tri_t, parts(running_grad[i]))) for i in each]
        powers_grad = [
            powers_grad[i] + nn(scored_t[i], summed_two[i]) + nn(k[i], score_states[i]) for i in each
        ]
        for i in each:
            rows = cuts[group[i]]
            backs[rows, :PAIR] = low(
                0.125 * (nn(scored_grad[i], keys_two[i]) + nt(summed_grad[i], key_state[group[i], :, :]))
            )
            backs[rows, PAIR : 2 * PAIR] = low(
                nn(scored_grad_t[i], queries_two[i]) + nt(powers_low[i], score_states[i])
            )
            total = later[i] + after_sum
            after_sum = total[:1, :]
            backs[rows, 3 * PAIR :] = low((powers_grad[i] + total) * powers[i])


def kept_shapes(length, lead=()):
    n = length // CHUNK
    shape = pltpu.HBM
    return (
        [shape(lead + (length, PAIR), BF16)] * 3
        + [shape(lead + (length, PAIR), F32)] * 4
        + [shape(lead + (n, PAIR, PAIR), BF16)] * 2
    )


def fixed(shape):
    return pl.BlockSpec(shape, lambda a: (0,) * len(shape))


def one_slot(members, slot):
    return [
        pl.BlockSpec((None,) + s.shape[1:], lambda a, rank=len(s.shape): (slot,) + (0,) * (rank - 1))
        for s in members
    ]


def by_step(members, first=0):
    return [
        pl.BlockSpec((None,) + s.shape[1:], lambda a, rank=len(s.shape): (a + first,) + (0,) * (rank - 1))
        for s in members
    ]


def anywhere(members):
    return [pl.BlockSpec(memory_space=pl.ANY)] * len(members)


def mark_spec():
    return pl.BlockSpec(memory_space=pltpu.SMEM)


MARK = jax.ShapeDtypeStruct((1,), F32)


def cost(micros):
    return pl.CostEstimate(flops=int(micros * 1e9), bytes_accessed=int(micros * 1e6), transcendentals=0)


def params(megabytes=56):
    return pltpu.CompilerParams(vmem_limit_bytes=megabytes * 1024 * 1024)


def select(width, offset, share, total):
    return ones_where(
        iota((width, total), 0) == offset + (iota((width, total), 1) & (share - 1))
    )


def owned(devices, share, total):
    return iota((devices, total), 0) == lax.shift_right_logical(
        iota((devices, total), 1), share.bit_length() - 1
    )


def spread(rows, offset, share, total):
    each = nn(rows, select(rows.shape[1], offset, share, total))
    return jnp.sum(jnp.where(owned(rows.shape[0], share, total), each, 0.0), axis=0, keepdims=True)


def collect(rows, devices, share):
    total = rows[0].shape[1]
    mine = owned(devices, share, total)
    out = jnp.zeros((devices, 128), F32)
    for i, row in enumerate(rows):
        rest = jnp.where(mine, row, 0.0)
        high = low(rest)
        pair = jnp.concatenate([high, low(rest - high.astype(F32))], axis=0)
        made = nt(pair, select(128, i * share, share, total))
        out = out + made[:devices] + made[devices:]
    return out


def own_device(core, chip, slots):
    return (lax.axis_index("seq") ^ (2 * chip + core)) * slots


def fill(weight, own_ref, pieces, slot):
    @pl.when(slot == 0)
    def _():
        weight[...] = own_ref[...]

    @pl.when(slot > 0)
    def _():
        rows = weight.shape[0] // len(pieces)
        mine = lax.axis_index("seq") if len(pieces) > 1 else 0
        start = pl.multiple_of((slot - 1) * rows, 16)
        for r, piece in enumerate(pieces):
            weight[pl.ds(pl.multiple_of((mine ^ r) * rows, rows), rows), :] = piece[pl.ds(start, rows), :]


def gather_vectors(pieces, rows, slots, vectors):
    for r, piece in enumerate(pieces):
        block = piece[(slots - 1) * rows :, :256].astype(F32)
        for a in range(slots):
            z = lax.rem(lax.axis_index("head") + slots - a, slots)
            source = own_device(r % 2, r // 2, slots) + z
            for i in range(2):
                part = block[a : a + 1, 128 * i : 128 * (i + 1)]
                vectors[pl.ds(source, 1), i : i + 1, :] = part[None]


def forward_kernel(count, slots, tokens_ref, own_ref, *refs):
    pieces, refs = refs[:count], refs[count:]
    if count == 1:
        given, refs = refs[0], refs[1:]
    normed_ref, rows_ref, residual_ref, second_ref, mark, heads_ref, weight = refs[:7]
    keep, staged, vectors = refs[7:-2], refs[-2], refs[-1]
    slot = pl.program_id(0)
    length, width = tokens_ref.shape
    share = width // vectors.shape[0]
    tiles = [slice(r, r + 256) for r in range(0, length, 256)]

    @pl.when(slot == 0)
    def _():
        if count == 1:
            vectors[...] = given[:, :8, :].astype(F32)
        else:
            gather_vectors(pieces, weight.shape[0] // count, slots, vectors)
        for i in range(9):
            part = low(vectors[:, 0 if i < 5 else 1, :])
            rows_ref[i : i + 1, :] = spread(part, (i if i < 5 else i - 5) * share, share, width)
        gain, shift = rows_ref[0:1, :], rows_ref[1:2, :]
        for rows in tiles:
            tokens = tokens_ref[rows, :].astype(F32)
            normal, _ = norm_parts(tokens)
            normed_ref[rows, :] = low(normal * gain + shift)
            residual_ref[rows, :] = tokens
        mark[0] = 1.0

    fill(weight, own_ref, pieces, slot)
    attend_forward(normed_ref, weight[:width, :], list(keep) + [staged])
    heads_ref[...] = staged[...]
    residual_ref[...] += nn(staged[...], weight[width:, :])

    @pl.when(slot == slots - 1)
    def _():
        gain, shift = rows_ref[2:3, :], rows_ref[3:4, :]
        for rows in tiles:
            normal, _ = norm_parts(residual_ref[rows, :])
            second_ref[rows, :] = low(normal * gain + shift)


def forward(tokens, own, pieces, vectors, devices, slots):
    length, width = tokens.shape
    shape = jax.ShapeDtypeStruct
    operands = [tokens, own, *pieces, *vectors]
    outs = [
        shape((length, width), BF16),
        shape((16, width), F32),
        shape((length, width), F32),
        shape((length, width), BF16),
    ]
    stacked_outs = [shape((slots, length, PAIR), BF16), pltpu.HBM((slots, width + PAIR, 4 * PAIR), BF16)]
    stacked_outs += kept_shapes(length, (slots,))
    made = pl.pallas_call(
        functools.partial(forward_kernel, len(pieces), slots),
        grid=(slots,),
        out_shape=outs + [MARK] + stacked_outs,
        in_specs=[fixed(o.shape) for o in operands],
        out_specs=[fixed(o.shape) for o in outs] + [mark_spec()] + by_step(stacked_outs),
        scratch_shapes=[pltpu.VMEM((length, PAIR), BF16), pltpu.VMEM((devices, 8, 128), F32)],
        compiler_params=params(44),
        cost_estimate=cost(17),
        name="attend_forward",
    )(*operands)
    return made[:5], made[5:]


GELU_A = 0.7978845608028654
GELU_B = 0.044715


def gelu_both(u):
    square = u * u
    bend = jnp.tanh(GELU_A * (u + GELU_B * (square * u)))
    half = 0.5 * (1.0 + bend)
    slope = half + 0.5 * u * (1.0 - bend * bend) * (GELU_A * (1.0 + 3.0 * GELU_B * square))
    return u * half, slope


def weight_copies(block, pieces, weights, sems):
    if len(pieces) == 1:
        return [pltpu.make_async_copy(pieces[0].at[block], weights.at[block], sems.at[block, 0])]
    copies = []
    for r, piece in enumerate(pieces):
        slots = piece.shape[0]
        copies.append(
            pltpu.make_async_copy(
                piece.at[:, pl.ds(2 * block, 2)],
                weights.at[block, pl.ds(own_device(r % 2, r // 2, slots), slots)],
                sems.at[block, len(copies)],
            )
        )
    return copies


def grad_copies(block, grads, outs, sems):
    if len(outs) == 1:
        return [pltpu.make_async_copy(grads.at[block], outs[0].at[block], sems.at[block, 0])]
    copies = []
    for core, out in enumerate(outs):
        chips, slots = out.shape[:2]
        for chip in range(chips):
            target = (2 * chip + ((lax.axis_index("seq") & 1) ^ core)) * slots
            copies.append(
                pltpu.make_async_copy(
                    grads.at[block, pl.ds(target, slots)],
                    out.at[chip, :, block],
                    sems.at[block, len(copies)],
                )
            )
    return copies


def ffn_kernel(count, second_ref, rows_ref, cotangent_ref, residual_hbm, *refs):
    pieces = refs[:count]
    result_hbm, branch_hbm, sums_ref = refs[count : count + 3]
    outs = refs[count + 3 : -11]
    (weights, grads, residual, total, back, result, branch, in_sems, out_sems, residual_sem, tile_sems) = refs[-11:]
    k = pl.program_id(0)
    length, width = second_ref.shape
    tiles = [slice(r, r + 256) for r in range(0, length, 256)]
    fetch = pltpu.make_async_copy(residual_hbm, residual, residual_sem)

    def leave(rows):
        tile = rows.start // 256
        return [
            pltpu.make_async_copy(source.at[rows, :], target.at[rows, :], tile_sems.at[i, tile])
            for i, (source, target) in enumerate([(result, result_hbm), (branch, branch_hbm)])
        ]

    @pl.when(k == 0)
    def _():
        for block in range(4):
            for copy in weight_copies(block, pieces, weights, in_sems):
                copy.start()
        fetch.start()
        total[...] = jnp.zeros_like(total)
        back[...] = jnp.zeros_like(back)

    for block in range(4):

        @pl.when(k == block)
        def _(block=block):
            for copy in weight_copies(block, pieces, weights, in_sems):
                copy.wait()

    expand = weights[k, :, 0].reshape(width, width)
    shrink = weights[k, :, 1].reshape(width, width)
    bias = rows_ref[pl.ds(5 + k, 1), :]
    bias_grad = jnp.zeros((1, width), F32)
    acts, hids = [], []
    for rows in tiles:
        hidden = nt(second_ref[rows, :], expand) + bias
        pull = nn(cotangent_ref[rows, :], shrink)
        value, slope = gelu_both(hidden)
        activated = low(value)
        hidden_grad = low(pull * slope)
        bias_grad = bias_grad + jnp.sum(hidden_grad.astype(F32), axis=0, keepdims=True)
        total[rows, :] += nt(activated, shrink)
        back[rows, :] += nn(hidden_grad, expand)
        acts.append(activated)
        hids.append(hidden_grad)
    sums_ref[pl.ds(5 + k, 1), :] = bias_grad
    grads[k, :, 1] = low(tn(cotangent_ref[...], jnp.concatenate(acts, axis=0))).reshape(
        width // 16, 16, width
    )
    grads[k, :, 0] = low(tn(jnp.concatenate(hids, axis=0), second_ref[...])).reshape(width // 16, 16, width)
    for block in range(4):

        @pl.when(k == block)
        def _(block=block):
            for copy in grad_copies(block, grads, outs, out_sems):
                copy.start()

    @pl.when(k == 3)
    def _():
        fetch.wait()
        gain, bias = rows_ref[2:3, :], rows_ref[4:5, :]
        gain_grad = jnp.zeros((1, width), F32)
        shift_grad = jnp.zeros((1, width), F32)
        outer = jnp.zeros((1, width), F32)
        for rows in tiles:
            base = residual[rows, :]
            result[rows, :] = low(base + total[rows, :] + bias)
            grad = back[rows, :]
            normal, rate = norm_parts(base)
            upstream = cotangent_ref[rows, :].astype(F32)
            gain_grad = gain_grad + jnp.sum(grad * normal, axis=0, keepdims=True)
            shift_grad = shift_grad + jnp.sum(grad, axis=0, keepdims=True)
            outer = outer + jnp.sum(upstream, axis=0, keepdims=True)
            branch[rows, :] = low(upstream + norm_back(grad, normal, rate, gain))
            for copy in leave(rows):
                copy.start()
        sums_ref[0:2, :] = jnp.zeros((2, width), F32)
        sums_ref[2:3, :] = gain_grad
        sums_ref[3:4, :] = shift_grad
        sums_ref[4:5, :] = outer
        for rows in tiles:
            for copy in leave(rows):
                copy.wait()
        for block in range(4):
            for copy in grad_copies(block, grads, outs, out_sems):
                copy.wait()


def feed_forward(second, rows, cotangent, residual, pieces, grad_shapes):
    length, width = second.shape
    shape = jax.ShapeDtypeStruct
    weights = (4, width // 16, 2, 16, width)
    outs = [
        shape((length, width), BF16),
        shape((length, width), BF16),
        shape((16, width), F32),
    ]
    return pl.pallas_call(
        functools.partial(ffn_kernel, len(pieces)),
        grid=(4,),
        out_shape=outs + [shape(s, BF16) for s in grad_shapes],
        in_specs=[fixed(o.shape) for o in (second, rows, cotangent)] + anywhere([residual, *pieces]),
        out_specs=anywhere(outs[:2]) + [fixed(outs[2].shape)] + anywhere(grad_shapes),
        scratch_shapes=[
            pltpu.VMEM(weights, BF16),
            pltpu.VMEM(weights, BF16),
            pltpu.VMEM((length, width), F32),
            pltpu.VMEM((length, width), F32),
            pltpu.VMEM((length, width), F32),
            pltpu.VMEM((length, width), BF16),
            pltpu.VMEM((length, width), BF16),
            pltpu.SemaphoreType.DMA((4, 8)),
            pltpu.SemaphoreType.DMA((4, 8)),
            pltpu.SemaphoreType.DMA,
            pltpu.SemaphoreType.DMA((2, length // 256)),
        ],
        compiler_params=params(44),
        cost_estimate=cost(22),
        name="feed_forward",
    )(second, rows, cotangent, residual, *pieces)


def heads_kernel(branch_ref, weight_ref, heads_ref, grad_ref, output_grad_ref, mark):
    slots = heads_ref.shape[0]
    weight = weight_ref[...].reshape(slots * PAIR, weight_ref.shape[2])
    grad = low(nt(branch_ref[...], weight))
    output_grad = low(tn(branch_ref[...], jnp.concatenate([heads_ref[a] for a in range(slots)], axis=1)))
    for a in range(slots):
        grad_ref[a] = grad[:, a * PAIR : (a + 1) * PAIR]
        output_grad_ref[a] = output_grad[:, a * PAIR : (a + 1) * PAIR]
    mark[0] = 1.0


def heads_back(branch, weights, heads):
    slots = heads.shape[0]
    length, width = branch.shape
    shape = jax.ShapeDtypeStruct
    outs = [shape((slots, length, PAIR), BF16), shape((slots, width, PAIR), BF16)]
    return pl.pallas_call(
        heads_kernel,
        grid=(1,),
        out_shape=outs + [MARK],
        in_specs=[
            fixed((length, width)),
            pl.BlockSpec((slots, PAIR, width), lambda a: (0, width // PAIR, 0)),
        ]
        + [fixed(heads.shape)],
        out_specs=[fixed(o.shape) for o in outs] + [mark_spec()],
        compiler_params=params(16),
        cost_estimate=cost(4),
        name="heads_back",
    )(branch, weights, heads)


def pair_grads(grad_ref, output_grad_ref, normed_ref, kept, backs, made):
    attend_backward(grad_ref, kept, backs)
    made[:, : 4 * PAIR] = low(tn(normed_ref[...], backs[...]))
    made[:, 4 * PAIR :] = output_grad_ref[...]


def leave_copies(slot, made, outs, sems):
    if len(outs) == 1:
        return [pltpu.make_async_copy(made, outs[0].at[slot], sems.at[0])]
    seq = lax.axis_index("seq")
    chips = outs[0].shape[0]
    rows = made.shape[0] // (2 * chips)
    copies = []
    for chip in range(chips):
        for core, out in enumerate((outs[0].at[chip], outs[1 + chip])):
            start = pl.multiple_of((seq ^ (2 * chip + core)) * rows, rows)
            copies.append(
                pltpu.make_async_copy(
                    made.at[pl.ds(start, rows), :],
                    out.at[pl.ds(pl.multiple_of(slot * rows, rows), rows), :],
                    sems.at[len(copies)],
                )
            )
    return copies


def back_kernel(waits, parts_out, slots, normed_ref, rows_ref, before_ref, tokens_hbm, residual_grad_hbm, *refs):
    refs = refs[waits:]
    weight, grad_ref, output_grad_ref, kept, refs = refs[0], refs[1], refs[2], refs[3:12], refs[12:]
    input_grad_ref, sums_ref, outs, mark = refs[0], refs[1], refs[2 : 2 + parts_out], refs[2 + parts_out]
    backs, made, total, tokens, residual_grad, vector_blocks, sems, out_sems = refs[3 + parts_out :]
    length, width = normed_ref.shape
    devices = sums_ref.shape[0]
    share = width // devices
    step, steps = pl.program_id(0), slots
    copies = [
        pltpu.make_async_copy(tokens_hbm, tokens, sems.at[0]),
        pltpu.make_async_copy(residual_grad_hbm, residual_grad, sems.at[1]),
    ]

    @pl.when(step == 0)
    def _():
        for copy in copies:
            copy.start()
        total[...] = jnp.zeros_like(total)
        mark[0] = 1.0

    parity = lax.rem(step, 2)

    @pl.when(step >= 2)
    def _():
        for copy in leave_copies(step - 2, made.at[parity], outs, out_sems.at[parity]):
            copy.wait()

    pair_grads(grad_ref, output_grad_ref, normed_ref, kept, backs, made.at[parity])
    for copy in leave_copies(step, made.at[parity], outs, out_sems.at[parity]):
        copy.start()
    total[...] += nt(backs[...], weight[:width, :])

    @pl.when(step == steps - 1)
    def _():
        for copy in copies:
            copy.wait()
        gain = rows_ref[0:1, :]
        gain_grad = jnp.zeros((1, width), F32)
        shift_grad = jnp.zeros((1, width), F32)
        for rows in [slice(r, r + 256) for r in range(0, length, 256)]:
            grad = total[rows, :]
            normal, rate = norm_parts(tokens[rows, :].astype(F32))
            gain_grad = gain_grad + jnp.sum(grad * normal, axis=0, keepdims=True)
            shift_grad = shift_grad + jnp.sum(grad, axis=0, keepdims=True)
            input_grad_ref[rows, :] = low(residual_grad[rows, :].astype(F32) + norm_back(grad, normal, rate, gain))
        small = [gain_grad, shift_grad] + [before_ref[i : i + 1, :] for i in range(2, 5)]
        sums_ref[:, :128] = collect(small, devices, share)
        sums_ref[:, 128:] = collect([before_ref[i : i + 1, :] for i in range(5, 9)], devices, share)
        leaving = []
        if parts_out > 1:
            z, chips = lax.axis_index("head"), outs[0].shape[0]
            for chip in range(chips):
                for core, out in enumerate((outs[0].at[chip], outs[1 + chip])):
                    n = len(leaving)
                    rows = [
                        sums_ref[pl.ds(own_device(core, chip, steps) + lax.rem(z + steps - a, steps), 1), :]
                        for a in range(steps)
                    ]
                    block = jnp.concatenate(rows + [jnp.zeros((16 - steps, 256), F32)], axis=0)
                    vector_blocks[n] = vector_rows(block, made.shape[2])
                    leaving.append(
                        pltpu.make_async_copy(
                            vector_blocks.at[n], out.at[pl.ds(out.shape[0] - 16, 16), :], sems.at[2 + n]
                        )
                    )
        for copy in leaving:
            copy.start()
        for last in (steps - 2, steps - 1):
            for copy in leave_copies(last, made.at[last % 2], outs, out_sems.at[last % 2]):
                copy.wait()
        for copy in leaving:
            copy.wait()


def backward(normed, rows, before, tokens, residual_grad, devices, waits, members, grad_shapes):
    length, width = normed.shape
    slots = members[0].shape[0]
    shape = jax.ShapeDtypeStruct
    outs = [shape((length, width), BF16), shape((devices, 256), F32)]
    grads = [shape(s, BF16) for s in grad_shapes]
    large = [tokens, residual_grad]
    return pl.pallas_call(
        functools.partial(back_kernel, len(waits), len(grad_shapes), slots),
        grid=(slots,),
        out_shape=outs + grads + [MARK],
        in_specs=[fixed(o.shape) for o in (normed, rows, before)] + anywhere(large + waits) + by_step(members),
        out_specs=[fixed(o.shape) for o in outs] + anywhere(grads) + [mark_spec()],
        scratch_shapes=[
            pltpu.VMEM((length, 4 * PAIR), BF16),
            pltpu.VMEM((2, width, 5 * PAIR), BF16),
            pltpu.VMEM((length, width), F32),
        ]
        + [pltpu.VMEM((length, width), m.dtype) for m in large]
        + [
            pltpu.VMEM((8, 16, 5 * PAIR), BF16),
            pltpu.SemaphoreType.DMA((10,)),
            pltpu.SemaphoreType.DMA((2, 8)),
        ],
        compiler_params=params(),
        cost_estimate=cost(27),
        name="attend_back",
    )(normed, rows, before, *large, *waits, *members)


def after(value, *others):
    return pl.pallas_call(
        lambda *refs: None,
        out_shape=jax.ShapeDtypeStruct(value.shape, value.dtype),
        in_specs=anywhere((value,) + others),
        out_specs=anywhere([value])[0],
        input_output_aliases={0: 0},
        name="after",
    )(value, *others)


def vector_values(block):
    return block[:, :256].astype(F32) + block[:, 256:512].astype(F32)


def vector_rows(values, width):
    high = low(values)
    rest = jnp.zeros((values.shape[0], width - 512), BF16)
    return jnp.concatenate([high, low(values - high.astype(F32)), rest], axis=1)


def join_kernel(chips, slots, ffn_ref, keep_ref, *refs):
    others, ffn_outs, outs = refs[:chips], refs[chips : chips + slots], refs[chips + slots :]
    z = lax.axis_index("head")
    for a, out in enumerate(ffn_outs):
        place = lax.rem(z + a, slots)
        out[...] = low(add(*[ffn_ref[c, pl.ds(place, 1)][0] for c in range(chips)]))
    body = keep_ref.shape[1] - 16
    for chip, out in enumerate(outs):
        out[:body, :] = low(add(keep_ref[chip, :body, :], others[chip][:body, :]))
        values = vector_values(keep_ref[chip, body:, :]) + vector_values(others[chip][body:, :])
        out[body:, :] = vector_rows(values, out.shape[1])


def join(ffn, keep, others):
    shape = jax.ShapeDtypeStruct
    chips, slots = ffn.shape[:2]
    operands = [ffn, keep, *others]
    outs = [shape(ffn.shape[2:], BF16)] * slots + [shape(keep.shape[1:], BF16)] * chips
    made = pl.pallas_call(
        functools.partial(join_kernel, chips, slots),
        grid=(1,),
        out_shape=outs,
        in_specs=[fixed(o.shape) for o in operands],
        out_specs=[fixed(o.shape) for o in outs],
        compiler_params=params(),
        cost_estimate=cost(3),
        name="join",
    )(*operands)
    return made[:slots], made[slots:]


def sum_plane_kernel(slots, pairs, mine_ref, vector_ref, sends, mark):
    rows = mine_ref.shape[0]
    values = functools.reduce(lambda x, y: x + y, [vector_values(p[slots * rows :, :]) for p in pairs])
    vector_ref[...] = values[:8, :]
    for a in range(slots):
        mine = add(*[p[a * rows : (a + 1) * rows, :] for p in pairs])
        if a == 0:
            mine_ref[...] = mine
        else:
            sends[a - 1][:rows, :] = low(mine)
            sends[a - 1][rows:, :] = vector_rows(jnp.broadcast_to(values[a : a + 1, :], (16, 256)), mine.shape[1])
    mark[0] = 1.0


def sum_plane(pairs, slots, waits):
    shape = jax.ShapeDtypeStruct
    rows, columns = (pairs[0].shape[0] - 16) // slots, pairs[0].shape[1]
    outs = [shape((rows, columns), F32), shape((8, 256), F32)]
    outs += [shape((rows + 16, columns), BF16)] * (slots - 1)

    def kernel(*refs):
        made = refs[len(pairs) + len(waits) :]
        sum_plane_kernel(slots, refs[: len(pairs)], made[0], made[1], made[2:-1], made[-1])

    return pl.pallas_call(
        kernel,
        grid=(1,),
        out_shape=outs + [MARK],
        in_specs=[fixed(p.shape) for p in pairs] + anywhere(waits),
        out_specs=[fixed(o.shape) for o in outs] + [mark_spec()],
        compiler_params=params(12),
        cost_estimate=cost(2),
        name="sum_plane",
    )(*pairs, *waits)


def settle_kernel(ffn, expand_ref, shrink_ref):
    blocks, _, share, width = ffn[0].shape
    total = add(*[f[...] for f in ffn])
    expand_ref[...] = total[:, 0].reshape(blocks * share, width).T
    for i in range(blocks):
        shrink_ref[:, i] = total[i, 1].T.reshape(width // share, share, share)


def settle(ffn, wait):
    shape = jax.ShapeDtypeStruct
    slots = len(ffn)
    blocks, _, share, width = ffn[0].shape
    outs = [shape((width, blocks * share), F32), shape((width // share, blocks, share, share), F32)]

    def kernel(*refs):
        settle_kernel(refs[:slots], *refs[slots + 1 :])

    return pl.pallas_call(
        kernel,
        grid=(1,),
        out_shape=outs,
        in_specs=[fixed(f.shape) for f in ffn] + anywhere([wait]),
        out_specs=[fixed(o.shape) for o in outs],
        compiler_params=params(12),
        cost_estimate=cost(3),
        name="settle",
    )(*ffn, wait)


def flip(count, bit):
    return [(i, i ^ bit) for i in range(count)]


def turn(count, by):
    return [(i, (i + by) % count) for i in range(count)]


def add(*members):
    return functools.reduce(lambda a, b: a + b, [m.astype(F32) for m in members])


def to_mate(shares, seqs):
    return lax.ppermute(shares, "seq", flip(seqs, 1))


def over_chips(shares, chips, seqs):
    return [shares] + [lax.ppermute(shares, "seq", flip(seqs, 2 * r)) for r in range(1, chips)]


def over_cores(held, seqs):
    return [member for h in held for member in (h, to_mate(h, seqs))]


def to_chips(shares, seqs):
    plane = [list(range(core, seqs, 2)) for core in range(2)]
    return lax.all_to_all(shares, "seq", 0, 0, axis_index_groups=plane, tiled=True)


def from_chips(sends, seqs):
    return [lax.ppermute(m, "seq", flip(seqs, 2 * r + 2)) for r, m in enumerate(sends)]


def body(
    inputs,
    attn_gain,
    attn_shift,
    query_weight,
    key_weight,
    value_weight,
    control_weight,
    output_weight,
    ffn_gain,
    ffn_shift,
    expand_weight,
    expand_bias,
    shrink_weight,
    shrink_bias,
    cotangent,
):
    seqs, slots = lax.axis_size("seq"), lax.axis_size("head")
    devices = seqs * slots
    chips = seqs // 2
    width = inputs.shape[1]
    share = width // devices
    hidden_share = expand_weight.shape[1]
    z = lax.axis_index("head")
    direct = seqs == 8 and slots == 4 and share == 16 and hidden_share == 4 * share

    own = jnp.concatenate(
        [
            jnp.concatenate([query_weight, key_weight, value_weight, control_weight], axis=1),
            output_weight,
        ],
        axis=0,
    )
    places = [(attn_gain, 0), (attn_shift, 1), (ffn_gain, 2), (ffn_shift, 3), (shrink_bias, 4)]
    row = functools.reduce(
        lambda a, b: a + b,
        [jnp.pad(m, (i * share, width - (i + 1) * share)) for m, i in places]
        + [jnp.pad(expand_bias, (128, width - 128 - hidden_share))],
    )
    block = jnp.pad(row[None, :], ((0, 15), (0, 0)))
    expand_t = expand_weight.T.reshape(4, share, width)
    shrink_t = shrink_weight.reshape(devices, 4, share, share).transpose(1, 3, 0, 2).reshape(4, share, width)
    load = jnp.stack([expand_t, shrink_t], axis=1)
    if direct:
        rows = own.shape[0] // seqs
        piece = lax.dynamic_slice_in_dim(own, lax.axis_index("seq") * rows, rows, axis=0)
        piece = jnp.concatenate([piece, block], axis=0)
        came = [lax.ppermute(piece, "head", turn(slots, a)) for a in range(1, slots)]
        for a in range(1, slots):
            block = block + jnp.pad(came[a - 1][rows : rows + 1], ((a, 15 - a), (0, 0)))
        near = jnp.concatenate([c[:rows] for c in came] + [block], axis=0)
        pieces, vectors = over_cores(over_chips(near, chips, seqs), seqs), []
        load = jnp.broadcast_to(load.reshape(1, 8, share, width), (slots, 8, share, width))
        load = lax.all_to_all(after(load, near), "head", 0, 0, tiled=True)
        held = over_chips(load, chips, seqs)
        tall = (slots * width // seqs + 16, 5 * PAIR)
        pair_shapes = [(chips,) + tall] + [tall] * chips
        ffn_shapes = [(chips, slots, 4, 2, 16, width)] * 2
    else:
        every = lax.all_gather(own, "head", axis=0, tiled=False)
        pieces = [jnp.concatenate([every[(z + slots - a) % slots] for a in range(1, slots)], axis=0)]
        block = jnp.concatenate([block[:1, :128], block[:1, 128:256], block[2:, :128]], axis=0)
        vectors = [lax.all_gather(block, ("seq", "head"), axis=0, tiled=False)]
        both = lax.all_gather(load, ("seq", "head"), axis=2, tiled=True)
        ffn_pieces = [both.reshape(4, 2, width // 16, 16, width).transpose(0, 2, 1, 3, 4)]
        pair_shapes = [(slots, width, 5 * PAIR)]
        ffn_shapes = [ffn_pieces[0].shape]

    (normed, rows, residual, second, _), (heads, weights, *members) = forward(
        inputs, own, pieces, vectors, devices, slots
    )
    if direct:
        ffn_pieces = over_cores(held[:-1] + [after(held[-1], second)], seqs)
    result, branch, sums, *ffn_grads = feed_forward(
        second, rows, cotangent, residual, ffn_pieces, ffn_shapes
    )
    heads_grad, output_grad, mark = heads_back(branch, weights, heads)
    members = [weights, heads_grad, output_grad, *members]
    waits = []
    if direct:
        ffn_mine = low(add(ffn_grads[0], to_mate(ffn_grads[1], seqs)) * mark[0])
        waits = [ffn_mine]
    input_grad, sums, *pair_grads, _ = backward(
        normed, rows, sums, inputs, branch, devices, waits, members, pair_shapes
    )

    if direct:
        keep, *sends = pair_grads
        ffn, pairs = join(to_chips(ffn_mine, seqs), keep, [to_mate(m, seqs) for m in sends])
        ffn = [ffn[0]] + [lax.ppermute(ffn[a], "head", turn(slots, a)) for a in range(1, slots)]
        pairs = [pairs[0]] + from_chips(pairs[1:], seqs)
        mine, sums, *sends, wait = sum_plane(pairs, slots, ffn[1:])
        expand_grad, shrink_grad = settle(ffn, wait)
        came = [lax.ppermute(m, "head", turn(slots, slots - 1 - a)) for a, m in enumerate(sends)]
        rows = mine.shape[0]
        pair_sum = add(mine, *[c[:rows] for c in came])
        sums = sums[0] + functools.reduce(
            lambda a, b: a + b, [c[rows, :256].astype(F32) + c[rows, 256:512].astype(F32) for c in came]
        )
    else:
        ffn_sum = lax.psum_scatter(
            ffn_grads[0].astype(F32).transpose(0, 2, 1, 3, 4).reshape(4, 2, width, width), ("seq", "head"), scatter_dimension=2, tiled=True
        )
        every = pair_grads[0].astype(F32)
        every = jnp.stack([every[(z + slots - p) % slots] for p in range(slots)])
        pair_sum = lax.psum_scatter(every, "head", scatter_dimension=0, tiled=False)
        pair_sum = lax.psum_scatter(pair_sum, "seq", scatter_dimension=0, tiled=True)

        sums = jnp.sum(
            lax.all_to_all(sums.reshape(devices, 1, 256), ("seq", "head"), 0, 0, tiled=True), axis=(0, 1)
        )
        expand_grad = ffn_sum[:, 0].reshape(hidden_share, width).T
        shrink_grad = ffn_sum[:, 1].reshape(4, share, devices, share).transpose(2, 0, 3, 1)

    vector = [sums[i * share : (i + 1) * share] for i in range(5)]
    return (
        result,
        input_grad,
        vector[0],
        vector[1],
        pair_sum[:, :PAIR],
        pair_sum[:, PAIR : 2 * PAIR],
        pair_sum[:, 2 * PAIR : 3 * PAIR],
        pair_sum[:, 3 * PAIR : 4 * PAIR],
        pair_sum[:, 4 * PAIR :].T,
        vector[2],
        vector[3],
        expand_grad,
        sums[128 : 128 + hidden_share],
        shrink_grad.reshape(devices * hidden_share, share),
        vector[4],
    )


def solution(mesh):
    placed = (
        P(("seq", "head"), None),
        P(("seq", "head")),
        P(("seq", "head")),
        P(None, "head"),
        P(None, "head"),
        P(None, "head"),
        P(None, "head"),
        P("head", None),
        P(("seq", "head")),
        P(("seq", "head")),
        P(None, ("seq", "head")),
        P(("seq", "head")),
        P(None, ("seq", "head")),
        P(("seq", "head")),
        P(("seq", "head"), None),
    )
    return jax.shard_map(
        body,
        mesh=mesh,
        in_specs=placed,
        out_specs=(
            P(("seq", "head"), None),
            P(("seq", "head"), None),
            P(("seq", "head")),
            P(("seq", "head")),
            P("seq", "head"),
            P("seq", "head"),
            P("seq", "head"),
            P("seq", "head"),
            P("head", "seq"),
            P(("seq", "head")),
            P(("seq", "head")),
            P(None, ("seq", "head")),
            P(("seq", "head")),
            P(None, ("seq", "head")),
            P(("seq", "head")),
        ),
        check_vma=False,
    )
```

```python
import functools

import jax
import jax.numpy as jnp
from jax import lax
from jax.experimental import pallas as pl
from jax.experimental.pallas import tpu as pltpu
from jax.sharding import PartitionSpec as P

EPSILON = 1e-5
CHUNK = 128
PAIR = 128
F32 = jnp.float32
BF16 = jnp.bfloat16


def nn(a, b):
    return lax.dot_general(a, b, (((1,), (0,)), ((), ())), preferred_element_type=F32)


def nt(a, b):
    return lax.dot_general(a, b, (((1,), (1,)), ((), ())), preferred_element_type=F32)


def tn(a, b):
    return lax.dot_general(a, b, (((0,), (0,)), ((), ())), preferred_element_type=F32)


def low(v):
    return v.astype(BF16)


def iota(shape, axis):
    return lax.broadcasted_iota(jnp.int32, shape, axis)


def first_half(shape):
    return iota(shape, 1) < PAIR // 2


def stacked(block):
    left = first_half(block.shape)
    zero = jnp.zeros_like(block)
    return jnp.concatenate([jnp.where(left, block, zero), jnp.where(left, zero, block)], axis=0)


def parts(v):
    high = low(v)
    return jnp.concatenate([high, low(v - high.astype(F32))], axis=1)


def whole(v):
    return v[:, :PAIR] + v[:, PAIR:]


def head_block(shape=(PAIR, PAIR)):
    return (iota(shape, 0) < PAIR // 2) == (iota(shape, 1) < PAIR // 2)


def causal_pair():
    return iota((CHUNK, 2 * CHUNK), 0) >= (iota((CHUNK, 2 * CHUNK), 1) & (CHUNK - 1))


def causal_pair_t():
    return iota((CHUNK, 2 * CHUNK), 0) <= (iota((CHUNK, 2 * CHUNK), 1) & (CHUNK - 1))


def ones_where(mask):
    return low(jnp.where(mask, 1.0, 0.0))


def norm_parts(tokens):
    average = jnp.mean(tokens, axis=-1, keepdims=True)
    centred = tokens - average
    rate = lax.rsqrt(jnp.mean(centred * centred, axis=-1, keepdims=True) + EPSILON)
    return centred * rate, rate


def norm_back(grad, normal, rate, gain):
    w = grad * gain
    return rate * (
        w
        - jnp.mean(w, axis=-1, keepdims=True)
        - normal * jnp.mean(w * normal, axis=-1, keepdims=True)
    )


def chunks(length):
    return [slice(c * CHUNK, (c + 1) * CHUNK) for c in range(length // CHUNK)]


def attend_forward(normed, weight, keep):
    q_ref, k_ref, v_ref, powers_ref, inverse_ref, score_ref, prob_ref, key_state, value_state, heads_ref = keep
    cuts = chunks(normed.shape[0])
    tri = ones_where(iota((CHUNK, CHUNK), 0) >= iota((CHUNK, CHUNK), 1))
    same = head_block()
    both = jnp.concatenate([ones_where(same)] * 2, axis=0)
    causal = causal_pair()
    left = first_half((CHUNK, PAIR))
    carried = jnp.zeros((1, PAIR), F32)
    key_sum = jnp.zeros((PAIR, PAIR), F32)
    value_sum = jnp.zeros((PAIR, PAIR), F32)

    def masked(product):
        return low(jnp.where(causal, product, 0.0))

    def lift(score):
        top_a = jnp.max(jnp.where(left, score, -jnp.inf), axis=-1, keepdims=True)
        top_b = jnp.max(jnp.where(left, -jnp.inf, score), axis=-1, keepdims=True)
        return jnp.exp(score - jnp.where(left, top_a, top_b))

    for first in range(0, len(cuts), 8):
        group = list(range(first, min(first + 8, len(cuts))))
        each = range(len(group))
        rows = slice(group[0] * CHUNK, (group[-1] + 1) * CHUNK)
        made = nn(normed[rows, :], weight)
        cut = [made[i * CHUNK : (i + 1) * CHUNK, :] for i in each]
        q = [low(low(m[:, :PAIR]).astype(F32) * 0.125) for m in cut]
        k = [low(m[:, PAIR : 2 * PAIR]) for m in cut]
        v = [low(m[:, 2 * PAIR : 3 * PAIR]) for m in cut]
        powers = [jnp.exp(m[:, 3 * PAIR :]) for m in cut]
        powers_low = [low(p) for p in powers]
        local = [whole(nn(tri, parts(p))) for p in powers]
        scored = [masked(nt(q[i], stacked(k[i]))) for i in each]
        inverse = []
        for i in each:
            running = local[i] + carried
            carried = running[CHUNK - 1 :, :]
            inverse.append(1.0 / running)
        powers_two = [stacked(m) for m in powers_low]
        for i, c in enumerate(group):
            key_state[c, :, :] = low(jnp.where(same, key_sum, 0.0))
            value_state[c, :, :] = low(jnp.where(same, value_sum, 0.0))
            if c + 1 < len(cuts):
                key_sum = key_sum + tn(k[i], powers_low[i])
                value_sum = value_sum + tn(powers_low[i], v[i])
        score = [
            (nn(scored[i], powers_two[i]) + nn(q[i], key_state[c, :, :])) * inverse[i]
            for i, c in enumerate(group)
        ]
        lifted = [lift(m) for m in score]
        prob = [lifted[i] / nn(parts(lifted[i]), both) for i in each]
        reading = [low(prob[i] * inverse[i]) for i in each]
        mixing = [masked(nt(reading[i], powers_two[i])) for i in each]
        for i, c in enumerate(group):
            q_ref[cuts[c], :] = q[i]
            k_ref[cuts[c], :] = k[i]
            v_ref[cuts[c], :] = v[i]
            powers_ref[cuts[c], :] = powers[i]
            inverse_ref[cuts[c], :] = inverse[i]
            score_ref[cuts[c], :] = score[i]
            prob_ref[cuts[c], :] = prob[i]
        for i, c in enumerate(group):
            heads_ref[cuts[c], :] = low(
                nn(mixing[i], stacked(v[i])) + nn(reading[i], value_state[c, :, :])
            )


def attend_backward(heads_grad, kept, backs):
    q_ref, k_ref, v_ref, powers_ref, inverse_ref, score_ref, prob_ref, key_state, value_state = kept
    cuts = chunks(heads_grad.shape[0])
    same = head_block()
    both = jnp.concatenate([ones_where(same)] * 2, axis=0)
    causal = causal_pair()
    causal_t = causal_pair_t()
    tri_t = ones_where(iota((CHUNK, CHUNK), 0) <= iota((CHUNK, CHUNK), 1))
    after_sum = jnp.zeros((1, PAIR), F32)
    read_sum = jnp.zeros((PAIR, PAIR), F32)
    score_sum = jnp.zeros((PAIR, PAIR), F32)

    def masked(product, mask):
        return low(jnp.where(mask, product, 0.0))

    for first in reversed(range(0, len(cuts), 4)):
        group = list(reversed(range(first, min(first + 4, len(cuts)))))
        load = lambda ref: [ref[cuts[c], :] for c in group]
        q, k, v, grad = load(q_ref), load(k_ref), load(v_ref), load(heads_grad)
        inverse, prob, powers = load(inverse_ref), load(prob_ref), load(powers_ref)
        each = range(len(group))
        powers_low = [low(p) for p in powers]
        reading = [low(prob[i] * inverse[i]) for i in each]
        powers_two, values_two = [stacked(m) for m in powers_low], [stacked(m) for m in v]
        grad_two, reading_two = [stacked(m) for m in grad], [stacked(m) for m in reading]
        mixing_grad = [masked(nt(grad[i], values_two[i]), causal) for i in each]
        reading_grad = [
            nn(mixing_grad[i], powers_two[i]) + nt(grad[i], value_state[group[i], :, :]) for i in each
        ]
        mixing_grad_t = [masked(nt(v[i], grad_two[i]), causal_t) for i in each]
        mixing_t = [masked(nt(powers_low[i], reading_two[i]), causal_t) for i in each]
        read_states = []
        for i in each:
            read_states.append(low(jnp.where(same, read_sum, 0.0)))
            if group[i]:
                read_sum = read_sum + tn(reading[i], grad[i])
        prob_grad = [reading_grad[i] * inverse[i] for i in each]
        weighed = [prob[i] * prob_grad[i] for i in each]
        slots_grad = [weighed[i] - prob[i] * nn(parts(weighed[i]), both) for i in each]
        summed_grad = [low(slots_grad[i] * inverse[i]) for i in each]
        running_grad = [
            -inverse[i] * (weighed[i] + slots_grad[i] * score_ref[cuts[group[i]], :]) for i in each
        ]
        powers_grad = [
            nn(mixing_grad_t[i], reading_two[i]) + nt(v[i], read_states[i]) for i in each
        ]
        for i in each:
            backs[cuts[group[i]], 2 * PAIR : 3 * PAIR] = low(
                nn(mixing_t[i], grad_two[i]) + nn(powers_low[i], read_states[i])
            )
        queries_two, keys_two = [stacked(m) for m in q], [stacked(m) for m in k]
        scored_t = [masked(nt(k[i], queries_two[i]), causal_t) for i in each]
        summed_two = [stacked(m) for m in summed_grad]
        score_states = []
        for i in each:
            score_states.append(low(jnp.where(same, score_sum, 0.0)))
            if group[i]:
                score_sum = score_sum + tn(q[i], summed_grad[i])
        scored_grad = [masked(nt(summed_grad[i], powers_two[i]), causal) for i in each]
        scored_grad_t = [masked(nt(powers_low[i], summed_two[i]), causal_t) for i in each]
        later = [whole(nn(tri_t, parts(running_grad[i]))) for i in each]
        powers_grad = [
            powers_grad[i] + nn(scored_t[i], summed_two[i]) + nn(k[i], score_states[i]) for i in each
        ]
        for i in each:
            rows = cuts[group[i]]
            backs[rows, :PAIR] = low(
                0.125 * (nn(scored_grad[i], keys_two[i]) + nt(summed_grad[i], key_state[group[i], :, :]))
            )
            backs[rows, PAIR : 2 * PAIR] = low(
                nn(scored_grad_t[i], queries_two[i]) + nt(powers_low[i], score_states[i])
            )
            total = later[i] + after_sum
            after_sum = total[:1, :]
            backs[rows, 3 * PAIR :] = low((powers_grad[i] + total) * powers[i])


def kept_shapes(length, lead=()):
    n = length // CHUNK
    shape = pltpu.HBM
    return (
        [shape(lead + (length, PAIR), BF16)] * 3
        + [shape(lead + (length, PAIR), F32)] * 4
        + [shape(lead + (n, PAIR, PAIR), BF16)] * 2
    )


def fixed(shape):
    return pl.BlockSpec(shape, lambda a: (0,) * len(shape))


def one_slot(members, slot):
    return [
        pl.BlockSpec((None,) + s.shape[1:], lambda a, rank=len(s.shape): (slot,) + (0,) * (rank - 1))
        for s in members
    ]


def by_step(members, first=0):
    return [
        pl.BlockSpec((None,) + s.shape[1:], lambda a, rank=len(s.shape): (a + first,) + (0,) * (rank - 1))
        for s in members
    ]


def anywhere(members):
    return [pl.BlockSpec(memory_space=pl.ANY)] * len(members)


def mark_spec():
    return pl.BlockSpec(memory_space=pltpu.SMEM)


MARK = jax.ShapeDtypeStruct((1,), F32)


def cost(micros):
    return pl.CostEstimate(flops=int(micros * 1e9), bytes_accessed=int(micros * 1e6), transcendentals=0)


def params(megabytes=56):
    return pltpu.CompilerParams(vmem_limit_bytes=megabytes * 1024 * 1024)


def select(width, offset, share, total):
    return ones_where(
        iota((width, total), 0) == offset + (iota((width, total), 1) & (share - 1))
    )


def owned(devices, share, total):
    return iota((devices, total), 0) == lax.shift_right_logical(
        iota((devices, total), 1), share.bit_length() - 1
    )


def spread(rows, offset, share, total):
    each = nn(rows, select(rows.shape[1], offset, share, total))
    return jnp.sum(jnp.where(owned(rows.shape[0], share, total), each, 0.0), axis=0, keepdims=True)


def collect(rows, devices, share):
    total = rows[0].shape[1]
    mine = owned(devices, share, total)
    out = jnp.zeros((devices, 128), F32)
    for i, row in enumerate(rows):
        rest = jnp.where(mine, row, 0.0)
        high = low(rest)
        pair = jnp.concatenate([high, low(rest - high.astype(F32))], axis=0)
        made = nt(pair, select(128, i * share, share, total))
        out = out + made[:devices] + made[devices:]
    return out


def own_device(core, chip, slots):
    return (lax.axis_index("seq") ^ (2 * chip + core)) * slots


def fill(weight, own_ref, pieces, slot):
    @pl.when(slot == 0)
    def _():
        weight[...] = own_ref[...]

    @pl.when(slot > 0)
    def _():
        rows = weight.shape[0] // len(pieces)
        mine = lax.axis_index("seq") if len(pieces) > 1 else 0
        start = pl.multiple_of((slot - 1) * rows, 16)
        for r, piece in enumerate(pieces):
            weight[pl.ds(pl.multiple_of((mine ^ r) * rows, rows), rows), :] = piece[pl.ds(start, rows), :]


def gather_vectors(pieces, rows, slots, vectors):
    for r, piece in enumerate(pieces):
        block = piece[(slots - 1) * rows :, :256].astype(F32)
        for a in range(slots):
            z = lax.rem(lax.axis_index("head") + slots - a, slots)
            source = own_device(r % 2, r // 2, slots) + z
            for i in range(2):
                part = block[a : a + 1, 128 * i : 128 * (i + 1)]
                vectors[pl.ds(source, 1), i : i + 1, :] = part[None]


def forward_kernel(count, slots, tokens_ref, own_ref, *refs):
    pieces, refs = refs[:count], refs[count:]
    if count == 1:
        given, refs = refs[0], refs[1:]
    normed_ref, rows_ref, residual_ref, second_ref, mark, heads_ref, weight = refs[:7]
    keep, staged, vectors = refs[7:-2], refs[-2], refs[-1]
    slot = pl.program_id(0)
    length, width = tokens_ref.shape
    share = width // vectors.shape[0]
    tiles = [slice(r, r + 256) for r in range(0, length, 256)]

    @pl.when(slot == 0)
    def _():
        if count == 1:
            vectors[...] = given[:, :8, :].astype(F32)
        else:
            gather_vectors(pieces, weight.shape[0] // count, slots, vectors)
        for i in range(9):
            part = low(vectors[:, 0 if i < 5 else 1, :])
            rows_ref[i : i + 1, :] = spread(part, (i if i < 5 else i - 5) * share, share, width)
        gain, shift = rows_ref[0:1, :], rows_ref[1:2, :]
        for rows in tiles:
            tokens = tokens_ref[rows, :].astype(F32)
            normal, _ = norm_parts(tokens)
            normed_ref[rows, :] = low(normal * gain + shift)
            residual_ref[rows, :] = tokens
        mark[0] = 1.0

    fill(weight, own_ref, pieces, slot)
    attend_forward(normed_ref, weight[:width, :], list(keep) + [staged])
    heads_ref[...] = staged[...]
    residual_ref[...] += nn(staged[...], weight[width:, :])

    @pl.when(slot == slots - 1)
    def _():
        gain, shift = rows_ref[2:3, :], rows_ref[3:4, :]
        for rows in tiles:
            normal, _ = norm_parts(residual_ref[rows, :])
            second_ref[rows, :] = low(normal * gain + shift)


def forward(tokens, own, pieces, vectors, devices, slots):
    length, width = tokens.shape
    shape = jax.ShapeDtypeStruct
    operands = [tokens, own, *pieces, *vectors]
    outs = [
        shape((length, width), BF16),
        shape((16, width), F32),
        shape((length, width), F32),
        shape((length, width), BF16),
    ]
    stacked_outs = [shape((slots, length, PAIR), BF16), pltpu.HBM((slots, width + PAIR, 4 * PAIR), BF16)]
    stacked_outs += kept_shapes(length, (slots,))
    made = pl.pallas_call(
        functools.partial(forward_kernel, len(pieces), slots),
        grid=(slots,),
        out_shape=outs + [MARK] + stacked_outs,
        in_specs=[fixed(o.shape) for o in operands],
        out_specs=[fixed(o.shape) for o in outs] + [mark_spec()] + by_step(stacked_outs),
        scratch_shapes=[pltpu.VMEM((length, PAIR), BF16), pltpu.VMEM((devices, 8, 128), F32)],
        compiler_params=params(44),
        cost_estimate=cost(17),
        name="attend_forward",
    )(*operands)
    return made[:5], made[5:]


GELU_A = 0.7978845608028654
GELU_B = 0.044715


def gelu_both(u):
    square = u * u
    bend = jnp.tanh(GELU_A * (u + GELU_B * (square * u)))
    half = 0.5 * (1.0 + bend)
    slope = half + 0.5 * u * (1.0 - bend * bend) * (GELU_A * (1.0 + 3.0 * GELU_B * square))
    return u * half, slope


def weight_copies(block, pieces, weights, sems):
    if len(pieces) == 1:
        return [pltpu.make_async_copy(pieces[0].at[block], weights.at[block], sems.at[block, 0])]
    copies = []
    for r, piece in enumerate(pieces):
        slots = piece.shape[0]
        copies.append(
            pltpu.make_async_copy(
                piece.at[:, pl.ds(2 * block, 2)],
                weights.at[block, pl.ds(own_device(r % 2, r // 2, slots), slots)],
                sems.at[block, len(copies)],
            )
        )
    return copies


def grad_copies(block, grads, outs, sems):
    if len(outs) == 1:
        return [pltpu.make_async_copy(grads.at[block], outs[0].at[block], sems.at[block, 0])]
    copies = []
    for core, out in enumerate(outs):
        chips, slots = out.shape[:2]
        for chip in range(chips):
            target = (2 * chip + ((lax.axis_index("seq") & 1) ^ core)) * slots
            copies.append(
                pltpu.make_async_copy(
                    grads.at[block, pl.ds(target, slots)],
                    out.at[chip, :, block],
                    sems.at[block, len(copies)],
                )
            )
    return copies


def ffn_kernel(count, second_ref, rows_ref, cotangent_hbm, residual_hbm, *refs):
    pieces = refs[:count]
    result_hbm, branch_hbm, sums_ref = refs[count : count + 3]
    outs = refs[count + 3 : -13]
    (weights, grads, residual, cotangent_ref, total, back, result, branch, in_sems, out_sems, residual_sem, tile_sems, cotangent_sems) = refs[-13:]
    k = pl.program_id(0)
    length, width = second_ref.shape
    tiles = [slice(r, r + 256) for r in range(0, length, 256)]
    fetch = pltpu.make_async_copy(residual_hbm, residual, residual_sem)

    def arrive(rows):
        return pltpu.make_async_copy(
            cotangent_hbm.at[rows, :], cotangent_ref.at[rows, :], cotangent_sems.at[rows.start // 256]
        )

    def leave(rows):
        tile = rows.start // 256
        return [
            pltpu.make_async_copy(source.at[rows, :], target.at[rows, :], tile_sems.at[i, tile])
            for i, (source, target) in enumerate([(result, result_hbm), (branch, branch_hbm)])
        ]

    @pl.when(k == 0)
    def _():
        for copy in weight_copies(0, pieces, weights, in_sems):
            copy.start()
        for rows in tiles:
            arrive(rows).start()
        for block in range(1, 4):
            for copy in weight_copies(block, pieces, weights, in_sems):
                copy.start()
        fetch.start()
        total[...] = jnp.zeros_like(total)
        back[...] = jnp.zeros_like(back)

    for block in range(4):

        @pl.when(k == block)
        def _(block=block):
            for copy in weight_copies(block, pieces, weights, in_sems):
                copy.wait()
            if block == 0:
                for rows in tiles:
                    arrive(rows).wait()

    expand = weights[k, :, 0].reshape(width, width)
    shrink = weights[k, :, 1].reshape(width, width)
    bias = rows_ref[pl.ds(5 + k, 1), :]
    bias_grad = jnp.zeros((1, width), F32)
    acts, hids = [], []
    for rows in tiles:
        hidden = nt(second_ref[rows, :], expand) + bias
        pull = nn(cotangent_ref[rows, :], shrink)
        value, slope = gelu_both(hidden)
        activated = low(value)
        hidden_grad = low(pull * slope)
        bias_grad = bias_grad + jnp.sum(hidden_grad.astype(F32), axis=0, keepdims=True)
        total[rows, :] += nt(activated, shrink)
        back[rows, :] += nn(hidden_grad, expand)
        acts.append(activated)
        hids.append(hidden_grad)
    sums_ref[pl.ds(5 + k, 1), :] = bias_grad
    grads[k, :, 1] = low(tn(cotangent_ref[...], jnp.concatenate(acts, axis=0))).reshape(
        width // 16, 16, width
    )
    grads[k, :, 0] = low(tn(jnp.concatenate(hids, axis=0), second_ref[...])).reshape(width // 16, 16, width)
    for block in range(4):

        @pl.when(k == block)
        def _(block=block):
            for copy in grad_copies(block, grads, outs, out_sems):
                copy.start()

    @pl.when(k == 3)
    def _():
        fetch.wait()
        gain, bias = rows_ref[2:3, :], rows_ref[4:5, :]
        gain_grad = jnp.zeros((1, width), F32)
        shift_grad = jnp.zeros((1, width), F32)
        outer = jnp.zeros((1, width), F32)
        for rows in tiles:
            base = residual[rows, :]
            result[rows, :] = low(base + total[rows, :] + bias)
            grad = back[rows, :]
            normal, rate = norm_parts(base)
            upstream = cotangent_ref[rows, :].astype(F32)
            gain_grad = gain_grad + jnp.sum(grad * normal, axis=0, keepdims=True)
            shift_grad = shift_grad + jnp.sum(grad, axis=0, keepdims=True)
            outer = outer + jnp.sum(upstream, axis=0, keepdims=True)
            branch[rows, :] = low(upstream + norm_back(grad, normal, rate, gain))
            for copy in leave(rows):
                copy.start()
        sums_ref[0:2, :] = jnp.zeros((2, width), F32)
        sums_ref[2:3, :] = gain_grad
        sums_ref[3:4, :] = shift_grad
        sums_ref[4:5, :] = outer
        for rows in tiles:
            for copy in leave(rows):
                copy.wait()
        for block in range(4):
            for copy in grad_copies(block, grads, outs, out_sems):
                copy.wait()


def feed_forward(second, rows, cotangent, residual, pieces, grad_shapes):
    length, width = second.shape
    shape = jax.ShapeDtypeStruct
    weights = (4, width // 16, 2, 16, width)
    outs = [
        shape((length, width), BF16),
        shape((length, width), BF16),
        shape((16, width), F32),
    ]
    return pl.pallas_call(
        functools.partial(ffn_kernel, len(pieces)),
        grid=(4,),
        out_shape=outs + [shape(s, BF16) for s in grad_shapes],
        in_specs=[fixed(o.shape) for o in (second, rows)]
        + [pl.BlockSpec(memory_space=pltpu.HBM)] * (2 + len(pieces)),
        out_specs=anywhere(outs[:2]) + [fixed(outs[2].shape)] + anywhere(grad_shapes),
        scratch_shapes=[
            pltpu.VMEM(weights, BF16),
            pltpu.VMEM(weights, BF16),
            pltpu.VMEM((length, width), F32),
            pltpu.VMEM((length, width), BF16),
            pltpu.VMEM((length, width), F32),
            pltpu.VMEM((length, width), F32),
            pltpu.VMEM((length, width), BF16),
            pltpu.VMEM((length, width), BF16),
            pltpu.SemaphoreType.DMA((4, 8)),
            pltpu.SemaphoreType.DMA((4, 8)),
            pltpu.SemaphoreType.DMA,
            pltpu.SemaphoreType.DMA((2, length // 256)),
            pltpu.SemaphoreType.DMA((length // 256,)),
        ],
        compiler_params=params(44),
        cost_estimate=cost(22),
        name="feed_forward",
    )(second, rows, cotangent, residual, *pieces)


def heads_kernel(branch_ref, weight_ref, heads_ref, grad_ref, output_grad_ref, mark):
    slots = heads_ref.shape[0]
    weight = weight_ref[...].reshape(slots * PAIR, weight_ref.shape[2])
    grad = low(nt(branch_ref[...], weight))
    output_grad = low(tn(branch_ref[...], jnp.concatenate([heads_ref[a] for a in range(slots)], axis=1)))
    for a in range(slots):
        grad_ref[a] = grad[:, a * PAIR : (a + 1) * PAIR]
        output_grad_ref[a] = output_grad[:, a * PAIR : (a + 1) * PAIR]
    mark[0] = 1.0


def heads_back(branch, weights, heads):
    slots = heads.shape[0]
    length, width = branch.shape
    shape = jax.ShapeDtypeStruct
    outs = [shape((slots, length, PAIR), BF16), shape((slots, width, PAIR), BF16)]
    return pl.pallas_call(
        heads_kernel,
        grid=(1,),
        out_shape=outs + [MARK],
        in_specs=[
            fixed((length, width)),
            pl.BlockSpec((slots, PAIR, width), lambda a: (0, width // PAIR, 0)),
        ]
        + [fixed(heads.shape)],
        out_specs=[fixed(o.shape) for o in outs] + [mark_spec()],
        compiler_params=params(16),
        cost_estimate=cost(4),
        name="heads_back",
    )(branch, weights, heads)


def pair_grads(grad_ref, output_grad_ref, normed_ref, kept, backs, made):
    attend_backward(grad_ref, kept, backs)
    made[:, : 4 * PAIR] = low(tn(normed_ref[...], backs[...]))
    made[:, 4 * PAIR :] = output_grad_ref[...]


def leave_copies(slot, made, outs, sems):
    if len(outs) == 1:
        return [pltpu.make_async_copy(made, outs[0].at[slot], sems.at[0])]
    seq = lax.axis_index("seq")
    chips = outs[0].shape[0]
    rows = made.shape[0] // (2 * chips)
    copies = []
    for chip in range(chips):
        for core, out in enumerate((outs[0].at[chip], outs[1 + chip])):
            start = pl.multiple_of((seq ^ (2 * chip + core)) * rows, rows)
            copies.append(
                pltpu.make_async_copy(
                    made.at[pl.ds(start, rows), :],
                    out.at[pl.ds(pl.multiple_of(slot * rows, rows), rows), :],
                    sems.at[len(copies)],
                )
            )
    return copies


def back_kernel(waits, parts_out, slots, normed_ref, rows_ref, before_ref, tokens_hbm, residual_grad_hbm, *refs):
    refs = refs[waits:]
    weight, grad_ref, output_grad_ref, kept, refs = refs[0], refs[1], refs[2], refs[3:12], refs[12:]
    input_grad_ref, sums_ref, outs, mark = refs[0], refs[1], refs[2 : 2 + parts_out], refs[2 + parts_out]
    backs, made, total, tokens, residual_grad, vector_blocks, sems, out_sems = refs[3 + parts_out :]
    length, width = normed_ref.shape
    devices = sums_ref.shape[0]
    share = width // devices
    step, steps = pl.program_id(0), slots
    copies = [
        pltpu.make_async_copy(tokens_hbm, tokens, sems.at[0]),
        pltpu.make_async_copy(residual_grad_hbm, residual_grad, sems.at[1]),
    ]

    @pl.when(step == 0)
    def _():
        for copy in copies:
            copy.start()
        total[...] = jnp.zeros_like(total)
        mark[0] = 1.0

    parity = lax.rem(step, 2)

    @pl.when(step >= 2)
    def _():
        for copy in leave_copies(step - 2, made.at[parity], outs, out_sems.at[parity]):
            copy.wait()

    pair_grads(grad_ref, output_grad_ref, normed_ref, kept, backs, made.at[parity])
    for copy in leave_copies(step, made.at[parity], outs, out_sems.at[parity]):
        copy.start()
    total[...] += nt(backs[...], weight[:width, :])

    @pl.when(step == steps - 1)
    def _():
        for copy in copies:
            copy.wait()
        gain = rows_ref[0:1, :]
        gain_grad = jnp.zeros((1, width), F32)
        shift_grad = jnp.zeros((1, width), F32)
        for rows in [slice(r, r + 256) for r in range(0, length, 256)]:
            grad = total[rows, :]
            normal, rate = norm_parts(tokens[rows, :].astype(F32))
            gain_grad = gain_grad + jnp.sum(grad * normal, axis=0, keepdims=True)
            shift_grad = shift_grad + jnp.sum(grad, axis=0, keepdims=True)
            input_grad_ref[rows, :] = low(residual_grad[rows, :].astype(F32) + norm_back(grad, normal, rate, gain))
        small = [gain_grad, shift_grad] + [before_ref[i : i + 1, :] for i in range(2, 5)]
        sums_ref[:, :128] = collect(small, devices, share)
        sums_ref[:, 128:] = collect([before_ref[i : i + 1, :] for i in range(5, 9)], devices, share)
        leaving = []
        if parts_out > 1:
            z, chips = lax.axis_index("head"), outs[0].shape[0]
            for chip in range(chips):
                for core, out in enumerate((outs[0].at[chip], outs[1 + chip])):
                    n = len(leaving)
                    rows = [
                        sums_ref[pl.ds(own_device(core, chip, steps) + lax.rem(z + steps - a, steps), 1), :]
                        for a in range(steps)
                    ]
                    block = jnp.concatenate(rows + [jnp.zeros((16 - steps, 256), F32)], axis=0)
                    vector_blocks[n] = vector_rows(block, made.shape[2])
                    leaving.append(
                        pltpu.make_async_copy(
                            vector_blocks.at[n], out.at[pl.ds(out.shape[0] - 16, 16), :], sems.at[2 + n]
                        )
                    )
        for copy in leaving:
            copy.start()
        for last in (steps - 2, steps - 1):
            for copy in leave_copies(last, made.at[last % 2], outs, out_sems.at[last % 2]):
                copy.wait()
        for copy in leaving:
            copy.wait()


def backward(normed, rows, before, tokens, residual_grad, devices, waits, members, grad_shapes):
    length, width = normed.shape
    slots = members[0].shape[0]
    shape = jax.ShapeDtypeStruct
    outs = [shape((length, width), BF16), shape((devices, 256), F32)]
    grads = [shape(s, BF16) for s in grad_shapes]
    large = [tokens, residual_grad]
    return pl.pallas_call(
        functools.partial(back_kernel, len(waits), len(grad_shapes), slots),
        grid=(slots,),
        out_shape=outs + grads + [MARK],
        in_specs=[fixed(o.shape) for o in (normed, rows, before)] + anywhere(large + waits) + by_step(members),
        out_specs=[fixed(o.shape) for o in outs] + anywhere(grads) + [mark_spec()],
        scratch_shapes=[
            pltpu.VMEM((length, 4 * PAIR), BF16),
            pltpu.VMEM((2, width, 5 * PAIR), BF16),
            pltpu.VMEM((length, width), F32),
        ]
        + [pltpu.VMEM((length, width), m.dtype) for m in large]
        + [
            pltpu.VMEM((8, 16, 5 * PAIR), BF16),
            pltpu.SemaphoreType.DMA((10,)),
            pltpu.SemaphoreType.DMA((2, 8)),
        ],
        compiler_params=params(),
        cost_estimate=cost(27),
        name="attend_back",
    )(normed, rows, before, *large, *waits, *members)


def after(value, *others):
    return pl.pallas_call(
        lambda *refs: None,
        out_shape=jax.ShapeDtypeStruct(value.shape, value.dtype),
        in_specs=anywhere((value,) + others),
        out_specs=anywhere([value])[0],
        input_output_aliases={0: 0},
        name="after",
    )(value, *others)


def vector_values(block):
    return block[:, :256].astype(F32) + block[:, 256:512].astype(F32)


def vector_rows(values, width):
    high = low(values)
    rest = jnp.zeros((values.shape[0], width - 512), BF16)
    return jnp.concatenate([high, low(values - high.astype(F32)), rest], axis=1)


def join_kernel(chips, slots, ffn_ref, keep_ref, *refs):
    others, ffn_outs, outs = refs[:chips], refs[chips : chips + slots], refs[chips + slots :]
    z = lax.axis_index("head")
    for a, out in enumerate(ffn_outs):
        place = lax.rem(z + a, slots)
        out[...] = low(add(*[ffn_ref[c, pl.ds(place, 1)][0] for c in range(chips)]))
    body = keep_ref.shape[1] - 16
    for chip, out in enumerate(outs):
        out[:body, :] = low(add(keep_ref[chip, :body, :], others[chip][:body, :]))
        values = vector_values(keep_ref[chip, body:, :]) + vector_values(others[chip][body:, :])
        out[body:, :] = vector_rows(values, out.shape[1])


def join(ffn, keep, others):
    shape = jax.ShapeDtypeStruct
    chips, slots = ffn.shape[:2]
    operands = [ffn, keep, *others]
    outs = [shape(ffn.shape[2:], BF16)] * slots + [shape(keep.shape[1:], BF16)] * chips
    made = pl.pallas_call(
        functools.partial(join_kernel, chips, slots),
        grid=(1,),
        out_shape=outs,
        in_specs=[fixed(o.shape) for o in operands],
        out_specs=[fixed(o.shape) for o in outs],
        compiler_params=params(44),
        cost_estimate=cost(3),
        name="join",
    )(*operands)
    return made[:slots], made[slots:]


def sum_plane_kernel(slots, pairs, mine_ref, vector_ref, sends, mark):
    rows = mine_ref.shape[0]
    values = functools.reduce(lambda x, y: x + y, [vector_values(p[slots * rows :, :]) for p in pairs])
    vector_ref[...] = values[:8, :]
    for a in range(slots):
        mine = add(*[p[a * rows : (a + 1) * rows, :] for p in pairs])
        if a == 0:
            mine_ref[...] = mine
        else:
            sends[a - 1][:rows, :] = low(mine)
            sends[a - 1][rows:, :] = vector_rows(jnp.broadcast_to(values[a : a + 1, :], (16, 256)), mine.shape[1])
    mark[0] = 1.0


def sum_plane(pairs, slots, waits):
    shape = jax.ShapeDtypeStruct
    rows, columns = (pairs[0].shape[0] - 16) // slots, pairs[0].shape[1]
    outs = [shape((rows, columns), F32), shape((8, 256), F32)]
    outs += [shape((rows + 16, columns), BF16)] * (slots - 1)

    def kernel(*refs):
        made = refs[len(pairs) + len(waits) :]
        sum_plane_kernel(slots, refs[: len(pairs)], made[0], made[1], made[2:-1], made[-1])

    return pl.pallas_call(
        kernel,
        grid=(1,),
        out_shape=outs + [MARK],
        in_specs=[fixed(p.shape) for p in pairs] + anywhere(waits),
        out_specs=[fixed(o.shape) for o in outs] + [mark_spec()],
        compiler_params=params(12),
        cost_estimate=cost(2),
        name="sum_plane",
    )(*pairs, *waits)


def settle_kernel(ffn, expand_ref, shrink_ref):
    blocks, _, share, width = ffn[0].shape
    total = add(*[f[...] for f in ffn])
    expand_ref[...] = total[:, 0].reshape(blocks * share, width).T
    for i in range(blocks):
        shrink_ref[:, i] = total[i, 1].T.reshape(width // share, share, share)


def settle(ffn, wait):
    shape = jax.ShapeDtypeStruct
    slots = len(ffn)
    blocks, _, share, width = ffn[0].shape
    outs = [shape((width, blocks * share), F32), shape((width // share, blocks, share, share), F32)]

    def kernel(*refs):
        settle_kernel(refs[:slots], *refs[slots + 1 :])

    return pl.pallas_call(
        kernel,
        grid=(1,),
        out_shape=outs,
        in_specs=[fixed(f.shape) for f in ffn] + anywhere([wait]),
        out_specs=[fixed(o.shape) for o in outs],
        compiler_params=params(12),
        cost_estimate=cost(3),
        name="settle",
    )(*ffn, wait)


def flip(count, bit):
    return [(i, i ^ bit) for i in range(count)]


def turn(count, by):
    return [(i, (i + by) % count) for i in range(count)]


def add(*members):
    return functools.reduce(lambda a, b: a + b, [m.astype(F32) for m in members])


def to_mate(shares, seqs):
    return lax.ppermute(shares, "seq", flip(seqs, 1))


def over_chips(shares, chips, seqs):
    return [shares] + [lax.ppermute(shares, "seq", flip(seqs, 2 * r)) for r in range(1, chips)]


def over_cores(held, seqs):
    return [member for h in held for member in (h, to_mate(h, seqs))]


def to_chips(shares, seqs):
    plane = [list(range(core, seqs, 2)) for core in range(2)]
    return lax.all_to_all(shares, "seq", 0, 0, axis_index_groups=plane, tiled=True)


def from_chips(sends, seqs):
    return [lax.ppermute(m, "seq", flip(seqs, 2 * r + 2)) for r, m in enumerate(sends)]


def body(
    inputs,
    attn_gain,
    attn_shift,
    query_weight,
    key_weight,
    value_weight,
    control_weight,
    output_weight,
    ffn_gain,
    ffn_shift,
    expand_weight,
    expand_bias,
    shrink_weight,
    shrink_bias,
    cotangent,
):
    seqs, slots = lax.axis_size("seq"), lax.axis_size("head")
    devices = seqs * slots
    chips = seqs // 2
    width = inputs.shape[1]
    share = width // devices
    hidden_share = expand_weight.shape[1]
    z = lax.axis_index("head")
    direct = seqs == 8 and slots == 4 and share == 16 and hidden_share == 4 * share

    own = jnp.concatenate(
        [
            jnp.concatenate([query_weight, key_weight, value_weight, control_weight], axis=1),
            output_weight,
        ],
        axis=0,
    )
    places = [(attn_gain, 0), (attn_shift, 1), (ffn_gain, 2), (ffn_shift, 3), (shrink_bias, 4)]
    row = functools.reduce(
        lambda a, b: a + b,
        [jnp.pad(m, (i * share, width - (i + 1) * share)) for m, i in places]
        + [jnp.pad(expand_bias, (128, width - 128 - hidden_share))],
    )
    block = jnp.pad(row[None, :], ((0, 15), (0, 0)))
    expand_t = expand_weight.T.reshape(4, share, width)
    shrink_t = shrink_weight.reshape(devices, 4, share, share).transpose(1, 3, 0, 2).reshape(4, share, width)
    load = jnp.stack([expand_t, shrink_t], axis=1)
    if direct:
        rows = own.shape[0] // seqs
        piece = lax.dynamic_slice_in_dim(own, lax.axis_index("seq") * rows, rows, axis=0)
        piece = jnp.concatenate([piece, block], axis=0)
        came = [lax.ppermute(piece, "head", turn(slots, a)) for a in range(1, slots)]
        for a in range(1, slots):
            block = block + jnp.pad(came[a - 1][rows : rows + 1], ((a, 15 - a), (0, 0)))
        near = jnp.concatenate([c[:rows] for c in came] + [block], axis=0)
        pieces, vectors = over_cores(over_chips(near, chips, seqs), seqs), []
        load = jnp.broadcast_to(load.reshape(1, 8, share, width), (slots, 8, share, width))
        load = lax.all_to_all(after(load, near), "head", 0, 0, tiled=True)
        held = over_chips(load, chips, seqs)
        tall = (slots * width // seqs + 16, 5 * PAIR)
        pair_shapes = [(chips,) + tall] + [tall] * chips
        ffn_shapes = [(chips, slots, 4, 2, 16, width)] * 2
    else:
        every = lax.all_gather(own, "head", axis=0, tiled=False)
        pieces = [jnp.concatenate([every[(z + slots - a) % slots] for a in range(1, slots)], axis=0)]
        block = jnp.concatenate([block[:1, :128], block[:1, 128:256], block[2:, :128]], axis=0)
        vectors = [lax.all_gather(block, ("seq", "head"), axis=0, tiled=False)]
        both = lax.all_gather(load, ("seq", "head"), axis=2, tiled=True)
        ffn_pieces = [both.reshape(4, 2, width // 16, 16, width).transpose(0, 2, 1, 3, 4)]
        pair_shapes = [(slots, width, 5 * PAIR)]
        ffn_shapes = [ffn_pieces[0].shape]

    (normed, rows, residual, second, mark), (heads, weights, *members) = forward(
        inputs, own, pieces, vectors, devices, slots
    )
    if direct:
        ffn_pieces = over_cores(held[:-1] + [low(held[-1].astype(F32) * mark[0])], seqs)
    result, branch, sums, *ffn_grads = feed_forward(
        second, rows, cotangent, residual, ffn_pieces, ffn_shapes
    )
    heads_grad, output_grad, _ = heads_back(branch, weights, heads)
    members = [weights, heads_grad, output_grad, *members]
    waits = []
    if direct:
        ffn_mine = low(add(ffn_grads[0], to_mate(ffn_grads[1], seqs)))
        waits = [ffn_mine]
    input_grad, sums, *pair_grads, _ = backward(
        normed, rows, sums, inputs, branch, devices, waits, members, pair_shapes
    )

    if direct:
        keep, *sends = pair_grads
        ffn, pairs = join(to_chips(ffn_mine, seqs), keep, [to_mate(m, seqs) for m in sends])
        ffn = [ffn[0]] + [lax.ppermute(ffn[a], "head", turn(slots, a)) for a in range(1, slots)]
        pairs = [pairs[0]] + from_chips(pairs[1:], seqs)
        mine, sums, *sends, wait = sum_plane(pairs, slots, ffn[1:])
        expand_grad, shrink_grad = settle(ffn, wait)
        came = [lax.ppermute(m, "head", turn(slots, slots - 1 - a)) for a, m in enumerate(sends)]
        rows = mine.shape[0]
        pair_sum = add(mine, *[c[:rows] for c in came])
        sums = sums[0] + functools.reduce(
            lambda a, b: a + b, [c[rows, :256].astype(F32) + c[rows, 256:512].astype(F32) for c in came]
        )
    else:
        ffn_sum = lax.psum_scatter(
            ffn_grads[0].astype(F32).transpose(0, 2, 1, 3, 4).reshape(4, 2, width, width), ("seq", "head"), scatter_dimension=2, tiled=True
        )
        every = pair_grads[0].astype(F32)
        every = jnp.stack([every[(z + slots - p) % slots] for p in range(slots)])
        pair_sum = lax.psum_scatter(every, "head", scatter_dimension=0, tiled=False)
        pair_sum = lax.psum_scatter(pair_sum, "seq", scatter_dimension=0, tiled=True)

        sums = jnp.sum(
            lax.all_to_all(sums.reshape(devices, 1, 256), ("seq", "head"), 0, 0, tiled=True), axis=(0, 1)
        )
        expand_grad = ffn_sum[:, 0].reshape(hidden_share, width).T
        shrink_grad = ffn_sum[:, 1].reshape(4, share, devices, share).transpose(2, 0, 3, 1)

    vector = [sums[i * share : (i + 1) * share] for i in range(5)]
    return (
        result,
        input_grad,
        vector[0],
        vector[1],
        pair_sum[:, :PAIR],
        pair_sum[:, PAIR : 2 * PAIR],
        pair_sum[:, 2 * PAIR : 3 * PAIR],
        pair_sum[:, 3 * PAIR : 4 * PAIR],
        pair_sum[:, 4 * PAIR :].T,
        vector[2],
        vector[3],
        expand_grad,
        sums[128 : 128 + hidden_share],
        shrink_grad.reshape(devices * hidden_share, share),
        vector[4],
    )


def solution(mesh):
    placed = (
        P(("seq", "head"), None),
        P(("seq", "head")),
        P(("seq", "head")),
        P(None, "head"),
        P(None, "head"),
        P(None, "head"),
        P(None, "head"),
        P("head", None),
        P(("seq", "head")),
        P(("seq", "head")),
        P(None, ("seq", "head")),
        P(("seq", "head")),
        P(None, ("seq", "head")),
        P(("seq", "head")),
        P(("seq", "head"), None),
    )
    return jax.shard_map(
        body,
        mesh=mesh,
        in_specs=placed,
        out_specs=(
            P(("seq", "head"), None),
            P(("seq", "head"), None),
            P(("seq", "head")),
            P(("seq", "head")),
            P("seq", "head"),
            P("seq", "head"),
            P("seq", "head"),
            P("seq", "head"),
            P("head", "seq"),
            P(("seq", "head")),
            P(("seq", "head")),
            P(None, ("seq", "head")),
            P(("seq", "head")),
            P(None, ("seq", "head")),
            P(("seq", "head")),
        ),
        check_vma=False,
    )
```

```python
import functools

import jax
import jax.numpy as jnp
from jax import lax
from jax.experimental import pallas as pl
from jax.experimental.pallas import tpu as pltpu
from jax.sharding import PartitionSpec as P

EPSILON = 1e-5
CHUNK = 128
PAIR = 128
F32 = jnp.float32
BF16 = jnp.bfloat16


def nn(a, b):
    return lax.dot_general(a, b, (((1,), (0,)), ((), ())), preferred_element_type=F32)


def nt(a, b):
    return lax.dot_general(a, b, (((1,), (1,)), ((), ())), preferred_element_type=F32)


def tn(a, b):
    return lax.dot_general(a, b, (((0,), (0,)), ((), ())), preferred_element_type=F32)


def low(v):
    return v.astype(BF16)


def iota(shape, axis):
    return lax.broadcasted_iota(jnp.int32, shape, axis)


def first_half(shape):
    return iota(shape, 1) < PAIR // 2


def stacked(block):
    left = first_half(block.shape)
    zero = jnp.zeros_like(block)
    return jnp.concatenate([jnp.where(left, block, zero), jnp.where(left, zero, block)], axis=0)


def parts(v):
    high = low(v)
    return jnp.concatenate([high, low(v - high.astype(F32))], axis=1)


def whole(v):
    return v[:, :PAIR] + v[:, PAIR:]


def head_block(shape=(PAIR, PAIR)):
    return (iota(shape, 0) < PAIR // 2) == (iota(shape, 1) < PAIR // 2)


def causal_pair():
    return iota((CHUNK, 2 * CHUNK), 0) >= (iota((CHUNK, 2 * CHUNK), 1) & (CHUNK - 1))


def causal_pair_t():
    return iota((CHUNK, 2 * CHUNK), 0) <= (iota((CHUNK, 2 * CHUNK), 1) & (CHUNK - 1))


def ones_where(mask):
    return low(jnp.where(mask, 1.0, 0.0))


def norm_parts(tokens):
    average = jnp.mean(tokens, axis=-1, keepdims=True)
    centred = tokens - average
    rate = lax.rsqrt(jnp.mean(centred * centred, axis=-1, keepdims=True) + EPSILON)
    return centred * rate, rate


def norm_back(grad, normal, rate, gain):
    w = grad * gain
    return rate * (
        w
        - jnp.mean(w, axis=-1, keepdims=True)
        - normal * jnp.mean(w * normal, axis=-1, keepdims=True)
    )


def chunks(length):
    return [slice(c * CHUNK, (c + 1) * CHUNK) for c in range(length // CHUNK)]


def attend_forward(normed, weight, keep):
    q_ref, k_ref, v_ref, powers_ref, inverse_ref, score_ref, prob_ref, key_state, value_state, heads_ref = keep
    cuts = chunks(normed.shape[0])
    tri = ones_where(iota((CHUNK, CHUNK), 0) >= iota((CHUNK, CHUNK), 1))
    same = head_block()
    both = jnp.concatenate([ones_where(same)] * 2, axis=0)
    causal = causal_pair()
    left = first_half((CHUNK, PAIR))
    carried = jnp.zeros((1, PAIR), F32)
    key_sum = jnp.zeros((PAIR, PAIR), F32)
    value_sum = jnp.zeros((PAIR, PAIR), F32)

    def masked(product):
        return low(jnp.where(causal, product, 0.0))

    def lift(score):
        top_a = jnp.max(jnp.where(left, score, -jnp.inf), axis=-1, keepdims=True)
        top_b = jnp.max(jnp.where(left, -jnp.inf, score), axis=-1, keepdims=True)
        return jnp.exp(score - jnp.where(left, top_a, top_b))

    for first in range(0, len(cuts), 8):
        group = list(range(first, min(first + 8, len(cuts))))
        each = range(len(group))
        rows = slice(group[0] * CHUNK, (group[-1] + 1) * CHUNK)
        made = nn(normed[rows, :], weight)
        cut = [made[i * CHUNK : (i + 1) * CHUNK, :] for i in each]
        q = [low(low(m[:, :PAIR]).astype(F32) * 0.125) for m in cut]
        k = [low(m[:, PAIR : 2 * PAIR]) for m in cut]
        v = [low(m[:, 2 * PAIR : 3 * PAIR]) for m in cut]
        powers = [jnp.exp(m[:, 3 * PAIR :]) for m in cut]
        powers_low = [low(p) for p in powers]
        local = [whole(nn(tri, parts(p))) for p in powers]
        scored = [masked(nt(q[i], stacked(k[i]))) for i in each]
        inverse = []
        for i in each:
            running = local[i] + carried
            carried = running[CHUNK - 1 :, :]
            inverse.append(1.0 / running)
        powers_two = [stacked(m) for m in powers_low]
        for i, c in enumerate(group):
            key_state[c, :, :] = low(jnp.where(same, key_sum, 0.0))
            value_state[c, :, :] = low(jnp.where(same, value_sum, 0.0))
            if c + 1 < len(cuts):
                key_sum = key_sum + tn(k[i], powers_low[i])
                value_sum = value_sum + tn(powers_low[i], v[i])
        score = [
            (nn(scored[i], powers_two[i]) + nn(q[i], key_state[c, :, :])) * inverse[i]
            for i, c in enumerate(group)
        ]
        lifted = [lift(m) for m in score]
        prob = [lifted[i] / nn(parts(lifted[i]), both) for i in each]
        reading = [low(prob[i] * inverse[i]) for i in each]
        mixing = [masked(nt(reading[i], powers_two[i])) for i in each]
        for i, c in enumerate(group):
            q_ref[cuts[c], :] = q[i]
            k_ref[cuts[c], :] = k[i]
            v_ref[cuts[c], :] = v[i]
            powers_ref[cuts[c], :] = powers[i]
            inverse_ref[cuts[c], :] = inverse[i]
            score_ref[cuts[c], :] = score[i]
            prob_ref[cuts[c], :] = prob[i]
        for i, c in enumerate(group):
            heads_ref[cuts[c], :] = low(
                nn(mixing[i], stacked(v[i])) + nn(reading[i], value_state[c, :, :])
            )


def attend_backward(heads_grad, kept, backs):
    q_ref, k_ref, v_ref, powers_ref, inverse_ref, score_ref, prob_ref, key_state, value_state = kept
    cuts = chunks(heads_grad.shape[0])
    same = head_block()
    both = jnp.concatenate([ones_where(same)] * 2, axis=0)
    causal = causal_pair()
    causal_t = causal_pair_t()
    tri_t = ones_where(iota((CHUNK, CHUNK), 0) <= iota((CHUNK, CHUNK), 1))
    after_sum = jnp.zeros((1, PAIR), F32)
    read_sum = jnp.zeros((PAIR, PAIR), F32)
    score_sum = jnp.zeros((PAIR, PAIR), F32)

    def masked(product, mask):
        return low(jnp.where(mask, product, 0.0))

    for first in reversed(range(0, len(cuts), 4)):
        group = list(reversed(range(first, min(first + 4, len(cuts)))))
        load = lambda ref: [ref[cuts[c], :] for c in group]
        q, k, v, grad = load(q_ref), load(k_ref), load(v_ref), load(heads_grad)
        inverse, prob, powers = load(inverse_ref), load(prob_ref), load(powers_ref)
        each = range(len(group))
        powers_low = [low(p) for p in powers]
        reading = [low(prob[i] * inverse[i]) for i in each]
        powers_two, values_two = [stacked(m) for m in powers_low], [stacked(m) for m in v]
        grad_two, reading_two = [stacked(m) for m in grad], [stacked(m) for m in reading]
        mixing_grad = [masked(nt(grad[i], values_two[i]), causal) for i in each]
        reading_grad = [
            nn(mixing_grad[i], powers_two[i]) + nt(grad[i], value_state[group[i], :, :]) for i in each
        ]
        mixing_grad_t = [masked(nt(v[i], grad_two[i]), causal_t) for i in each]
        mixing_t = [masked(nt(powers_low[i], reading_two[i]), causal_t) for i in each]
        read_states = []
        for i in each:
            read_states.append(low(jnp.where(same, read_sum, 0.0)))
            if group[i]:
                read_sum = read_sum + tn(reading[i], grad[i])
        prob_grad = [reading_grad[i] * inverse[i] for i in each]
        weighed = [prob[i] * prob_grad[i] for i in each]
        slots_grad = [weighed[i] - prob[i] * nn(parts(weighed[i]), both) for i in each]
        summed_grad = [low(slots_grad[i] * inverse[i]) for i in each]
        running_grad = [
            -inverse[i] * (weighed[i] + slots_grad[i] * score_ref[cuts[group[i]], :]) for i in each
        ]
        powers_grad = [
            nn(mixing_grad_t[i], reading_two[i]) + nt(v[i], read_states[i]) for i in each
        ]
        for i in each:
            backs[cuts[group[i]], 2 * PAIR : 3 * PAIR] = low(
                nn(mixing_t[i], grad_two[i]) + nn(powers_low[i], read_states[i])
            )
        queries_two, keys_two = [stacked(m) for m in q], [stacked(m) for m in k]
        scored_t = [masked(nt(k[i], queries_two[i]), causal_t) for i in each]
        summed_two = [stacked(m) for m in summed_grad]
        score_states = []
        for i in each:
            score_states.append(low(jnp.where(same, score_sum, 0.0)))
            if group[i]:
                score_sum = score_sum + tn(q[i], summed_grad[i])
        scored_grad = [masked(nt(summed_grad[i], powers_two[i]), causal) for i in each]
        scored_grad_t = [masked(nt(powers_low[i], summed_two[i]), causal_t) for i in each]
        later = [whole(nn(tri_t, parts(running_grad[i]))) for i in each]
        powers_grad = [
            powers_grad[i] + nn(scored_t[i], summed_two[i]) + nn(k[i], score_states[i]) for i in each
        ]
        for i in each:
            rows = cuts[group[i]]
            backs[rows, :PAIR] = low(
                0.125 * (nn(scored_grad[i], keys_two[i]) + nt(summed_grad[i], key_state[group[i], :, :]))
            )
            backs[rows, PAIR : 2 * PAIR] = low(
                nn(scored_grad_t[i], queries_two[i]) + nt(powers_low[i], score_states[i])
            )
            total = later[i] + after_sum
            after_sum = total[:1, :]
            backs[rows, 3 * PAIR :] = low((powers_grad[i] + total) * powers[i])


def kept_shapes(length, lead=()):
    n = length // CHUNK
    shape = pltpu.HBM
    return (
        [shape(lead + (length, PAIR), BF16)] * 3
        + [shape(lead + (length, PAIR), F32)] * 4
        + [shape(lead + (n, PAIR, PAIR), BF16)] * 2
    )


def fixed(shape):
    return pl.BlockSpec(shape, lambda a: (0,) * len(shape))


def one_slot(members, slot):
    return [
        pl.BlockSpec((None,) + s.shape[1:], lambda a, rank=len(s.shape): (slot,) + (0,) * (rank - 1))
        for s in members
    ]


def by_step(members, first=0):
    return [
        pl.BlockSpec((None,) + s.shape[1:], lambda a, rank=len(s.shape): (a + first,) + (0,) * (rank - 1))
        for s in members
    ]


def anywhere(members):
    return [pl.BlockSpec(memory_space=pl.ANY)] * len(members)


def mark_spec():
    return pl.BlockSpec(memory_space=pltpu.SMEM)


MARK = jax.ShapeDtypeStruct((1,), F32)


def cost(micros):
    return pl.CostEstimate(flops=int(micros * 1e9), bytes_accessed=int(micros * 1e6), transcendentals=0)


def params(megabytes=56):
    return pltpu.CompilerParams(vmem_limit_bytes=megabytes * 1024 * 1024)


def select(width, offset, share, total):
    return ones_where(
        iota((width, total), 0) == offset + (iota((width, total), 1) & (share - 1))
    )


def owned(devices, share, total):
    return iota((devices, total), 0) == lax.shift_right_logical(
        iota((devices, total), 1), share.bit_length() - 1
    )


def spread(rows, offset, share, total):
    each = nn(rows, select(rows.shape[1], offset, share, total))
    return jnp.sum(jnp.where(owned(rows.shape[0], share, total), each, 0.0), axis=0, keepdims=True)


def collect(rows, devices, share):
    total = rows[0].shape[1]
    mine = owned(devices, share, total)
    out = jnp.zeros((devices, 128), F32)
    for i, row in enumerate(rows):
        rest = jnp.where(mine, row, 0.0)
        high = low(rest)
        pair = jnp.concatenate([high, low(rest - high.astype(F32))], axis=0)
        made = nt(pair, select(128, i * share, share, total))
        out = out + made[:devices] + made[devices:]
    return out


def own_device(core, chip, slots):
    return (lax.axis_index("seq") ^ (2 * chip + core)) * slots


def fill(weight, own_ref, pieces, slot):
    @pl.when(slot == 0)
    def _():
        weight[...] = own_ref[...]

    @pl.when(slot > 0)
    def _():
        rows = weight.shape[0] // len(pieces)
        mine = lax.axis_index("seq") if len(pieces) > 1 else 0
        start = pl.multiple_of((3 - slot if len(pieces) > 1 else slot - 1) * rows, 16)
        for r, piece in enumerate(pieces):
            weight[pl.ds(pl.multiple_of((mine ^ r) * rows, rows), rows), :] = piece[pl.ds(start, rows), :]


def gather_vectors(pieces, rows, slots, vectors):
    for r, piece in enumerate(pieces):
        block = piece[(slots - 1) * rows :, :256].astype(F32)
        for a in range(slots):
            z = lax.rem(lax.axis_index("head") + slots - a, slots)
            source = own_device(r % 2, r // 2, slots) + z
            for i in range(2):
                part = block[a : a + 1, 128 * i : 128 * (i + 1)]
                vectors[pl.ds(source, 1), i : i + 1, :] = part[None]


def forward_kernel(count, slots, tokens_ref, own_ref, *refs):
    pieces, refs = refs[:count], refs[count:]
    if count == 1:
        given, refs = refs[0], refs[1:]
    normed_ref, rows_ref, residual_ref, second_ref, mark, heads_ref, weight = refs[:7]
    keep, staged, vectors = refs[7:-2], refs[-2], refs[-1]
    slot = pl.program_id(0)
    length, width = tokens_ref.shape
    share = width // vectors.shape[0]
    tiles = [slice(r, r + 256) for r in range(0, length, 256)]

    @pl.when(slot == 0)
    def _():
        if count == 1:
            vectors[...] = given[:, :8, :].astype(F32)
        else:
            gather_vectors(pieces, weight.shape[0] // count, slots, vectors)
        for i in range(9):
            part = low(vectors[:, 0 if i < 5 else 1, :])
            rows_ref[i : i + 1, :] = spread(part, (i if i < 5 else i - 5) * share, share, width)
        gain, shift = rows_ref[0:1, :], rows_ref[1:2, :]
        for rows in tiles:
            tokens = tokens_ref[rows, :].astype(F32)
            normal, _ = norm_parts(tokens)
            normed_ref[rows, :] = low(normal * gain + shift)
            residual_ref[rows, :] = tokens
        mark[0] = 1.0

    fill(weight, own_ref, pieces, slot)
    attend_forward(normed_ref, weight[:width, :], list(keep) + [staged])
    heads_ref[...] = staged[...]
    residual_ref[...] += nn(staged[...], weight[width:, :])

    @pl.when(slot == slots - 1)
    def _():
        gain, shift = rows_ref[2:3, :], rows_ref[3:4, :]
        for rows in tiles:
            normal, _ = norm_parts(residual_ref[rows, :])
            second_ref[rows, :] = low(normal * gain + shift)


def forward(tokens, own, pieces, vectors, devices, slots):
    length, width = tokens.shape
    shape = jax.ShapeDtypeStruct
    operands = [tokens, own, *pieces, *vectors]
    outs = [
        shape((length, width), BF16),
        shape((16, width), F32),
        shape((length, width), F32),
        shape((length, width), BF16),
    ]
    stacked_outs = [shape((slots, length, PAIR), BF16), pltpu.HBM((slots, width + PAIR, 4 * PAIR), BF16)]
    stacked_outs += kept_shapes(length, (slots,))
    made = pl.pallas_call(
        functools.partial(forward_kernel, len(pieces), slots),
        grid=(slots,),
        out_shape=outs + [MARK] + stacked_outs,
        in_specs=[fixed(o.shape) for o in operands],
        out_specs=[fixed(o.shape) for o in outs] + [mark_spec()] + by_step(stacked_outs),
        scratch_shapes=[pltpu.VMEM((length, PAIR), BF16), pltpu.VMEM((devices, 8, 128), F32)],
        compiler_params=params(44),
        cost_estimate=cost(17),
        name="attend_forward",
    )(*operands)
    return made[:5], made[5:]


GELU_A = 0.7978845608028654
GELU_B = 0.044715


def gelu_both(u):
    square = u * u
    half = 0.5 + 0.5 * jnp.tanh(u * (GELU_A + GELU_A * GELU_B * square))
    value = u * half
    return value, half + value * (1.0 - half) * (2.0 * GELU_A + 6.0 * GELU_A * GELU_B * square)


def weight_copies(block, pieces, weights, sems):
    if len(pieces) == 1:
        return [pltpu.make_async_copy(pieces[0].at[block], weights.at[block], sems.at[block, 0])]
    copies = []
    for r, piece in enumerate(pieces):
        slots = piece.shape[0]
        copies.append(
            pltpu.make_async_copy(
                piece.at[:, pl.ds(2 * block, 2)],
                weights.at[block, pl.ds(own_device(r % 2, r // 2, slots), slots)],
                sems.at[block, len(copies)],
            )
        )
    return copies


def grad_copies(block, grads, outs, sems):
    if len(outs) == 1:
        return [pltpu.make_async_copy(grads.at[block], outs[0].at[block], sems.at[block, 0])]
    copies = []
    for core, out in enumerate(outs):
        chips, slots = out.shape[:2]
        for chip in range(chips):
            target = (2 * chip + ((lax.axis_index("seq") & 1) ^ core)) * slots
            copies.append(
                pltpu.make_async_copy(
                    grads.at[block, pl.ds(target, slots)],
                    out.at[chip, :, block],
                    sems.at[block, len(copies)],
                )
            )
    return copies


def ffn_kernel(count, second_ref, rows_ref, cotangent_hbm, residual_hbm, *refs):
    pieces = refs[:count]
    result_hbm, branch_hbm, sums_ref = refs[count : count + 3]
    outs = refs[count + 3 : -13]
    (weights, grads, residual, cotangent_ref, total, back, result, branch, in_sems, out_sems, residual_sem, tile_sems, cotangent_sems) = refs[-13:]
    k = pl.program_id(0)
    length, width = second_ref.shape
    tiles = [slice(r, r + 256) for r in range(0, length, 256)]
    fetch = pltpu.make_async_copy(residual_hbm, residual, residual_sem)

    def arrive(rows):
        return pltpu.make_async_copy(
            cotangent_hbm.at[rows, :], cotangent_ref.at[rows, :], cotangent_sems.at[rows.start // 256]
        )

    def leave(rows):
        tile = rows.start // 256
        return [
            pltpu.make_async_copy(source.at[rows, :], target.at[rows, :], tile_sems.at[i, tile])
            for i, (source, target) in enumerate([(result, result_hbm), (branch, branch_hbm)])
        ]

    @pl.when(k == 0)
    def _():
        for copy in weight_copies(0, pieces, weights, in_sems):
            copy.start()
        for rows in tiles:
            arrive(rows).start()
        for block in range(1, 4):
            for copy in weight_copies(block, pieces, weights, in_sems):
                copy.start()
        fetch.start()
        total[...] = jnp.zeros_like(total)
        back[...] = jnp.zeros_like(back)

    for block in range(4):

        @pl.when(k == block)
        def _(block=block):
            for copy in weight_copies(block, pieces, weights, in_sems):
                copy.wait()
            if block == 0:
                for rows in tiles:
                    arrive(rows).wait()

    expand = weights[k, :, 0].reshape(width, width)
    shrink = weights[k, :, 1].reshape(width, width)
    bias = rows_ref[pl.ds(5 + k, 1), :]
    bias_grad = jnp.zeros((1, width), F32)
    acts, hids = [], []
    for rows in tiles:
        hidden = nt(second_ref[rows, :], expand) + bias
        pull = nn(cotangent_ref[rows, :], shrink)
        value, slope = gelu_both(hidden)
        activated = low(value)
        hidden_grad = low(pull * slope)
        bias_grad = bias_grad + jnp.sum(hidden_grad.astype(F32), axis=0, keepdims=True)
        total[rows, :] += nt(activated, shrink)
        back[rows, :] += nn(hidden_grad, expand)
        acts.append(activated)
        hids.append(hidden_grad)
    sums_ref[pl.ds(5 + k, 1), :] = bias_grad
    grads[k, :, 1] = low(tn(cotangent_ref[...], jnp.concatenate(acts, axis=0))).reshape(
        width // 16, 16, width
    )
    grads[k, :, 0] = low(tn(jnp.concatenate(hids, axis=0), second_ref[...])).reshape(width // 16, 16, width)
    for block in range(4):

        @pl.when(k == block)
        def _(block=block):
            for copy in grad_copies(block, grads, outs, out_sems):
                copy.start()

    @pl.when(k == 3)
    def _():
        fetch.wait()
        gain, bias = rows_ref[2:3, :], rows_ref[4:5, :]
        gain_grad = jnp.zeros((1, width), F32)
        shift_grad = jnp.zeros((1, width), F32)
        outer = jnp.zeros((1, width), F32)
        for rows in tiles:
            base = residual[rows, :]
            result[rows, :] = low(base + total[rows, :] + bias)
            grad = back[rows, :]
            normal, rate = norm_parts(base)
            upstream = cotangent_ref[rows, :].astype(F32)
            gain_grad = gain_grad + jnp.sum(grad * normal, axis=0, keepdims=True)
            shift_grad = shift_grad + jnp.sum(grad, axis=0, keepdims=True)
            outer = outer + jnp.sum(upstream, axis=0, keepdims=True)
            branch[rows, :] = low(upstream + norm_back(grad, normal, rate, gain))
            for copy in leave(rows):
                copy.start()
        sums_ref[0:2, :] = jnp.zeros((2, width), F32)
        sums_ref[2:3, :] = gain_grad
        sums_ref[3:4, :] = shift_grad
        sums_ref[4:5, :] = outer
        for rows in tiles:
            for copy in leave(rows):
                copy.wait()
        for block in range(4):
            for copy in grad_copies(block, grads, outs, out_sems):
                copy.wait()


def feed_forward(second, rows, cotangent, residual, pieces, grad_shapes):
    length, width = second.shape
    shape = jax.ShapeDtypeStruct
    weights = (4, width // 16, 2, 16, width)
    outs = [
        shape((length, width), BF16),
        shape((length, width), BF16),
        shape((16, width), F32),
    ]
    return pl.pallas_call(
        functools.partial(ffn_kernel, len(pieces)),
        grid=(4,),
        out_shape=outs + [shape(s, BF16) for s in grad_shapes],
        in_specs=[fixed(o.shape) for o in (second, rows)]
        + [pl.BlockSpec(memory_space=pltpu.HBM)] * (2 + len(pieces)),
        out_specs=anywhere(outs[:2]) + [fixed(outs[2].shape)] + anywhere(grad_shapes),
        scratch_shapes=[
            pltpu.VMEM(weights, BF16),
            pltpu.VMEM(weights, BF16),
            pltpu.VMEM((length, width), F32),
            pltpu.VMEM((length, width), BF16),
            pltpu.VMEM((length, width), F32),
            pltpu.VMEM((length, width), F32),
            pltpu.VMEM((length, width), BF16),
            pltpu.VMEM((length, width), BF16),
            pltpu.SemaphoreType.DMA((4, 8)),
            pltpu.SemaphoreType.DMA((4, 8)),
            pltpu.SemaphoreType.DMA,
            pltpu.SemaphoreType.DMA((2, length // 256)),
            pltpu.SemaphoreType.DMA((length // 256,)),
        ],
        compiler_params=params(44),
        cost_estimate=cost(22),
        name="feed_forward",
    )(second, rows, cotangent, residual, *pieces)


def heads_kernel(branch_ref, weight_ref, heads_ref, grad_ref, output_grad_ref, mark):
    slots = heads_ref.shape[0]
    weight = weight_ref[...].reshape(slots * PAIR, weight_ref.shape[2])
    grad = low(nt(branch_ref[...], weight))
    output_grad = low(tn(branch_ref[...], jnp.concatenate([heads_ref[a] for a in range(slots)], axis=1)))
    for a in range(slots):
        grad_ref[a] = grad[:, a * PAIR : (a + 1) * PAIR]
        output_grad_ref[a] = output_grad[:, a * PAIR : (a + 1) * PAIR]
    mark[0] = 1.0


def heads_back(branch, weights, heads):
    slots = heads.shape[0]
    length, width = branch.shape
    shape = jax.ShapeDtypeStruct
    outs = [shape((slots, length, PAIR), BF16), shape((slots, width, PAIR), BF16)]
    return pl.pallas_call(
        heads_kernel,
        grid=(1,),
        out_shape=outs + [MARK],
        in_specs=[
            fixed((length, width)),
            pl.BlockSpec((slots, PAIR, width), lambda a: (0, width // PAIR, 0)),
        ]
        + [fixed(heads.shape)],
        out_specs=[fixed(o.shape) for o in outs] + [mark_spec()],
        compiler_params=params(16),
        cost_estimate=cost(4),
        name="heads_back",
    )(branch, weights, heads)


def pair_grads(grad_ref, output_grad_ref, normed_ref, kept, backs, made):
    attend_backward(grad_ref, kept, backs)
    made[:, : 4 * PAIR] = low(tn(normed_ref[...], backs[...]))
    made[:, 4 * PAIR :] = output_grad_ref[...]


def leave_copies(slot, made, outs, sems):
    if len(outs) == 1:
        return [pltpu.make_async_copy(made, outs[0].at[slot], sems.at[0])]
    seq = lax.axis_index("seq")
    chips = outs[0].shape[0]
    rows = made.shape[0] // (2 * chips)
    copies = []
    for chip in range(chips):
        for core, out in enumerate((outs[0].at[chip], outs[1 + chip])):
            start = pl.multiple_of((seq ^ (2 * chip + core)) * rows, rows)
            copies.append(
                pltpu.make_async_copy(
                    made.at[pl.ds(start, rows), :],
                    out.at[pl.ds(pl.multiple_of(slot * rows, rows), rows), :],
                    sems.at[len(copies)],
                )
            )
    return copies


def back_kernel(waits, parts_out, slots, normed_ref, rows_ref, before_ref, tokens_hbm, residual_grad_hbm, *refs):
    refs = refs[waits:]
    weight, grad_ref, output_grad_ref, kept, refs = refs[0], refs[1], refs[2], refs[3:12], refs[12:]
    input_grad_ref, sums_ref, outs, mark = refs[0], refs[1], refs[2 : 2 + parts_out], refs[2 + parts_out]
    backs, made, total, tokens, residual_grad, vector_blocks, sems, out_sems = refs[3 + parts_out :]
    length, width = normed_ref.shape
    devices = sums_ref.shape[0]
    share = width // devices
    step, steps = pl.program_id(0), slots
    copies = [
        pltpu.make_async_copy(tokens_hbm, tokens, sems.at[0]),
        pltpu.make_async_copy(residual_grad_hbm, residual_grad, sems.at[1]),
    ]

    @pl.when(step == 0)
    def _():
        for copy in copies:
            copy.start()
        total[...] = jnp.zeros_like(total)
        mark[0] = 1.0

    parity = lax.rem(step, 2)

    @pl.when(step >= 2)
    def _():
        for copy in leave_copies(step - 2, made.at[parity], outs, out_sems.at[parity]):
            copy.wait()

    pair_grads(grad_ref, output_grad_ref, normed_ref, kept, backs, made.at[parity])
    for copy in leave_copies(step, made.at[parity], outs, out_sems.at[parity]):
        copy.start()
    total[...] += nt(backs[...], weight[:width, :])

    @pl.when(step == steps - 1)
    def _():
        for copy in copies:
            copy.wait()
        gain = rows_ref[0:1, :]
        gain_grad = jnp.zeros((1, width), F32)
        shift_grad = jnp.zeros((1, width), F32)
        for rows in [slice(r, r + 256) for r in range(0, length, 256)]:
            grad = total[rows, :]
            normal, rate = norm_parts(tokens[rows, :].astype(F32))
            gain_grad = gain_grad + jnp.sum(grad * normal, axis=0, keepdims=True)
            shift_grad = shift_grad + jnp.sum(grad, axis=0, keepdims=True)
            input_grad_ref[rows, :] = low(residual_grad[rows, :].astype(F32) + norm_back(grad, normal, rate, gain))
        small = [gain_grad, shift_grad] + [before_ref[i : i + 1, :] for i in range(2, 5)]
        sums_ref[:, :128] = collect(small, devices, share)
        sums_ref[:, 128:] = collect([before_ref[i : i + 1, :] for i in range(5, 9)], devices, share)
        leaving = []
        if parts_out > 1:
            z, chips = lax.axis_index("head"), outs[0].shape[0]
            for chip in range(chips):
                for core, out in enumerate((outs[0].at[chip], outs[1 + chip])):
                    n = len(leaving)
                    rows = [
                        sums_ref[pl.ds(own_device(core, chip, steps) + lax.rem(z + steps - a, steps), 1), :]
                        for a in range(steps)
                    ]
                    block = jnp.concatenate(rows + [jnp.zeros((16 - steps, 256), F32)], axis=0)
                    vector_blocks[n] = vector_rows(block, made.shape[2])
                    leaving.append(
                        pltpu.make_async_copy(
                            vector_blocks.at[n], out.at[pl.ds(out.shape[0] - 16, 16), :], sems.at[2 + n]
                        )
                    )
        for copy in leaving:
            copy.start()
        for last in (steps - 2, steps - 1):
            for copy in leave_copies(last, made.at[last % 2], outs, out_sems.at[last % 2]):
                copy.wait()
        for copy in leaving:
            copy.wait()


def backward(normed, rows, before, tokens, residual_grad, devices, waits, members, grad_shapes):
    length, width = normed.shape
    slots = members[0].shape[0]
    shape = jax.ShapeDtypeStruct
    outs = [shape((length, width), BF16), shape((devices, 256), F32)]
    grads = [shape(s, BF16) for s in grad_shapes]
    large = [tokens, residual_grad]
    return pl.pallas_call(
        functools.partial(back_kernel, len(waits), len(grad_shapes), slots),
        grid=(slots,),
        out_shape=outs + grads + [MARK],
        in_specs=[fixed(o.shape) for o in (normed, rows, before)] + anywhere(large + waits) + by_step(members),
        out_specs=[fixed(o.shape) for o in outs] + anywhere(grads) + [mark_spec()],
        scratch_shapes=[
            pltpu.VMEM((length, 4 * PAIR), BF16),
            pltpu.VMEM((2, width, 5 * PAIR), BF16),
            pltpu.VMEM((length, width), F32),
        ]
        + [pltpu.VMEM((length, width), m.dtype) for m in large]
        + [
            pltpu.VMEM((8, 16, 5 * PAIR), BF16),
            pltpu.SemaphoreType.DMA((10,)),
            pltpu.SemaphoreType.DMA((2, 8)),
        ],
        compiler_params=params(),
        cost_estimate=cost(27),
        name="attend_back",
    )(normed, rows, before, *large, *waits, *members)


def after(value, *others):
    return pl.pallas_call(
        lambda *refs: None,
        out_shape=jax.ShapeDtypeStruct(value.shape, value.dtype),
        in_specs=anywhere((value,) + others),
        out_specs=anywhere([value])[0],
        input_output_aliases={0: 0},
        name="after",
    )(value, *others)


def near_kernel(slots, block_ref, load_ref, *refs):
    came, (near_ref, loads_ref) = refs[: slots - 1], refs[slots - 1 :]
    rows = came[0].shape[0] - 16
    for a, piece in enumerate(came):
        near_ref[a * rows : (a + 1) * rows, :] = piece[:rows, :]
    lines = [block_ref[...].astype(F32)[0:1, :]]
    lines += [piece[rows:, :].astype(F32)[0:1, :] for piece in reversed(came)]
    lines += [jnp.zeros((16 - slots, block_ref.shape[1]), F32)]
    near_ref[(slots - 1) * rows :, :] = low(jnp.concatenate(lines, axis=0))
    for z in range(slots):
        loads_ref[z] = load_ref[...]


def join_near(block, load, came):
    shape = jax.ShapeDtypeStruct
    slots = len(came) + 1
    rows = came[0].shape[0] - 16
    operands = [block, load, *came]
    outs = [
        shape(((slots - 1) * rows + 16, block.shape[1]), BF16),
        shape((slots,) + load.shape, BF16),
    ]
    return pl.pallas_call(
        functools.partial(near_kernel, slots),
        grid=(1,),
        out_shape=outs,
        in_specs=[fixed(o.shape) for o in operands],
        out_specs=[fixed(o.shape) for o in outs],
        compiler_params=params(12),
        cost_estimate=cost(1),
        name="join_near",
    )(*operands)


def vector_values(block):
    return block[:, :256].astype(F32) + block[:, 256:512].astype(F32)


def vector_rows(values, width):
    high = low(values)
    rest = jnp.zeros((values.shape[0], width - 512), BF16)
    return jnp.concatenate([high, low(values - high.astype(F32)), rest], axis=1)


def join_kernel(chips, slots, ffn_ref, keep_ref, *refs):
    others, ffn_outs, outs = refs[:chips], refs[chips : chips + slots], refs[chips + slots :]
    z = lax.axis_index("head")
    for a, out in enumerate(ffn_outs):
        place = lax.rem(z + a, slots)
        out[...] = low(add(*[ffn_ref[c, pl.ds(place, 1)][0] for c in range(chips)]))
    body = keep_ref.shape[1] - 16
    for chip, out in enumerate(outs):
        out[:body, :] = low(add(keep_ref[chip, :body, :], others[chip][:body, :]))
        values = vector_values(keep_ref[chip, body:, :]) + vector_values(others[chip][body:, :])
        out[body:, :] = vector_rows(values, out.shape[1])


def join(ffn, keep, others):
    shape = jax.ShapeDtypeStruct
    chips, slots = ffn.shape[:2]
    operands = [ffn, keep, *others]
    outs = [shape(ffn.shape[2:], BF16)] * slots + [shape(keep.shape[1:], BF16)] * chips
    made = pl.pallas_call(
        functools.partial(join_kernel, chips, slots),
        grid=(1,),
        out_shape=outs,
        in_specs=[fixed(o.shape) for o in operands],
        out_specs=[fixed(o.shape) for o in outs],
        compiler_params=params(44),
        cost_estimate=cost(3),
        name="join",
    )(*operands)
    return made[:slots], made[slots:]


def sum_plane_kernel(slots, pairs, mine_ref, vector_ref, sends, mark):
    rows = mine_ref.shape[0]
    values = functools.reduce(lambda x, y: x + y, [vector_values(p[slots * rows :, :]) for p in pairs])
    vector_ref[...] = values[:8, :]
    for a in range(slots):
        mine = add(*[p[a * rows : (a + 1) * rows, :] for p in pairs])
        if a == 0:
            mine_ref[...] = mine
        else:
            sends[a - 1][:rows, :] = low(mine)
            sends[a - 1][rows:, :] = vector_rows(jnp.broadcast_to(values[a : a + 1, :], (16, 256)), mine.shape[1])
    mark[0] = 1.0


def sum_plane(pairs, slots, waits):
    shape = jax.ShapeDtypeStruct
    rows, columns = (pairs[0].shape[0] - 16) // slots, pairs[0].shape[1]
    outs = [shape((rows, columns), F32), shape((8, 256), F32)]
    outs += [shape((rows + 16, columns), BF16)] * (slots - 1)

    def kernel(*refs):
        made = refs[len(pairs) + len(waits) :]
        sum_plane_kernel(slots, refs[: len(pairs)], made[0], made[1], made[2:-1], made[-1])

    return pl.pallas_call(
        kernel,
        grid=(1,),
        out_shape=outs + [MARK],
        in_specs=[fixed(p.shape) for p in pairs] + anywhere(waits),
        out_specs=[fixed(o.shape) for o in outs] + [mark_spec()],
        compiler_params=params(12),
        cost_estimate=cost(2),
        name="sum_plane",
    )(*pairs, *waits)


def settle_kernel(ffn, expand_ref, shrink_ref):
    blocks, _, share, width = ffn[0].shape
    total = add(*[f[...] for f in ffn])
    expand_ref[...] = total[:, 0].reshape(blocks * share, width).T
    for i in range(blocks):
        shrink_ref[:, i] = total[i, 1].T.reshape(width // share, share, share)


def settle(ffn, wait):
    shape = jax.ShapeDtypeStruct
    slots = len(ffn)
    blocks, _, share, width = ffn[0].shape
    outs = [shape((width, blocks * share), F32), shape((width // share, blocks, share, share), F32)]

    def kernel(*refs):
        settle_kernel(refs[:slots], *refs[slots + 1 :])

    return pl.pallas_call(
        kernel,
        grid=(1,),
        out_shape=outs,
        in_specs=[fixed(f.shape) for f in ffn] + anywhere([wait]),
        out_specs=[fixed(o.shape) for o in outs],
        compiler_params=params(12),
        cost_estimate=cost(3),
        name="settle",
    )(*ffn, wait)


def finish_kernel(share, hidden_share, mine_ref, sums_ref, *refs):
    came, parts, vectors = refs[:3], refs[3:8], refs[8:]
    rows = mine_ref.shape[0]
    total = add(mine_ref[...], *[c[:rows, :] for c in came])
    for i, part in enumerate(parts):
        part[...] = total[:, i * PAIR : (i + 1) * PAIR]
    values = add(sums_ref[0:1, :], *[vector_values(c[rows:, :])[0:1, :] for c in came])
    for i, vector in enumerate(vectors[:-1]):
        vector[...] = values[0, i * share : (i + 1) * share]
    vectors[-1][...] = values[0, 128 : 128 + hidden_share]


def finish(mine, sums, came, share, hidden_share):
    shape = jax.ShapeDtypeStruct
    operands = [mine, sums, *came]
    outs = [shape((mine.shape[0], PAIR), F32)] * 5 + [shape((share,), F32)] * 5 + [shape((hidden_share,), F32)]
    made = pl.pallas_call(
        functools.partial(finish_kernel, share, hidden_share),
        grid=(1,),
        out_shape=outs,
        in_specs=[fixed(o.shape) for o in operands],
        out_specs=[fixed(o.shape) for o in outs],
        compiler_params=params(12),
        cost_estimate=cost(1),
        name="finish",
    )(*operands)
    return made[:5], made[5:]


def flip(count, bit):
    return [(i, i ^ bit) for i in range(count)]


def turn(count, by):
    return [(i, (i + by) % count) for i in range(count)]


def add(*members):
    return functools.reduce(lambda a, b: a + b, [m.astype(F32) for m in members])


def to_mate(shares, seqs):
    return lax.ppermute(shares, "seq", flip(seqs, 1))


def over_chips(shares, chips, seqs):
    return [shares] + [lax.ppermute(shares, "seq", flip(seqs, 2 * r)) for r in range(1, chips)]


def over_cores(held, seqs):
    return [member for h in held for member in (h, to_mate(h, seqs))]


def to_chips(shares, seqs):
    plane = [list(range(core, seqs, 2)) for core in range(2)]
    return lax.all_to_all(shares, "seq", 0, 0, axis_index_groups=plane, tiled=True)


def from_chips(sends, seqs):
    return [lax.ppermute(m, "seq", flip(seqs, 2 * r + 2)) for r, m in enumerate(sends)]


def body(
    inputs,
    attn_gain,
    attn_shift,
    query_weight,
    key_weight,
    value_weight,
    control_weight,
    output_weight,
    ffn_gain,
    ffn_shift,
    expand_weight,
    expand_bias,
    shrink_weight,
    shrink_bias,
    cotangent,
):
    seqs, slots = lax.axis_size("seq"), lax.axis_size("head")
    devices = seqs * slots
    chips = seqs // 2
    width = inputs.shape[1]
    share = width // devices
    hidden_share = expand_weight.shape[1]
    z = lax.axis_index("head")
    direct = seqs == 8 and slots == 4 and share == 16 and hidden_share == 4 * share

    own = jnp.concatenate(
        [
            jnp.concatenate([query_weight, key_weight, value_weight, control_weight], axis=1),
            output_weight,
        ],
        axis=0,
    )
    places = [(attn_gain, 0), (attn_shift, 1), (ffn_gain, 2), (ffn_shift, 3), (shrink_bias, 4)]
    row = functools.reduce(
        lambda a, b: a + b,
        [jnp.pad(m, (i * share, width - (i + 1) * share)) for m, i in places]
        + [jnp.pad(expand_bias, (128, width - 128 - hidden_share))],
    )
    block = jnp.pad(row[None, :], ((0, 15), (0, 0)))
    expand_t = expand_weight.T.reshape(4, share, width)
    shrink_t = shrink_weight.reshape(devices, 4, share, share).transpose(1, 3, 0, 2).reshape(4, share, width)
    load = jnp.stack([expand_t, shrink_t], axis=1)
    if direct:
        rows = own.shape[0] // seqs
        piece = lax.dynamic_slice_in_dim(own, lax.axis_index("seq") * rows, rows, axis=0)
        piece = jnp.concatenate([piece, block], axis=0)
        came = [lax.ppermute(piece, "head", turn(slots, a)) for a in range(1, slots)]
        near, loads = join_near(block, load.reshape(8, share, width), came[::-1])
        pieces, vectors = over_cores(over_chips(near, chips, seqs), seqs), []
        load = lax.all_to_all(loads, "head", 0, 0, tiled=True)
        held = over_chips(load, chips, seqs)
        tall = (slots * width // seqs + 16, 5 * PAIR)
        pair_shapes = [(chips,) + tall] + [tall] * chips
        ffn_shapes = [(chips, slots, 4, 2, 16, width)] * 2
    else:
        every = lax.all_gather(own, "head", axis=0, tiled=False)
        pieces = [jnp.concatenate([every[(z + slots - a) % slots] for a in range(1, slots)], axis=0)]
        block = jnp.concatenate([block[:1, :128], block[:1, 128:256], block[2:, :128]], axis=0)
        vectors = [lax.all_gather(block, ("seq", "head"), axis=0, tiled=False)]
        both = lax.all_gather(load, ("seq", "head"), axis=2, tiled=True)
        ffn_pieces = [both.reshape(4, 2, width // 16, 16, width).transpose(0, 2, 1, 3, 4)]
        pair_shapes = [(slots, width, 5 * PAIR)]
        ffn_shapes = [ffn_pieces[0].shape]

    (normed, rows, residual, second, mark), (heads, weights, *members) = forward(
        inputs, own, pieces, vectors, devices, slots
    )
    if direct:
        ffn_pieces = over_cores(held[:-1] + [low(held[-1].astype(F32) * mark[0])], seqs)
    result, branch, sums, *ffn_grads = feed_forward(
        second, rows, cotangent, residual, ffn_pieces, ffn_shapes
    )
    heads_grad, output_grad, _ = heads_back(branch, weights, heads)
    members = [weights, heads_grad, output_grad, *members]
    waits = []
    if direct:
        ffn_mine = low(add(ffn_grads[0], to_mate(ffn_grads[1], seqs)))
        waits = [ffn_mine]
    input_grad, sums, *pair_grads, _ = backward(
        normed, rows, sums, inputs, branch, devices, waits, members, pair_shapes
    )

    if direct:
        keep, *sends = pair_grads
        ffn, pairs = join(to_chips(ffn_mine, seqs), keep, [to_mate(m, seqs) for m in sends])
        ffn = [ffn[0]] + [lax.ppermute(ffn[a], "head", turn(slots, a)) for a in range(1, slots)]
        pairs = [pairs[0]] + from_chips(pairs[1:], seqs)
        mine, sums, *sends, wait = sum_plane(pairs, slots, ffn[1:])
        expand_grad, shrink_grad = settle(ffn, wait)
        came = [lax.ppermute(m, "head", turn(slots, slots - 1 - a)) for a, m in enumerate(sends)]
        parts, vector = finish(mine, sums, came[::-1], share, hidden_share)
    else:
        ffn_sum = lax.psum_scatter(
            ffn_grads[0].astype(F32).transpose(0, 2, 1, 3, 4).reshape(4, 2, width, width), ("seq", "head"), scatter_dimension=2, tiled=True
        )
        every = pair_grads[0].astype(F32)
        every = jnp.stack([every[(z + slots - p) % slots] for p in range(slots)])
        pair_sum = lax.psum_scatter(every, "head", scatter_dimension=0, tiled=False)
        pair_sum = lax.psum_scatter(pair_sum, "seq", scatter_dimension=0, tiled=True)

        sums = jnp.sum(
            lax.all_to_all(sums.reshape(devices, 1, 256), ("seq", "head"), 0, 0, tiled=True), axis=(0, 1)
        )
        expand_grad = ffn_sum[:, 0].reshape(hidden_share, width).T
        shrink_grad = ffn_sum[:, 1].reshape(4, share, devices, share).transpose(2, 0, 3, 1)

        parts = [pair_sum[:, i * PAIR : (i + 1) * PAIR] for i in range(5)]
        vector = [sums[i * share : (i + 1) * share] for i in range(5)] + [sums[128 : 128 + hidden_share]]

    return (
        result,
        input_grad,
        vector[0],
        vector[1],
        *parts[:4],
        parts[4].T,
        vector[2],
        vector[3],
        expand_grad,
        vector[5],
        shrink_grad.reshape(devices * hidden_share, share),
        vector[4],
    )


def solution(mesh):
    placed = (
        P(("seq", "head"), None),
        P(("seq", "head")),
        P(("seq", "head")),
        P(None, "head"),
        P(None, "head"),
        P(None, "head"),
        P(None, "head"),
        P("head", None),
        P(("seq", "head")),
        P(("seq", "head")),
        P(None, ("seq", "head")),
        P(("seq", "head")),
        P(None, ("seq", "head")),
        P(("seq", "head")),
        P(("seq", "head"), None),
    )
    return jax.shard_map(
        body,
        mesh=mesh,
        in_specs=placed,
        out_specs=(
            P(("seq", "head"), None),
            P(("seq", "head"), None),
            P(("seq", "head")),
            P(("seq", "head")),
            P("seq", "head"),
            P("seq", "head"),
            P("seq", "head"),
            P("seq", "head"),
            P("head", "seq"),
            P(("seq", "head")),
            P(("seq", "head")),
            P(None, ("seq", "head")),
            P(("seq", "head")),
            P(None, ("seq", "head")),
            P(("seq", "head")),
        ),
        check_vma=False,
    )
```

```python
import functools

import jax
import jax.numpy as jnp
from jax import lax
from jax.experimental import pallas as pl
from jax.experimental.pallas import tpu as pltpu
from jax.sharding import PartitionSpec as P

EPSILON = 1e-5
CHUNK = 128
PAIR = 128
F32 = jnp.float32
BF16 = jnp.bfloat16


def nn(a, b):
    return lax.dot_general(a, b, (((1,), (0,)), ((), ())), preferred_element_type=F32)


def nt(a, b):
    return lax.dot_general(a, b, (((1,), (1,)), ((), ())), preferred_element_type=F32)


def tn(a, b):
    return lax.dot_general(a, b, (((0,), (0,)), ((), ())), preferred_element_type=F32)


def low(v):
    return v.astype(BF16)


def iota(shape, axis):
    return lax.broadcasted_iota(jnp.int32, shape, axis)


def first_half(shape):
    return iota(shape, 1) < PAIR // 2


def stacked(block):
    left = first_half(block.shape)
    zero = jnp.zeros_like(block)
    return jnp.concatenate([jnp.where(left, block, zero), jnp.where(left, zero, block)], axis=0)


def parts(v):
    high = low(v)
    return jnp.concatenate([high, low(v - high.astype(F32))], axis=1)


def whole(v):
    return v[:, :PAIR] + v[:, PAIR:]


def head_block(shape=(PAIR, PAIR)):
    return (iota(shape, 0) < PAIR // 2) == (iota(shape, 1) < PAIR // 2)


def causal_pair():
    return iota((CHUNK, 2 * CHUNK), 0) >= (iota((CHUNK, 2 * CHUNK), 1) & (CHUNK - 1))


def causal_pair_t():
    return iota((CHUNK, 2 * CHUNK), 0) <= (iota((CHUNK, 2 * CHUNK), 1) & (CHUNK - 1))


def ones_where(mask):
    return low(jnp.where(mask, 1.0, 0.0))


def norm_parts(tokens):
    average = jnp.mean(tokens, axis=-1, keepdims=True)
    centred = tokens - average
    rate = lax.rsqrt(jnp.mean(centred * centred, axis=-1, keepdims=True) + EPSILON)
    return centred * rate, rate


def norm_back(grad, normal, rate, gain):
    w = grad * gain
    return rate * (
        w
        - jnp.mean(w, axis=-1, keepdims=True)
        - normal * jnp.mean(w * normal, axis=-1, keepdims=True)
    )


def chunks(length):
    return [slice(c * CHUNK, (c + 1) * CHUNK) for c in range(length // CHUNK)]


def attend_forward(normed, weight, keep):
    q_ref, k_ref, v_ref, powers_ref, inverse_ref, score_ref, prob_ref, key_state, value_state, heads_ref = keep
    cuts = chunks(normed.shape[0])
    tri = ones_where(iota((CHUNK, CHUNK), 0) >= iota((CHUNK, CHUNK), 1))
    same = head_block()
    both = jnp.concatenate([ones_where(same)] * 2, axis=0)
    causal = causal_pair()
    left = first_half((CHUNK, PAIR))
    carried = jnp.zeros((1, PAIR), F32)
    key_sum = jnp.zeros((PAIR, PAIR), F32)
    value_sum = jnp.zeros((PAIR, PAIR), F32)

    def masked(product):
        return low(jnp.where(causal, product, 0.0))

    def lift(score):
        top_a = jnp.max(jnp.where(left, score, -jnp.inf), axis=-1, keepdims=True)
        top_b = jnp.max(jnp.where(left, -jnp.inf, score), axis=-1, keepdims=True)
        return jnp.exp(score - jnp.where(left, top_a, top_b))

    for first in range(0, len(cuts), 8):
        group = list(range(first, min(first + 8, len(cuts))))
        each = range(len(group))
        rows = slice(group[0] * CHUNK, (group[-1] + 1) * CHUNK)
        made = nn(normed[rows, :], weight)
        cut = [made[i * CHUNK : (i + 1) * CHUNK, :] for i in each]
        q = [low(low(m[:, :PAIR]).astype(F32) * 0.125) for m in cut]
        k = [low(m[:, PAIR : 2 * PAIR]) for m in cut]
        v = [low(m[:, 2 * PAIR : 3 * PAIR]) for m in cut]
        powers = [jnp.exp(m[:, 3 * PAIR :]) for m in cut]
        powers_low = [low(p) for p in powers]
        local = [whole(nn(tri, parts(p))) for p in powers]
        scored = [masked(nt(q[i], stacked(k[i]))) for i in each]
        inverse = []
        for i in each:
            running = local[i] + carried
            carried = running[CHUNK - 1 :, :]
            inverse.append(1.0 / running)
        powers_two = [stacked(m) for m in powers_low]
        for i, c in enumerate(group):
            key_state[c, :, :] = low(jnp.where(same, key_sum, 0.0))
            value_state[c, :, :] = low(jnp.where(same, value_sum, 0.0))
            if c + 1 < len(cuts):
                key_sum = key_sum + tn(k[i], powers_low[i])
                value_sum = value_sum + tn(powers_low[i], v[i])
        score = [
            (nn(scored[i], powers_two[i]) + nn(q[i], key_state[c, :, :])) * inverse[i]
            for i, c in enumerate(group)
        ]
        lifted = [lift(m) for m in score]
        prob = [lifted[i] / nn(parts(lifted[i]), both) for i in each]
        reading = [low(prob[i] * inverse[i]) for i in each]
        mixing = [masked(nt(reading[i], powers_two[i])) for i in each]
        for i, c in enumerate(group):
            q_ref[cuts[c], :] = q[i]
            k_ref[cuts[c], :] = k[i]
            v_ref[cuts[c], :] = v[i]
            powers_ref[cuts[c], :] = powers[i]
            inverse_ref[cuts[c], :] = inverse[i]
            score_ref[cuts[c], :] = score[i]
            prob_ref[cuts[c], :] = prob[i]
        for i, c in enumerate(group):
            heads_ref[cuts[c], :] = low(
                nn(mixing[i], stacked(v[i])) + nn(reading[i], value_state[c, :, :])
            )


def attend_backward(heads_grad, kept, backs):
    q_ref, k_ref, v_ref, powers_ref, inverse_ref, score_ref, prob_ref, key_state, value_state = kept
    cuts = chunks(heads_grad.shape[0])
    same = head_block()
    both = jnp.concatenate([ones_where(same)] * 2, axis=0)
    causal = causal_pair()
    causal_t = causal_pair_t()
    tri_t = ones_where(iota((CHUNK, CHUNK), 0) <= iota((CHUNK, CHUNK), 1))
    after_sum = jnp.zeros((1, PAIR), F32)
    read_sum = jnp.zeros((PAIR, PAIR), F32)
    score_sum = jnp.zeros((PAIR, PAIR), F32)

    def masked(product, mask):
        return low(jnp.where(mask, product, 0.0))

    for first in reversed(range(0, len(cuts), 4)):
        group = list(reversed(range(first, min(first + 4, len(cuts)))))
        load = lambda ref: [ref[cuts[c], :] for c in group]
        q, k, v, grad = load(q_ref), load(k_ref), load(v_ref), load(heads_grad)
        inverse, prob, powers = load(inverse_ref), load(prob_ref), load(powers_ref)
        each = range(len(group))
        powers_low = [low(p) for p in powers]
        reading = [low(prob[i] * inverse[i]) for i in each]
        powers_two, values_two = [stacked(m) for m in powers_low], [stacked(m) for m in v]
        grad_two, reading_two = [stacked(m) for m in grad], [stacked(m) for m in reading]
        mixing_grad = [masked(nt(grad[i], values_two[i]), causal) for i in each]
        reading_grad = [
            nn(mixing_grad[i], powers_two[i]) + nt(grad[i], value_state[group[i], :, :]) for i in each
        ]
        mixing_grad_t = [masked(nt(v[i], grad_two[i]), causal_t) for i in each]
        mixing_t = [masked(nt(powers_low[i], reading_two[i]), causal_t) for i in each]
        read_states = []
        for i in each:
            read_states.append(low(jnp.where(same, read_sum, 0.0)))
            if group[i]:
                read_sum = read_sum + tn(reading[i], grad[i])
        prob_grad = [reading_grad[i] * inverse[i] for i in each]
        weighed = [prob[i] * prob_grad[i] for i in each]
        slots_grad = [weighed[i] - prob[i] * nn(parts(weighed[i]), both) for i in each]
        summed_grad = [low(slots_grad[i] * inverse[i]) for i in each]
        running_grad = [
            -inverse[i] * (weighed[i] + slots_grad[i] * score_ref[cuts[group[i]], :]) for i in each
        ]
        powers_grad = [
            nn(mixing_grad_t[i], reading_two[i]) + nt(v[i], read_states[i]) for i in each
        ]
        for i in each:
            backs[cuts[group[i]], 2 * PAIR : 3 * PAIR] = low(
                nn(mixing_t[i], grad_two[i]) + nn(powers_low[i], read_states[i])
            )
        queries_two, keys_two = [stacked(m) for m in q], [stacked(m) for m in k]
        scored_t = [masked(nt(k[i], queries_two[i]), causal_t) for i in each]
        summed_two = [stacked(m) for m in summed_grad]
        score_states = []
        for i in each:
            score_states.append(low(jnp.where(same, score_sum, 0.0)))
            if group[i]:
                score_sum = score_sum + tn(q[i], summed_grad[i])
        scored_grad = [masked(nt(summed_grad[i], powers_two[i]), causal) for i in each]
        scored_grad_t = [masked(nt(powers_low[i], summed_two[i]), causal_t) for i in each]
        later = [whole(nn(tri_t, parts(running_grad[i]))) for i in each]
        powers_grad = [
            powers_grad[i] + nn(scored_t[i], summed_two[i]) + nn(k[i], score_states[i]) for i in each
        ]
        for i in each:
            rows = cuts[group[i]]
            backs[rows, :PAIR] = low(
                0.125 * (nn(scored_grad[i], keys_two[i]) + nt(summed_grad[i], key_state[group[i], :, :]))
            )
            backs[rows, PAIR : 2 * PAIR] = low(
                nn(scored_grad_t[i], queries_two[i]) + nt(powers_low[i], score_states[i])
            )
            total = later[i] + after_sum
            after_sum = total[:1, :]
            backs[rows, 3 * PAIR :] = low((powers_grad[i] + total) * powers[i])


def kept_shapes(length, lead=()):
    n = length // CHUNK
    shape = pltpu.HBM
    return (
        [shape(lead + (length, PAIR), BF16)] * 3
        + [shape(lead + (length, PAIR), F32)] * 4
        + [shape(lead + (n, PAIR, PAIR), BF16)] * 2
    )


def fixed(shape):
    return pl.BlockSpec(shape, lambda a: (0,) * len(shape))


def one_slot(members, slot):
    return [
        pl.BlockSpec((None,) + s.shape[1:], lambda a, rank=len(s.shape): (slot,) + (0,) * (rank - 1))
        for s in members
    ]


def by_step(members, first=0):
    return [
        pl.BlockSpec((None,) + s.shape[1:], lambda a, rank=len(s.shape): (a + first,) + (0,) * (rank - 1))
        for s in members
    ]


def anywhere(members):
    return [pl.BlockSpec(memory_space=pl.ANY)] * len(members)


def mark_spec():
    return pl.BlockSpec(memory_space=pltpu.SMEM)


MARK = jax.ShapeDtypeStruct((1,), F32)


def cost(micros):
    return pl.CostEstimate(flops=int(micros * 1e9), bytes_accessed=int(micros * 1e6), transcendentals=0)


def params(megabytes=56):
    return pltpu.CompilerParams(vmem_limit_bytes=megabytes * 1024 * 1024)


def select(width, offset, share, total):
    return ones_where(
        iota((width, total), 0) == offset + (iota((width, total), 1) & (share - 1))
    )


def owned(devices, share, total):
    return iota((devices, total), 0) == lax.shift_right_logical(
        iota((devices, total), 1), share.bit_length() - 1
    )


def spread(rows, offset, share, total):
    each = nn(rows, select(rows.shape[1], offset, share, total))
    return jnp.sum(jnp.where(owned(rows.shape[0], share, total), each, 0.0), axis=0, keepdims=True)


def collect(rows, devices, share):
    total = rows[0].shape[1]
    mine = owned(devices, share, total)
    out = jnp.zeros((devices, 128), F32)
    for i, row in enumerate(rows):
        rest = jnp.where(mine, row, 0.0)
        high = low(rest)
        pair = jnp.concatenate([high, low(rest - high.astype(F32))], axis=0)
        made = nt(pair, select(128, i * share, share, total))
        out = out + made[:devices] + made[devices:]
    return out


def own_device(core, chip, slots):
    return (lax.axis_index("seq") ^ (2 * chip + core)) * slots


def fill(weight, own_ref, pieces, slot):
    @pl.when(slot == 0)
    def _():
        weight[...] = own_ref[...]

    @pl.when(slot > 0)
    def _():
        rows = weight.shape[0] // len(pieces)
        mine = lax.axis_index("seq") if len(pieces) > 1 else 0
        start = pl.multiple_of((3 - slot if len(pieces) > 1 else slot - 1) * rows, 16)
        for r, piece in enumerate(pieces):
            weight[pl.ds(pl.multiple_of((mine ^ r) * rows, rows), rows), :] = piece[pl.ds(start, rows), :]


def gather_vectors(pieces, rows, slots, vectors):
    for r, piece in enumerate(pieces):
        block = piece[(slots - 1) * rows :, :256].astype(F32)
        for a in range(slots):
            z = lax.rem(lax.axis_index("head") + slots - a, slots)
            source = own_device(r % 2, r // 2, slots) + z
            for i in range(2):
                part = block[a : a + 1, 128 * i : 128 * (i + 1)]
                vectors[pl.ds(source, 1), i : i + 1, :] = part[None]


def forward_kernel(count, slots, tokens_ref, own_ref, *refs):
    pieces, refs = refs[:count], refs[count:]
    if count == 1:
        given, refs = refs[0], refs[1:]
    normed_ref, rows_ref, residual_ref, second_ref, mark, heads_ref, weight = refs[:7]
    keep, staged, vectors = refs[7:-2], refs[-2], refs[-1]
    slot = pl.program_id(0)
    length, width = tokens_ref.shape
    share = width // vectors.shape[0]
    tiles = [slice(r, r + 256) for r in range(0, length, 256)]

    @pl.when(slot == 0)
    def _():
        if count == 1:
            vectors[...] = given[:, :8, :].astype(F32)
        else:
            gather_vectors(pieces, weight.shape[0] // count, slots, vectors)
        for i in range(9):
            part = low(vectors[:, 0 if i < 5 else 1, :])
            rows_ref[i : i + 1, :] = spread(part, (i if i < 5 else i - 5) * share, share, width)
        gain, shift = rows_ref[0:1, :], rows_ref[1:2, :]
        for rows in tiles:
            tokens = tokens_ref[rows, :].astype(F32)
            normal, _ = norm_parts(tokens)
            normed_ref[rows, :] = low(normal * gain + shift)
            residual_ref[rows, :] = tokens
        mark[0] = 1.0

    fill(weight, own_ref, pieces, slot)
    attend_forward(normed_ref, weight[:width, :], list(keep) + [staged])
    heads_ref[...] = staged[...]
    residual_ref[...] += nn(staged[...], weight[width:, :])

    @pl.when(slot == slots - 1)
    def _():
        gain, shift = rows_ref[2:3, :], rows_ref[3:4, :]
        for rows in tiles:
            normal, _ = norm_parts(residual_ref[rows, :])
            second_ref[rows, :] = low(normal * gain + shift)


def forward(tokens, own, pieces, vectors, devices, slots):
    length, width = tokens.shape
    shape = jax.ShapeDtypeStruct
    operands = [tokens, own, *pieces, *vectors]
    outs = [
        shape((length, width), BF16),
        shape((16, width), F32),
        shape((length, width), F32),
        shape((length, width), BF16),
    ]
    stacked_outs = [shape((slots, length, PAIR), BF16), pltpu.HBM((slots, width + PAIR, 4 * PAIR), BF16)]
    stacked_outs += kept_shapes(length, (slots,))
    made = pl.pallas_call(
        functools.partial(forward_kernel, len(pieces), slots),
        grid=(slots,),
        out_shape=outs + [MARK] + stacked_outs,
        in_specs=[fixed(o.shape) for o in operands],
        out_specs=[fixed(o.shape) for o in outs] + [mark_spec()] + by_step(stacked_outs),
        scratch_shapes=[pltpu.VMEM((length, PAIR), BF16), pltpu.VMEM((devices, 8, 128), F32)],
        compiler_params=params(44),
        cost_estimate=cost(17),
        name="attend_forward",
    )(*operands)
    return made[:5], made[5:]


GELU_A = 0.7978845608028654
GELU_B = 0.044715


def gelu_both(u):
    square = u * u
    half = 0.5 + 0.5 * jnp.tanh(u * (GELU_A + GELU_A * GELU_B * square))
    value = u * half
    return value, half + value * (1.0 - half) * (2.0 * GELU_A + 6.0 * GELU_A * GELU_B * square)


def weight_copies(block, pieces, weights, sems):
    if len(pieces) == 1:
        return [pltpu.make_async_copy(pieces[0].at[block], weights.at[block], sems.at[block, 0])]
    copies = []
    for r, piece in enumerate(pieces):
        slots = piece.shape[0]
        copies.append(
            pltpu.make_async_copy(
                piece.at[:, pl.ds(2 * block, 2)],
                weights.at[block, pl.ds(own_device(r % 2, r // 2, slots), slots)],
                sems.at[block, len(copies)],
            )
        )
    return copies


def grad_copies(block, grads, outs, sems):
    if len(outs) == 1:
        return [pltpu.make_async_copy(grads.at[block], outs[0].at[block], sems.at[block, 0])]
    copies = []
    for core, out in enumerate(outs):
        chips, slots = out.shape[:2]
        for chip in range(chips):
            target = (2 * chip + ((lax.axis_index("seq") & 1) ^ core)) * slots
            copies.append(
                pltpu.make_async_copy(
                    grads.at[block, pl.ds(target, slots)],
                    out.at[chip, :, block],
                    sems.at[block, len(copies)],
                )
            )
    return copies


def ffn_kernel(count, second_ref, rows_ref, cotangent_hbm, *refs):
    pieces = refs[:count]
    total, back, sums_ref = refs[count : count + 3]
    outs = refs[count + 3 : -6]
    weights, grads, cotangent_ref, in_sems, out_sems, cotangent_sems = refs[-6:]
    k = pl.program_id(0)
    length, width = second_ref.shape
    tiles = [slice(r, r + 256) for r in range(0, length, 256)]

    def arrive(rows):
        return pltpu.make_async_copy(
            cotangent_hbm.at[rows, :], cotangent_ref.at[rows, :], cotangent_sems.at[rows.start // 256]
        )

    @pl.when(k == 0)
    def _():
        for copy in weight_copies(0, pieces, weights, in_sems):
            copy.start()
        for rows in tiles:
            arrive(rows).start()
        for block in range(1, 4):
            for copy in weight_copies(block, pieces, weights, in_sems):
                copy.start()
        total[...] = jnp.zeros_like(total)
        back[...] = jnp.zeros_like(back)

    for block in range(4):

        @pl.when(k == block)
        def _(block=block):
            for copy in weight_copies(block, pieces, weights, in_sems):
                copy.wait()
            if block == 0:
                for rows in tiles:
                    arrive(rows).wait()

    expand = weights[k, :, 0].reshape(width, width)
    shrink = weights[k, :, 1].reshape(width, width)
    bias = rows_ref[pl.ds(5 + k, 1), :]
    bias_grad = jnp.zeros((1, width), F32)
    acts, hids = [], []
    for rows in tiles:
        hidden = nt(second_ref[rows, :], expand) + bias
        pull = nn(cotangent_ref[rows, :], shrink)
        value, slope = gelu_both(hidden)
        activated = low(value)
        hidden_grad = low(pull * slope)
        bias_grad = bias_grad + jnp.sum(hidden_grad.astype(F32), axis=0, keepdims=True)
        total[rows, :] += nt(activated, shrink)
        back[rows, :] += nn(hidden_grad, expand)
        acts.append(activated)
        hids.append(hidden_grad)
    sums_ref[pl.ds(5 + k, 1), :] = bias_grad
    grads[k, :, 1] = low(tn(cotangent_ref[...], jnp.concatenate(acts, axis=0))).reshape(
        width // 16, 16, width
    )
    grads[k, :, 0] = low(tn(jnp.concatenate(hids, axis=0), second_ref[...])).reshape(width // 16, 16, width)
    for block in range(4):

        @pl.when(k == block)
        def _(block=block):
            for copy in grad_copies(block, grads, outs, out_sems):
                copy.start()

    @pl.when(k == 3)
    def _():
        for block in range(4):
            for copy in grad_copies(block, grads, outs, out_sems):
                copy.wait()


def feed_forward(second, rows, cotangent, pieces, grad_shapes):
    length, width = second.shape
    shape = jax.ShapeDtypeStruct
    weights = (4, width // 16, 2, 16, width)
    outs = [shape((length, width), F32), shape((length, width), F32), shape((16, width), F32)]
    return pl.pallas_call(
        functools.partial(ffn_kernel, len(pieces)),
        grid=(4,),
        out_shape=outs + [shape(s, BF16) for s in grad_shapes],
        in_specs=[fixed(o.shape) for o in (second, rows)]
        + [pl.BlockSpec(memory_space=pltpu.HBM)] * (1 + len(pieces)),
        out_specs=[fixed(o.shape) for o in outs] + anywhere(grad_shapes),
        scratch_shapes=[
            pltpu.VMEM(weights, BF16),
            pltpu.VMEM(weights, BF16),
            pltpu.VMEM((length, width), BF16),
            pltpu.SemaphoreType.DMA((4, 8)),
            pltpu.SemaphoreType.DMA((4, 8)),
            pltpu.SemaphoreType.DMA((length // 256,)),
        ],
        compiler_params=params(36),
        cost_estimate=cost(21),
        name="feed_forward",
    )(second, rows, cotangent, *pieces)


def heads_kernel(total_ref, back_ref, residual_ref, rows_ref, cotangent_ref, sums_in, weight_ref, heads_ref,
                 result_ref, branch, sums_ref, grad_ref, output_grad_ref):
    slots = heads_ref.shape[0]
    length, width = total_ref.shape
    gain, bias = rows_ref[2:3, :], rows_ref[4:5, :]
    gain_grad = jnp.zeros((1, width), F32)
    shift_grad = jnp.zeros((1, width), F32)
    outer = jnp.zeros((1, width), F32)
    for rows in [slice(r, r + 256) for r in range(0, length, 256)]:
        base = residual_ref[rows, :]
        result_ref[rows, :] = low(base + total_ref[rows, :] + bias)
        grad = back_ref[rows, :]
        normal, rate = norm_parts(base)
        upstream = cotangent_ref[rows, :].astype(F32)
        gain_grad = gain_grad + jnp.sum(grad * normal, axis=0, keepdims=True)
        shift_grad = shift_grad + jnp.sum(grad, axis=0, keepdims=True)
        outer = outer + jnp.sum(upstream, axis=0, keepdims=True)
        branch[rows, :] = low(upstream + norm_back(grad, normal, rate, gain))
    sums_ref[...] = sums_in[...]
    sums_ref[2:3, :] = gain_grad
    sums_ref[3:4, :] = shift_grad
    sums_ref[4:5, :] = outer
    weight = weight_ref[...].reshape(slots * PAIR, width)
    grad = low(nt(branch[...], weight))
    heads = jnp.concatenate([heads_ref[a] for a in range(slots)], axis=1)
    output_grad = low(tn(branch[...], heads))
    for a in range(slots):
        grad_ref[a] = grad[:, a * PAIR : (a + 1) * PAIR]
        output_grad_ref[a] = output_grad[:, a * PAIR : (a + 1) * PAIR]


def heads_back(total, back, residual, rows, cotangent, sums, weights, heads):
    slots, length, pair = heads.shape
    width = total.shape[1]
    shape = jax.ShapeDtypeStruct
    operands = [total, back, residual, rows, cotangent, sums]
    outs = [
        shape((length, width), BF16),
        pltpu.HBM((length, width), BF16),
        pltpu.HBM(sums.shape, F32),
        pltpu.HBM((slots, length, pair), BF16),
        pltpu.HBM((slots, width, pair), BF16),
    ]
    return pl.pallas_call(
        heads_kernel,
        grid=(1,),
        out_shape=outs,
        in_specs=[fixed(o.shape) for o in operands]
        + [pl.BlockSpec((slots, pair, width), lambda a: (0, width // pair, 0)), fixed(heads.shape)],
        out_specs=[fixed(o.shape) for o in outs],
        compiler_params=params(28),
        cost_estimate=cost(4),
        name="heads_back",
    )(*operands, weights, heads)


def leave_copies(slot, made, outs, sems):
    if len(outs) == 1:
        return [pltpu.make_async_copy(made, outs[0].at[slot], sems.at[0])]
    seq = lax.axis_index("seq")
    chips = outs[0].shape[0]
    rows = made.shape[0] // (2 * chips)
    copies = []
    for chip in range(chips):
        for core, out in enumerate((outs[0].at[chip], outs[1 + chip])):
            start = pl.multiple_of((seq ^ (2 * chip + core)) * rows, rows)
            copies.append(
                pltpu.make_async_copy(
                    made.at[pl.ds(start, rows), :],
                    out.at[pl.ds(pl.multiple_of(slot * rows, rows), rows), :],
                    sems.at[len(copies)],
                )
            )
    return copies


def back_kernel(waits, parts_out, slots, rows_ref, before_ref, normed_hbm, tokens_hbm, residual_grad_hbm, *refs):
    refs = refs[waits:]
    weight, grad_ref, output_grad_ref, kept, refs = refs[0], refs[1], refs[2], refs[3:12], refs[12:]
    input_grad_hbm, sums_ref, outs, mark = refs[0], refs[1], refs[2 : 2 + parts_out], refs[2 + parts_out]
    (backs, made, total, input_grad_ref, normed_ref, tokens, residual_grad, vector_blocks, sems, out_sems, tile_sems) = refs[3 + parts_out :]
    length, width = normed_ref.shape
    devices = sums_ref.shape[0]
    share = width // devices
    step, steps = pl.program_id(0), slots
    copies = [
        pltpu.make_async_copy(tokens_hbm, tokens, sems.at[0]),
        pltpu.make_async_copy(residual_grad_hbm, residual_grad, sems.at[1]),
    ]
    fetch = pltpu.make_async_copy(normed_hbm, normed_ref, tile_sems.at[length // 256])

    @pl.when(step == 0)
    def _():
        fetch.start()
        for copy in copies:
            copy.start()
        total[...] = jnp.zeros_like(total)
        mark[0] = 1.0

    parity = lax.rem(step, 2)

    @pl.when(step >= 2)
    def _():
        for copy in leave_copies(step - 2, made.at[parity], outs, out_sems.at[parity]):
            copy.wait()

    attend_backward(grad_ref, kept, backs)

    @pl.when(step == 0)
    def _():
        fetch.wait()

    made[parity, :, : 4 * PAIR] = low(tn(normed_ref[...], backs[...]))
    made[parity, :, 4 * PAIR :] = output_grad_ref[...]
    for copy in leave_copies(step, made.at[parity], outs, out_sems.at[parity]):
        copy.start()
    total[...] += nt(backs[...], weight[:width, :])

    @pl.when(step == steps - 1)
    def _():
        for copy in copies:
            copy.wait()
        gain = rows_ref[0:1, :]
        gain_grad = jnp.zeros((1, width), F32)
        shift_grad = jnp.zeros((1, width), F32)
        left = []
        for rows in [slice(r, r + 256) for r in range(0, length, 256)]:
            grad = total[rows, :]
            normal, rate = norm_parts(tokens[rows, :].astype(F32))
            gain_grad = gain_grad + jnp.sum(grad * normal, axis=0, keepdims=True)
            shift_grad = shift_grad + jnp.sum(grad, axis=0, keepdims=True)
            input_grad_ref[rows, :] = low(residual_grad[rows, :].astype(F32) + norm_back(grad, normal, rate, gain))
            left.append(
                pltpu.make_async_copy(
                    input_grad_ref.at[rows, :], input_grad_hbm.at[rows, :], tile_sems.at[rows.start // 256]
                )
            )
            left[-1].start()
        small = [gain_grad, shift_grad] + [before_ref[i : i + 1, :] for i in range(2, 5)]
        sums_ref[:, :128] = collect(small, devices, share)
        sums_ref[:, 128:] = collect([before_ref[i : i + 1, :] for i in range(5, 9)], devices, share)
        leaving = []
        if parts_out > 1:
            z, chips = lax.axis_index("head"), outs[0].shape[0]
            for chip in range(chips):
                for core, out in enumerate((outs[0].at[chip], outs[1 + chip])):
                    n = len(leaving)
                    rows = [
                        sums_ref[pl.ds(own_device(core, chip, steps) + lax.rem(z + steps - a, steps), 1), :]
                        for a in range(steps)
                    ]
                    block = jnp.concatenate(rows + [jnp.zeros((16 - steps, 256), F32)], axis=0)
                    vector_blocks[n] = vector_rows(block, made.shape[2])
                    leaving.append(
                        pltpu.make_async_copy(
                            vector_blocks.at[n], out.at[pl.ds(out.shape[0] - 16, 16), :], sems.at[2 + n]
                        )
                    )
        for copy in leaving:
            copy.start()
        for last in (steps - 2, steps - 1):
            for copy in leave_copies(last, made.at[last % 2], outs, out_sems.at[last % 2]):
                copy.wait()
        for copy in leaving + left:
            copy.wait()


def backward(normed, rows, before, tokens, residual_grad, devices, waits, members, grad_shapes):
    length, width = normed.shape
    slots = members[0].shape[0]
    shape = jax.ShapeDtypeStruct
    outs = [pltpu.HBM((length, width), BF16), shape((devices, 256), F32)]
    grads = [shape(s, BF16) for s in grad_shapes]
    large = [normed, tokens, residual_grad]
    return pl.pallas_call(
        functools.partial(back_kernel, len(waits), len(grad_shapes), slots),
        grid=(slots,),
        out_shape=outs + grads + [MARK],
        in_specs=[fixed(o.shape) for o in (rows, before)] + anywhere(large + waits) + by_step(members),
        out_specs=[pl.BlockSpec(memory_space=pltpu.HBM), fixed(outs[1].shape)] + anywhere(grads) + [mark_spec()],
        scratch_shapes=[
            pltpu.VMEM((length, 4 * PAIR), BF16),
            pltpu.VMEM((2, width, 5 * PAIR), BF16),
            pltpu.VMEM((length, width), F32),
            pltpu.VMEM((length, width), BF16),
        ]
        + [pltpu.VMEM((length, width), m.dtype) for m in large]
        + [
            pltpu.VMEM((8, 16, 5 * PAIR), BF16),
            pltpu.SemaphoreType.DMA((10,)),
            pltpu.SemaphoreType.DMA((2, 8)),
            pltpu.SemaphoreType.DMA((length // 256 + 1,)),
        ],
        compiler_params=params(),
        cost_estimate=cost(27),
        name="attend_back",
    )(rows, before, *large, *waits, *members)


def after(value, *others):
    return pl.pallas_call(
        lambda *refs: None,
        out_shape=jax.ShapeDtypeStruct(value.shape, value.dtype),
        in_specs=anywhere((value,) + others),
        out_specs=anywhere([value])[0],
        input_output_aliases={0: 0},
        name="after",
    )(value, *others)


def near_kernel(slots, block_ref, load_ref, *refs):
    came, (near_ref, loads_ref) = refs[: slots - 1], refs[slots - 1 :]
    rows = came[0].shape[0] - 16
    for a, piece in enumerate(came):
        near_ref[a * rows : (a + 1) * rows, :] = piece[:rows, :]
    lines = [block_ref[...].astype(F32)[0:1, :]]
    lines += [piece[rows:, :].astype(F32)[0:1, :] for piece in reversed(came)]
    lines += [jnp.zeros((16 - slots, block_ref.shape[1]), F32)]
    near_ref[(slots - 1) * rows :, :] = low(jnp.concatenate(lines, axis=0))
    for z in range(slots):
        loads_ref[z] = load_ref[...]


def join_near(block, load, came):
    shape = jax.ShapeDtypeStruct
    slots = len(came) + 1
    rows = came[0].shape[0] - 16
    operands = [block, load, *came]
    outs = [
        shape(((slots - 1) * rows + 16, block.shape[1]), BF16),
        shape((slots,) + load.shape, BF16),
    ]
    return pl.pallas_call(
        functools.partial(near_kernel, slots),
        grid=(1,),
        out_shape=outs,
        in_specs=[fixed(o.shape) for o in operands],
        out_specs=[fixed(o.shape) for o in outs],
        compiler_params=params(12),
        cost_estimate=cost(1),
        name="join_near",
    )(*operands)


def vector_values(block):
    return block[:, :256].astype(F32) + block[:, 256:512].astype(F32)


def vector_rows(values, width):
    high = low(values)
    rest = jnp.zeros((values.shape[0], width - 512), BF16)
    return jnp.concatenate([high, low(values - high.astype(F32)), rest], axis=1)


def halve_kernel(keep_ref, other_ref, out_ref):
    out_ref[...] = low(add(keep_ref[...], other_ref[...]))


def halve(keep, other):
    return pl.pallas_call(
        halve_kernel,
        grid=(keep.shape[0],),
        out_shape=pltpu.HBM(keep.shape, BF16),
        in_specs=by_step([keep, other]),
        out_specs=by_step([keep])[0],
        compiler_params=params(44),
        cost_estimate=cost(2),
        name="halve",
    )(keep, other)


def join_kernel(chips, slots, ffn_ref, keep_hbm, *refs):
    others, ffn_outs, outs = refs[:chips], refs[chips : chips + slots], refs[chips + slots : -2]
    keep_ref, sems = refs[-2:]
    copies = [pltpu.make_async_copy(keep_hbm.at[c], keep_ref.at[c], sems.at[c]) for c in range(chips)]
    for copy in copies:
        copy.start()
    z = lax.axis_index("head")
    for a, out in enumerate(ffn_outs):
        place = lax.rem(z + a, slots)
        out[...] = low(add(*[ffn_ref[c, pl.ds(place, 1)][0] for c in range(chips)]))
    body = keep_ref.shape[1] - 16
    for chip, out in enumerate(outs):
        copies[chip].wait()
        out[:body, :] = low(add(keep_ref[chip, :body, :], others[chip][:body, :]))
        values = vector_values(keep_ref[chip, body:, :]) + vector_values(others[chip][body:, :])
        out[body:, :] = vector_rows(values, out.shape[1])


def join(ffn, keep, others):
    shape = jax.ShapeDtypeStruct
    chips, slots = ffn.shape[:2]
    operands = [ffn, pltpu.with_memory_space_constraint(keep, pltpu.HBM), *others]
    outs = [shape(ffn.shape[2:], BF16)] * slots + [shape(keep.shape[1:], BF16)] * chips
    made = pl.pallas_call(
        functools.partial(join_kernel, chips, slots),
        grid=(1,),
        out_shape=outs,
        in_specs=[fixed(ffn.shape), pl.BlockSpec(memory_space=pltpu.HBM)] + [fixed(o.shape) for o in others],
        out_specs=[fixed(o.shape) for o in outs],
        scratch_shapes=[pltpu.VMEM(keep.shape, BF16), pltpu.SemaphoreType.DMA((chips,))],
        compiler_params=params(44),
        cost_estimate=cost(3),
        name="join",
    )(*operands)
    return made[:slots], made[slots:]


def sum_plane_kernel(slots, pairs, mine_ref, vector_ref, sends, mark):
    rows = mine_ref.shape[0]
    values = functools.reduce(lambda x, y: x + y, [vector_values(p[slots * rows :, :]) for p in pairs])
    vector_ref[...] = values[:8, :]
    for a in range(slots):
        mine = add(*[p[a * rows : (a + 1) * rows, :] for p in pairs])
        if a == 0:
            mine_ref[...] = mine
        else:
            sends[a - 1][:rows, :] = low(mine)
            sends[a - 1][rows:, :] = vector_rows(jnp.broadcast_to(values[a : a + 1, :], (16, 256)), mine.shape[1])
    mark[0] = 1.0


def sum_plane(pairs, slots, waits):
    shape = jax.ShapeDtypeStruct
    rows, columns = (pairs[0].shape[0] - 16) // slots, pairs[0].shape[1]
    outs = [shape((rows, columns), F32), shape((8, 256), F32)]
    outs += [shape((rows + 16, columns), BF16)] * (slots - 1)

    def kernel(*refs):
        made = refs[len(pairs) + len(waits) :]
        sum_plane_kernel(slots, refs[: len(pairs)], made[0], made[1], made[2:-1], made[-1])

    return pl.pallas_call(
        kernel,
        grid=(1,),
        out_shape=outs + [MARK],
        in_specs=[fixed(p.shape) for p in pairs] + anywhere(waits),
        out_specs=[fixed(o.shape) for o in outs] + [mark_spec()],
        compiler_params=params(12),
        cost_estimate=cost(2),
        name="sum_plane",
    )(*pairs, *waits)


def settle_kernel(ffn, expand_ref, shrink_ref):
    blocks, _, share, width = ffn[0].shape
    total = add(*[f[...] for f in ffn])
    expand_ref[...] = total[:, 0].reshape(blocks * share, width).T
    for i in range(blocks):
        shrink_ref[:, i] = total[i, 1].T.reshape(width // share, share, share)


def settle(ffn, wait):
    shape = jax.ShapeDtypeStruct
    slots = len(ffn)
    blocks, _, share, width = ffn[0].shape
    outs = [shape((width, blocks * share), F32), shape((width // share, blocks, share, share), F32)]

    def kernel(*refs):
        settle_kernel(refs[:slots], *refs[slots + 1 :])

    return pl.pallas_call(
        kernel,
        grid=(1,),
        out_shape=outs,
        in_specs=[fixed(f.shape) for f in ffn] + anywhere([wait]),
        out_specs=[fixed(o.shape) for o in outs],
        compiler_params=params(12),
        cost_estimate=cost(3),
        name="settle",
    )(*ffn, wait)


def finish_kernel(share, hidden_share, mine_ref, sums_ref, *refs):
    came, parts, vectors = refs[:3], refs[3:8], refs[8:]
    rows = mine_ref.shape[0]
    total = add(mine_ref[...], *[c[:rows, :] for c in came])
    for i, part in enumerate(parts):
        part[...] = total[:, i * PAIR : (i + 1) * PAIR]
    values = add(sums_ref[0:1, :], *[vector_values(c[rows:, :])[0:1, :] for c in came])
    for i, vector in enumerate(vectors[:-1]):
        vector[...] = values[0, i * share : (i + 1) * share]
    vectors[-1][...] = values[0, 128 : 128 + hidden_share]


def finish(mine, sums, came, share, hidden_share):
    shape = jax.ShapeDtypeStruct
    operands = [mine, sums, *came]
    outs = [shape((mine.shape[0], PAIR), F32)] * 5 + [shape((share,), F32)] * 5 + [shape((hidden_share,), F32)]
    made = pl.pallas_call(
        functools.partial(finish_kernel, share, hidden_share),
        grid=(1,),
        out_shape=outs,
        in_specs=[fixed(o.shape) for o in operands],
        out_specs=[fixed(o.shape) for o in outs],
        compiler_params=params(12),
        cost_estimate=cost(1),
        name="finish",
    )(*operands)
    return made[:5], made[5:]


def flip(count, bit):
    return [(i, i ^ bit) for i in range(count)]


def turn(count, by):
    return [(i, (i + by) % count) for i in range(count)]


def add(*members):
    return functools.reduce(lambda a, b: a + b, [m.astype(F32) for m in members])


def to_mate(shares, seqs):
    return lax.ppermute(shares, "seq", flip(seqs, 1))


def over_chips(shares, chips, seqs):
    return [shares] + [lax.ppermute(shares, "seq", flip(seqs, 2 * r)) for r in range(1, chips)]


def over_cores(held, seqs):
    return [member for h in held for member in (h, to_mate(h, seqs))]


def to_chips(shares, seqs):
    plane = [list(range(core, seqs, 2)) for core in range(2)]
    return lax.all_to_all(shares, "seq", 0, 0, axis_index_groups=plane, tiled=True)


def from_chips(sends, seqs):
    return [lax.ppermute(m, "seq", flip(seqs, 2 * r + 2)) for r, m in enumerate(sends)]


def body(
    inputs,
    attn_gain,
    attn_shift,
    query_weight,
    key_weight,
    value_weight,
    control_weight,
    output_weight,
    ffn_gain,
    ffn_shift,
    expand_weight,
    expand_bias,
    shrink_weight,
    shrink_bias,
    cotangent,
):
    seqs, slots = lax.axis_size("seq"), lax.axis_size("head")
    devices = seqs * slots
    chips = seqs // 2
    width = inputs.shape[1]
    share = width // devices
    hidden_share = expand_weight.shape[1]
    z = lax.axis_index("head")
    direct = seqs == 8 and slots == 4 and share == 16 and hidden_share == 4 * share

    own = jnp.concatenate(
        [
            jnp.concatenate([query_weight, key_weight, value_weight, control_weight], axis=1),
            output_weight,
        ],
        axis=0,
    )
    places = [(attn_gain, 0), (attn_shift, 1), (ffn_gain, 2), (ffn_shift, 3), (shrink_bias, 4)]
    row = functools.reduce(
        lambda a, b: a + b,
        [jnp.pad(m, (i * share, width - (i + 1) * share)) for m, i in places]
        + [jnp.pad(expand_bias, (128, width - 128 - hidden_share))],
    )
    block = jnp.pad(row[None, :], ((0, 15), (0, 0)))
    expand_t = expand_weight.T.reshape(4, share, width)
    shrink_t = shrink_weight.reshape(devices, 4, share, share).transpose(1, 3, 0, 2).reshape(4, share, width)
    load = jnp.stack([expand_t, shrink_t], axis=1)
    if direct:
        rows = own.shape[0] // seqs
        piece = lax.dynamic_slice_in_dim(own, lax.axis_index("seq") * rows, rows, axis=0)
        piece = jnp.concatenate([piece, block], axis=0)
        came = [lax.ppermute(piece, "head", turn(slots, a)) for a in range(1, slots)]
        near, loads = join_near(block, load.reshape(8, share, width), came[::-1])
        pieces, vectors = over_cores(over_chips(near, chips, seqs), seqs), []
        load = lax.all_to_all(loads, "head", 0, 0, tiled=True)
        held = over_chips(load, chips, seqs)
        tall = (slots * width // seqs + 16, 5 * PAIR)
        pair_shapes = [(chips,) + tall] + [tall] * chips
        ffn_shapes = [(chips, slots, 4, 2, 16, width)] * 2
    else:
        every = lax.all_gather(own, "head", axis=0, tiled=False)
        pieces = [jnp.concatenate([every[(z + slots - a) % slots] for a in range(1, slots)], axis=0)]
        block = jnp.concatenate([block[:1, :128], block[:1, 128:256], block[2:, :128]], axis=0)
        vectors = [lax.all_gather(block, ("seq", "head"), axis=0, tiled=False)]
        both = lax.all_gather(load, ("seq", "head"), axis=2, tiled=True)
        ffn_pieces = [both.reshape(4, 2, width // 16, 16, width).transpose(0, 2, 1, 3, 4)]
        pair_shapes = [(slots, width, 5 * PAIR)]
        ffn_shapes = [ffn_pieces[0].shape]

    (normed, rows, residual, second, mark), (heads, weights, *members) = forward(
        inputs, own, pieces, vectors, devices, slots
    )
    if direct:
        ffn_pieces = over_cores(held[:-1] + [low(held[-1].astype(F32) * mark[0])], seqs)
    total, back, sums, *ffn_grads = feed_forward(second, rows, cotangent, ffn_pieces, ffn_shapes)
    result, branch, sums, heads_grad, output_grad = heads_back(
        total, back, residual, rows, cotangent, sums, weights, heads
    )
    members = [weights, heads_grad, output_grad, *members]
    waits = []
    if direct:
        ffn_mine = halve(ffn_grads[0], to_mate(ffn_grads[1], seqs))
        waits = [ffn_mine]
    input_grad, sums, *pair_grads, _ = backward(
        normed, rows, sums, inputs, branch, devices, waits, members, pair_shapes
    )

    if direct:
        keep, *sends = pair_grads
        ffn, pairs = join(to_chips(ffn_mine, seqs), keep, [to_mate(m, seqs) for m in sends])
        ffn = [ffn[0]] + [lax.ppermute(ffn[a], "head", turn(slots, a)) for a in range(1, slots)]
        pairs = [pairs[0]] + from_chips(pairs[1:], seqs)
        mine, sums, *sends, wait = sum_plane(pairs, slots, ffn[1:])
        expand_grad, shrink_grad = settle(ffn, wait)
        came = [lax.ppermute(m, "head", turn(slots, slots - 1 - a)) for a, m in enumerate(sends)]
        parts, vector = finish(mine, sums, came[::-1], share, hidden_share)
    else:
        ffn_sum = lax.psum_scatter(
            ffn_grads[0].astype(F32).transpose(0, 2, 1, 3, 4).reshape(4, 2, width, width), ("seq", "head"), scatter_dimension=2, tiled=True
        )
        every = pair_grads[0].astype(F32)
        every = jnp.stack([every[(z + slots - p) % slots] for p in range(slots)])
        pair_sum = lax.psum_scatter(every, "head", scatter_dimension=0, tiled=False)
        pair_sum = lax.psum_scatter(pair_sum, "seq", scatter_dimension=0, tiled=True)

        sums = jnp.sum(
            lax.all_to_all(sums.reshape(devices, 1, 256), ("seq", "head"), 0, 0, tiled=True), axis=(0, 1)
        )
        expand_grad = ffn_sum[:, 0].reshape(hidden_share, width).T
        shrink_grad = ffn_sum[:, 1].reshape(4, share, devices, share).transpose(2, 0, 3, 1)

        parts = [pair_sum[:, i * PAIR : (i + 1) * PAIR] for i in range(5)]
        vector = [sums[i * share : (i + 1) * share] for i in range(5)] + [sums[128 : 128 + hidden_share]]

    return (
        result,
        input_grad,
        vector[0],
        vector[1],
        *parts[:4],
        parts[4].T,
        vector[2],
        vector[3],
        expand_grad,
        vector[5],
        shrink_grad.reshape(devices * hidden_share, share),
        vector[4],
    )


def solution(mesh):
    placed = (
        P(("seq", "head"), None),
        P(("seq", "head")),
        P(("seq", "head")),
        P(None, "head"),
        P(None, "head"),
        P(None, "head"),
        P(None, "head"),
        P("head", None),
        P(("seq", "head")),
        P(("seq", "head")),
        P(None, ("seq", "head")),
        P(("seq", "head")),
        P(None, ("seq", "head")),
        P(("seq", "head")),
        P(("seq", "head"), None),
    )
    return jax.shard_map(
        body,
        mesh=mesh,
        in_specs=placed,
        out_specs=(
            P(("seq", "head"), None),
            P(("seq", "head"), None),
            P(("seq", "head")),
            P(("seq", "head")),
            P("seq", "head"),
            P("seq", "head"),
            P("seq", "head"),
            P("seq", "head"),
            P("head", "seq"),
            P(("seq", "head")),
            P(("seq", "head")),
            P(None, ("seq", "head")),
            P(("seq", "head")),
            P(None, ("seq", "head")),
            P(("seq", "head")),
        ),
        check_vma=False,
    )
```

```python
import functools

import jax
import jax.numpy as jnp
from jax import lax
from jax.experimental import pallas as pl
from jax.experimental.pallas import tpu as pltpu
from jax.sharding import PartitionSpec as P

EPSILON = 1e-5
CHUNK = 128
PAIR = 128
F32 = jnp.float32
BF16 = jnp.bfloat16


def nn(a, b):
    return lax.dot_general(a, b, (((1,), (0,)), ((), ())), preferred_element_type=F32)


def nt(a, b):
    return lax.dot_general(a, b, (((1,), (1,)), ((), ())), preferred_element_type=F32)


def tn(a, b):
    return lax.dot_general(a, b, (((0,), (0,)), ((), ())), preferred_element_type=F32)


def low(v):
    return v.astype(BF16)


def iota(shape, axis):
    return lax.broadcasted_iota(jnp.int32, shape, axis)


def first_half(shape):
    return iota(shape, 1) < PAIR // 2


def stacked(block):
    left = first_half(block.shape)
    zero = jnp.zeros_like(block)
    return jnp.concatenate([jnp.where(left, block, zero), jnp.where(left, zero, block)], axis=0)


def parts(v):
    high = low(v)
    return jnp.concatenate([high, low(v - high.astype(F32))], axis=1)


def whole(v):
    return v[:, :PAIR] + v[:, PAIR:]


def head_block(shape=(PAIR, PAIR)):
    return (iota(shape, 0) < PAIR // 2) == (iota(shape, 1) < PAIR // 2)


def causal_pair():
    return iota((CHUNK, 2 * CHUNK), 0) >= (iota((CHUNK, 2 * CHUNK), 1) & (CHUNK - 1))


def causal_pair_t():
    return iota((CHUNK, 2 * CHUNK), 0) <= (iota((CHUNK, 2 * CHUNK), 1) & (CHUNK - 1))


def ones_where(mask):
    return low(jnp.where(mask, 1.0, 0.0))


def norm_parts(tokens):
    average = jnp.mean(tokens, axis=-1, keepdims=True)
    centred = tokens - average
    rate = lax.rsqrt(jnp.mean(centred * centred, axis=-1, keepdims=True) + EPSILON)
    return centred * rate, rate


def norm_back(grad, normal, rate, gain):
    w = grad * gain
    return rate * (
        w
        - jnp.mean(w, axis=-1, keepdims=True)
        - normal * jnp.mean(w * normal, axis=-1, keepdims=True)
    )


def chunks(length):
    return [slice(c * CHUNK, (c + 1) * CHUNK) for c in range(length // CHUNK)]


def attend_forward(normed, weight, keep):
    q_ref, k_ref, v_ref, powers_ref, inverse_ref, score_ref, prob_ref, key_state, value_state, heads_ref = keep
    cuts = chunks(normed.shape[0])
    tri = ones_where(iota((CHUNK, CHUNK), 0) >= iota((CHUNK, CHUNK), 1))
    same = head_block()
    both = jnp.concatenate([ones_where(same)] * 2, axis=0)
    causal = causal_pair()
    left = first_half((CHUNK, PAIR))
    carried = jnp.zeros((1, PAIR), F32)
    key_sum = jnp.zeros((PAIR, PAIR), F32)
    value_sum = jnp.zeros((PAIR, PAIR), F32)

    def masked(product):
        return low(jnp.where(causal, product, 0.0))

    def lift(score):
        top_a = jnp.max(jnp.where(left, score, -jnp.inf), axis=-1, keepdims=True)
        top_b = jnp.max(jnp.where(left, -jnp.inf, score), axis=-1, keepdims=True)
        return jnp.exp(score - jnp.where(left, top_a, top_b))

    for first in range(0, len(cuts), 8):
        group = list(range(first, min(first + 8, len(cuts))))
        each = range(len(group))
        rows = slice(group[0] * CHUNK, (group[-1] + 1) * CHUNK)
        made = nn(normed[rows, :], weight)
        cut = [made[i * CHUNK : (i + 1) * CHUNK, :] for i in each]
        q = [low(low(m[:, :PAIR]).astype(F32) * 0.125) for m in cut]
        k = [low(m[:, PAIR : 2 * PAIR]) for m in cut]
        v = [low(m[:, 2 * PAIR : 3 * PAIR]) for m in cut]
        powers = [jnp.exp(m[:, 3 * PAIR :]) for m in cut]
        powers_low = [low(p) for p in powers]
        local = [whole(nn(tri, parts(p))) for p in powers]
        scored = [masked(nt(q[i], stacked(k[i]))) for i in each]
        inverse = []
        for i in each:
            running = local[i] + carried
            carried = running[CHUNK - 1 :, :]
            inverse.append(1.0 / running)
        powers_two = [stacked(m) for m in powers_low]
        for i, c in enumerate(group):
            key_state[c, :, :] = low(jnp.where(same, key_sum, 0.0))
            value_state[c, :, :] = low(jnp.where(same, value_sum, 0.0))
            if c + 1 < len(cuts):
                key_sum = key_sum + tn(k[i], powers_low[i])
                value_sum = value_sum + tn(powers_low[i], v[i])
        score = [
            (nn(scored[i], powers_two[i]) + nn(q[i], key_state[c, :, :])) * inverse[i]
            for i, c in enumerate(group)
        ]
        lifted = [lift(m) for m in score]
        prob = [lifted[i] / nn(parts(lifted[i]), both) for i in each]
        reading = [low(prob[i] * inverse[i]) for i in each]
        mixing = [masked(nt(reading[i], powers_two[i])) for i in each]
        for i, c in enumerate(group):
            q_ref[cuts[c], :] = q[i]
            k_ref[cuts[c], :] = k[i]
            v_ref[cuts[c], :] = v[i]
            powers_ref[cuts[c], :] = powers[i]
            inverse_ref[cuts[c], :] = inverse[i]
            score_ref[cuts[c], :] = score[i]
            prob_ref[cuts[c], :] = prob[i]
        for i, c in enumerate(group):
            heads_ref[cuts[c], :] = low(
                nn(mixing[i], stacked(v[i])) + nn(reading[i], value_state[c, :, :])
            )


def attend_backward(heads_grad, kept, backs):
    q_ref, k_ref, v_ref, powers_ref, inverse_ref, score_ref, prob_ref, key_state, value_state = kept
    cuts = chunks(heads_grad.shape[0])
    same = head_block()
    both = jnp.concatenate([ones_where(same)] * 2, axis=0)
    causal = causal_pair()
    causal_t = causal_pair_t()
    tri_t = ones_where(iota((CHUNK, CHUNK), 0) <= iota((CHUNK, CHUNK), 1))
    after_sum = jnp.zeros((1, PAIR), F32)
    read_sum = jnp.zeros((PAIR, PAIR), F32)
    score_sum = jnp.zeros((PAIR, PAIR), F32)

    def masked(product, mask):
        return low(jnp.where(mask, product, 0.0))

    for first in reversed(range(0, len(cuts), 4)):
        group = list(reversed(range(first, min(first + 4, len(cuts)))))
        load = lambda ref: [ref[cuts[c], :] for c in group]
        q, k, v, grad = load(q_ref), load(k_ref), load(v_ref), load(heads_grad)
        inverse, prob, powers = load(inverse_ref), load(prob_ref), load(powers_ref)
        each = range(len(group))
        powers_low = [low(p) for p in powers]
        reading = [low(prob[i] * inverse[i]) for i in each]
        powers_two, values_two = [stacked(m) for m in powers_low], [stacked(m) for m in v]
        grad_two, reading_two = [stacked(m) for m in grad], [stacked(m) for m in reading]
        mixing_grad = [masked(nt(grad[i], values_two[i]), causal) for i in each]
        reading_grad = [
            nn(mixing_grad[i], powers_two[i]) + nt(grad[i], value_state[group[i], :, :]) for i in each
        ]
        mixing_grad_t = [masked(nt(v[i], grad_two[i]), causal_t) for i in each]
        mixing_t = [masked(nt(powers_low[i], reading_two[i]), causal_t) for i in each]
        read_states = []
        for i in each:
            read_states.append(low(jnp.where(same, read_sum, 0.0)))
            if group[i]:
                read_sum = read_sum + tn(reading[i], grad[i])
        prob_grad = [reading_grad[i] * inverse[i] for i in each]
        weighed = [prob[i] * prob_grad[i] for i in each]
        slots_grad = [weighed[i] - prob[i] * nn(parts(weighed[i]), both) for i in each]
        summed_grad = [low(slots_grad[i] * inverse[i]) for i in each]
        running_grad = [
            -inverse[i] * (weighed[i] + slots_grad[i] * score_ref[cuts[group[i]], :]) for i in each
        ]
        powers_grad = [
            nn(mixing_grad_t[i], reading_two[i]) + nt(v[i], read_states[i]) for i in each
        ]
        for i in each:
            backs[cuts[group[i]], 2 * PAIR : 3 * PAIR] = low(
                nn(mixing_t[i], grad_two[i]) + nn(powers_low[i], read_states[i])
            )
        queries_two, keys_two = [stacked(m) for m in q], [stacked(m) for m in k]
        scored_t = [masked(nt(k[i], queries_two[i]), causal_t) for i in each]
        summed_two = [stacked(m) for m in summed_grad]
        score_states = []
        for i in each:
            score_states.append(low(jnp.where(same, score_sum, 0.0)))
            if group[i]:
                score_sum = score_sum + tn(q[i], summed_grad[i])
        scored_grad = [masked(nt(summed_grad[i], powers_two[i]), causal) for i in each]
        scored_grad_t = [masked(nt(powers_low[i], summed_two[i]), causal_t) for i in each]
        later = [whole(nn(tri_t, parts(running_grad[i]))) for i in each]
        powers_grad = [
            powers_grad[i] + nn(scored_t[i], summed_two[i]) + nn(k[i], score_states[i]) for i in each
        ]
        for i in each:
            rows = cuts[group[i]]
            backs[rows, :PAIR] = low(
                0.125 * (nn(scored_grad[i], keys_two[i]) + nt(summed_grad[i], key_state[group[i], :, :]))
            )
            backs[rows, PAIR : 2 * PAIR] = low(
                nn(scored_grad_t[i], queries_two[i]) + nt(powers_low[i], score_states[i])
            )
            total = later[i] + after_sum
            after_sum = total[:1, :]
            backs[rows, 3 * PAIR :] = low((powers_grad[i] + total) * powers[i])


def kept_shapes(length, lead=()):
    n = length // CHUNK
    shape = pltpu.HBM
    return (
        [shape(lead + (length, PAIR), BF16)] * 3
        + [shape(lead + (length, PAIR), F32)] * 4
        + [shape(lead + (n, PAIR, PAIR), BF16)] * 2
    )


def fixed(shape):
    return pl.BlockSpec(shape, lambda a: (0,) * len(shape))


def one_slot(members, slot):
    return [
        pl.BlockSpec((None,) + s.shape[1:], lambda a, rank=len(s.shape): (slot,) + (0,) * (rank - 1))
        for s in members
    ]


def by_step(members, first=0):
    return [
        pl.BlockSpec((None,) + s.shape[1:], lambda a, rank=len(s.shape): (a + first,) + (0,) * (rank - 1))
        for s in members
    ]


def anywhere(members):
    return [pl.BlockSpec(memory_space=pl.ANY)] * len(members)


def mark_spec():
    return pl.BlockSpec(memory_space=pltpu.SMEM)


MARK = jax.ShapeDtypeStruct((1,), F32)


def cost(micros):
    return pl.CostEstimate(flops=int(micros * 1e9), bytes_accessed=int(micros * 1e6), transcendentals=0)


def params(megabytes=56):
    return pltpu.CompilerParams(vmem_limit_bytes=megabytes * 1024 * 1024)


def select(width, offset, share, total):
    return ones_where(
        iota((width, total), 0) == offset + (iota((width, total), 1) & (share - 1))
    )


def owned(devices, share, total):
    return iota((devices, total), 0) == lax.shift_right_logical(
        iota((devices, total), 1), share.bit_length() - 1
    )


def spread(rows, offset, share, total):
    each = nn(rows, select(rows.shape[1], offset, share, total))
    return jnp.sum(jnp.where(owned(rows.shape[0], share, total), each, 0.0), axis=0, keepdims=True)


def collect(rows, devices, share):
    total = rows[0].shape[1]
    mine = owned(devices, share, total)
    out = jnp.zeros((devices, 128), F32)
    for i, row in enumerate(rows):
        rest = jnp.where(mine, row, 0.0)
        high = low(rest)
        pair = jnp.concatenate([high, low(rest - high.astype(F32))], axis=0)
        made = nt(pair, select(128, i * share, share, total))
        out = out + made[:devices] + made[devices:]
    return out


def own_device(core, chip, slots):
    return (lax.axis_index("seq") ^ (2 * chip + core)) * slots


def fill(weight, own_ref, pieces, slot):
    @pl.when(slot == 0)
    def _():
        weight[...] = own_ref[...]

    @pl.when(slot > 0)
    def _():
        rows = weight.shape[0] // len(pieces)
        mine = lax.axis_index("seq") if len(pieces) > 1 else 0
        start = pl.multiple_of((3 - slot if len(pieces) > 1 else slot - 1) * rows, 16)
        for r, piece in enumerate(pieces):
            weight[pl.ds(pl.multiple_of((mine ^ r) * rows, rows), rows), :] = piece[pl.ds(start, rows), :]


def gather_vectors(pieces, rows, slots, vectors):
    for r, piece in enumerate(pieces):
        block = piece[(slots - 1) * rows :, :256].astype(F32)
        for a in range(slots):
            z = lax.rem(lax.axis_index("head") + slots - a, slots)
            source = own_device(r % 2, r // 2, slots) + z
            for i in range(2):
                part = block[a : a + 1, 128 * i : 128 * (i + 1)]
                vectors[pl.ds(source, 1), i : i + 1, :] = part[None]


def forward_kernel(count, slots, tokens_ref, own_ref, *refs):
    pieces, refs = refs[:count], refs[count:]
    if count == 1:
        given, refs = refs[0], refs[1:]
    normed_ref, rows_ref, residual_ref, second_ref, mark, heads_ref, weight = refs[:7]
    keep, staged, vectors = refs[7:-2], refs[-2], refs[-1]
    slot = pl.program_id(0)
    length, width = tokens_ref.shape
    share = width // vectors.shape[0]
    tiles = [slice(r, r + 256) for r in range(0, length, 256)]

    @pl.when(slot == 0)
    def _():
        if count == 1:
            vectors[...] = given[:, :8, :].astype(F32)
        else:
            gather_vectors(pieces, weight.shape[0] // count, slots, vectors)
        for i in range(9):
            part = low(vectors[:, 0 if i < 5 else 1, :])
            rows_ref[i : i + 1, :] = spread(part, (i if i < 5 else i - 5) * share, share, width)
        gain, shift = rows_ref[0:1, :], rows_ref[1:2, :]
        for rows in tiles:
            tokens = tokens_ref[rows, :].astype(F32)
            normal, _ = norm_parts(tokens)
            normed_ref[rows, :] = low(normal * gain + shift)
            residual_ref[rows, :] = tokens
        mark[0] = 1.0

    fill(weight, own_ref, pieces, slot)
    attend_forward(normed_ref, weight[:width, :], list(keep) + [staged])
    heads_ref[...] = staged[...]
    residual_ref[...] += nn(staged[...], weight[width:, :])

    @pl.when(slot == slots - 1)
    def _():
        gain, shift = rows_ref[2:3, :], rows_ref[3:4, :]
        for rows in tiles:
            normal, _ = norm_parts(residual_ref[rows, :])
            second_ref[rows, :] = low(normal * gain + shift)


def forward(tokens, own, pieces, vectors, devices, slots):
    length, width = tokens.shape
    shape = jax.ShapeDtypeStruct
    operands = [tokens, own, *pieces, *vectors]
    outs = [
        shape((length, width), BF16),
        shape((16, width), F32),
        shape((length, width), F32),
        shape((length, width), BF16),
    ]
    stacked_outs = [shape((slots, length, PAIR), BF16), pltpu.HBM((slots, width + PAIR, 4 * PAIR), BF16)]
    stacked_outs += kept_shapes(length, (slots,))
    made = pl.pallas_call(
        functools.partial(forward_kernel, len(pieces), slots),
        grid=(slots,),
        out_shape=outs + [MARK] + stacked_outs,
        in_specs=[fixed(o.shape) for o in operands],
        out_specs=[fixed(o.shape) for o in outs] + [mark_spec()] + by_step(stacked_outs),
        scratch_shapes=[pltpu.VMEM((length, PAIR), BF16), pltpu.VMEM((devices, 8, 128), F32)],
        compiler_params=params(44),
        cost_estimate=cost(17),
        name="attend_forward",
    )(*operands)
    return made[:5], made[5:]


GELU_A = 0.7978845608028654
GELU_B = 0.044715


def gelu_both(u):
    square = u * u
    half = 0.5 + 0.5 * jnp.tanh(u * (GELU_A + GELU_A * GELU_B * square))
    value = u * half
    return value, half + value * (1.0 - half) * (2.0 * GELU_A + 6.0 * GELU_A * GELU_B * square)


def weight_copies(block, pieces, weights, sems):
    if len(pieces) == 1:
        return [pltpu.make_async_copy(pieces[0].at[block], weights.at[block], sems.at[block, 0])]
    copies = []
    for r, piece in enumerate(pieces):
        slots = piece.shape[0]
        copies.append(
            pltpu.make_async_copy(
                piece.at[:, pl.ds(2 * block, 2)],
                weights.at[block, pl.ds(own_device(r % 2, r // 2, slots), slots)],
                sems.at[block, len(copies)],
            )
        )
    return copies


def grad_copies(block, grads, outs, sems):
    if len(outs) == 1:
        return [pltpu.make_async_copy(grads.at[block], outs[0].at[block], sems.at[block, 0])]
    copies = []
    for core, out in enumerate(outs):
        chips, slots = out.shape[:2]
        for chip in range(chips):
            target = (2 * chip + ((lax.axis_index("seq") & 1) ^ core)) * slots
            copies.append(
                pltpu.make_async_copy(
                    grads.at[block, pl.ds(target, slots)],
                    out.at[chip, :, block],
                    sems.at[block, len(copies)],
                )
            )
    return copies


def ffn_kernel(count, second_ref, rows_ref, cotangent_hbm, *refs):
    pieces = refs[:count]
    total, back, sums_ref = refs[count : count + 3]
    outs = refs[count + 3 : -6]
    weights, grads, cotangent_ref, in_sems, out_sems, cotangent_sems = refs[-6:]
    k = pl.program_id(0)
    length, width = second_ref.shape
    tiles = [slice(r, r + 256) for r in range(0, length, 256)]

    def arrive(rows):
        return pltpu.make_async_copy(
            cotangent_hbm.at[rows, :], cotangent_ref.at[rows, :], cotangent_sems.at[rows.start // 256]
        )

    @pl.when(k == 0)
    def _():
        for copy in weight_copies(0, pieces, weights, in_sems):
            copy.start()
        for rows in tiles:
            arrive(rows).start()
        for block in range(1, 4):
            for copy in weight_copies(block, pieces, weights, in_sems):
                copy.start()
        total[...] = jnp.zeros_like(total)
        back[...] = jnp.zeros_like(back)

    for block in range(4):

        @pl.when(k == block)
        def _(block=block):
            for copy in weight_copies(block, pieces, weights, in_sems):
                copy.wait()
            if block == 0:
                for rows in tiles:
                    arrive(rows).wait()

    expand = weights[k, :, 0].reshape(width, width)
    shrink = weights[k, :, 1].reshape(width, width)
    bias = rows_ref[pl.ds(5 + k, 1), :]
    bias_grad = jnp.zeros((1, width), F32)
    acts, hids = [], []
    for rows in tiles:
        hidden = nt(second_ref[rows, :], expand) + bias
        pull = nn(cotangent_ref[rows, :], shrink)
        value, slope = gelu_both(hidden)
        activated = low(value)
        hidden_grad = low(pull * slope)
        bias_grad = bias_grad + jnp.sum(hidden_grad.astype(F32), axis=0, keepdims=True)
        total[rows, :] += nt(activated, shrink)
        back[rows, :] += nn(hidden_grad, expand)
        acts.append(activated)
        hids.append(hidden_grad)
    sums_ref[pl.ds(5 + k, 1), :] = bias_grad
    grads[k, :, 1] = low(tn(cotangent_ref[...], jnp.concatenate(acts, axis=0))).reshape(
        width // 16, 16, width
    )
    grads[k, :, 0] = low(tn(jnp.concatenate(hids, axis=0), second_ref[...])).reshape(width // 16, 16, width)
    for block in range(4):

        @pl.when(k == block)
        def _(block=block):
            for copy in grad_copies(block, grads, outs, out_sems):
                copy.start()

    @pl.when(k == 3)
    def _():
        for block in range(4):
            for copy in grad_copies(block, grads, outs, out_sems):
                copy.wait()


def feed_forward(second, rows, cotangent, pieces, grad_shapes):
    length, width = second.shape
    shape = jax.ShapeDtypeStruct
    weights = (4, width // 16, 2, 16, width)
    outs = [shape((length, width), F32), shape((length, width), F32), shape((16, width), F32)]
    return pl.pallas_call(
        functools.partial(ffn_kernel, len(pieces)),
        grid=(4,),
        out_shape=outs + [shape(s, BF16) for s in grad_shapes],
        in_specs=[fixed(o.shape) for o in (second, rows)]
        + [pl.BlockSpec(memory_space=pltpu.HBM)] * (1 + len(pieces)),
        out_specs=[fixed(o.shape) for o in outs] + anywhere(grad_shapes),
        scratch_shapes=[
            pltpu.VMEM(weights, BF16),
            pltpu.VMEM(weights, BF16),
            pltpu.VMEM((length, width), BF16),
            pltpu.SemaphoreType.DMA((4, 8)),
            pltpu.SemaphoreType.DMA((4, 8)),
            pltpu.SemaphoreType.DMA((length // 256,)),
        ],
        compiler_params=params(36),
        cost_estimate=cost(21),
        name="feed_forward",
    )(second, rows, cotangent, *pieces)


def heads_kernel(total_ref, back_ref, residual_ref, rows_ref, cotangent_ref, sums_in, weight_ref, heads_ref,
                 result_ref, branch, sums_ref, grad_ref, *refs):
    slots = heads_ref.shape[0]
    outs, staged = refs[:-1], refs[-1]
    length, width = total_ref.shape
    gain, bias = rows_ref[2:3, :], rows_ref[4:5, :]
    gain_grad = jnp.zeros((1, width), F32)
    shift_grad = jnp.zeros((1, width), F32)
    outer = jnp.zeros((1, width), F32)
    for rows in [slice(r, r + 256) for r in range(0, length, 256)]:
        base = residual_ref[rows, :]
        result_ref[rows, :] = low(base + total_ref[rows, :] + bias)
        grad = back_ref[rows, :]
        normal, rate = norm_parts(base)
        upstream = cotangent_ref[rows, :].astype(F32)
        gain_grad = gain_grad + jnp.sum(grad * normal, axis=0, keepdims=True)
        shift_grad = shift_grad + jnp.sum(grad, axis=0, keepdims=True)
        outer = outer + jnp.sum(upstream, axis=0, keepdims=True)
        branch[rows, :] = low(upstream + norm_back(grad, normal, rate, gain))
    sums_ref[...] = sums_in[...]
    sums_ref[2:3, :] = gain_grad
    sums_ref[3:4, :] = shift_grad
    sums_ref[4:5, :] = outer
    weight = weight_ref[...].reshape(slots * PAIR, width)
    grad = low(nt(branch[...], weight))
    heads = jnp.concatenate([heads_ref[a] for a in range(slots)], axis=1)
    staged[...] = low(tn(branch[...], heads))
    for a in range(slots):
        grad_ref[a] = grad[:, a * PAIR : (a + 1) * PAIR]
    if len(outs) == 1:
        outs[0][...] = staged[...]
        return
    seq, z = lax.axis_index("seq"), lax.axis_index("head")
    chips = outs[0].shape[0]
    for core, out in enumerate(outs):
        for chip in range(chips):
            start = pl.multiple_of((2 * chip + ((seq & 1) ^ core)) * 64, 64)
            for there in range(slots):
                slot = lax.rem(z + slots - there, slots)
                block = staged[pl.ds(start, 64), pl.ds(pl.multiple_of(slot * PAIR, PAIR), PAIR)]
                out[chip, there] = jnp.concatenate([block[16 * i : 16 * i + 16, :] for i in range(4)], axis=1)


def heads_back(total, back, residual, rows, cotangent, sums, weights, heads, grad_shapes):
    slots, length, pair = heads.shape
    width = total.shape[1]
    shape = jax.ShapeDtypeStruct
    operands = [total, back, residual, rows, cotangent, sums]
    outs = [
        shape((length, width), BF16),
        pltpu.HBM((length, width), BF16),
        pltpu.HBM(sums.shape, F32),
        pltpu.HBM((slots, length, pair), BF16),
    ]
    outs += [shape(s, BF16) for s in grad_shapes]
    return pl.pallas_call(
        heads_kernel,
        grid=(1,),
        out_shape=outs,
        in_specs=[fixed(o.shape) for o in operands]
        + [pl.BlockSpec((slots, pair, width), lambda a: (0, width // pair, 0)), fixed(heads.shape)],
        out_specs=[fixed(o.shape) for o in outs],
        scratch_shapes=[pltpu.VMEM((width, slots * pair), BF16)],
        compiler_params=params(28),
        cost_estimate=cost(4),
        name="heads_back",
    )(*operands, weights, heads)


def leave_copies(slot, made, outs, sems):
    if len(outs) == 1:
        return [pltpu.make_async_copy(made, outs[0].at[slot], sems.at[0])]
    seq = lax.axis_index("seq")
    chips = outs[0].shape[0]
    rows = made.shape[0] // (2 * chips)
    copies = []
    for chip in range(chips):
        for core, out in enumerate((outs[0].at[chip], outs[1 + chip])):
            start = pl.multiple_of((seq ^ (2 * chip + core)) * rows, rows)
            copies.append(
                pltpu.make_async_copy(
                    made.at[pl.ds(start, rows), :],
                    out.at[pl.ds(pl.multiple_of(slot * rows, rows), rows), :],
                    sems.at[len(copies)],
                )
            )
    return copies


def back_kernel(waits, parts_out, slots, rows_ref, before_ref, normed_hbm, tokens_hbm, residual_grad_hbm, *refs):
    refs = refs[waits:]
    weight, grad_ref, kept, refs = refs[0], refs[1], refs[2:11], refs[11:]
    input_grad_hbm, sums_ref, outs, mark = refs[0], refs[1], refs[2 : 2 + parts_out], refs[2 + parts_out]
    (backs, made, total, input_grad_ref, normed_ref, tokens, residual_grad, vector_blocks, sems, out_sems, tile_sems) = refs[3 + parts_out :]
    length, width = normed_ref.shape
    devices = sums_ref.shape[0]
    share = width // devices
    step, steps = pl.program_id(0), slots
    copies = [
        pltpu.make_async_copy(tokens_hbm, tokens, sems.at[0]),
        pltpu.make_async_copy(residual_grad_hbm, residual_grad, sems.at[1]),
    ]
    fetch = pltpu.make_async_copy(normed_hbm, normed_ref, tile_sems.at[length // 256])

    @pl.when(step == 0)
    def _():
        fetch.start()
        for copy in copies:
            copy.start()
        total[...] = jnp.zeros_like(total)
        mark[0] = 1.0

    parity = lax.rem(step, 2)

    @pl.when(step >= 2)
    def _():
        for copy in leave_copies(step - 2, made.at[parity], outs, out_sems.at[parity]):
            copy.wait()

    attend_backward(grad_ref, kept, backs)

    @pl.when(step == 0)
    def _():
        fetch.wait()

    made[parity] = low(tn(normed_ref[...], backs[...]))
    for copy in leave_copies(step, made.at[parity], outs, out_sems.at[parity]):
        copy.start()
    total[...] += nt(backs[...], weight[:width, :])

    @pl.when(step == steps - 1)
    def _():
        for copy in copies:
            copy.wait()
        gain = rows_ref[0:1, :]
        gain_grad = jnp.zeros((1, width), F32)
        shift_grad = jnp.zeros((1, width), F32)
        left = []
        for rows in [slice(r, r + 256) for r in range(0, length, 256)]:
            grad = total[rows, :]
            normal, rate = norm_parts(tokens[rows, :].astype(F32))
            gain_grad = gain_grad + jnp.sum(grad * normal, axis=0, keepdims=True)
            shift_grad = shift_grad + jnp.sum(grad, axis=0, keepdims=True)
            input_grad_ref[rows, :] = low(residual_grad[rows, :].astype(F32) + norm_back(grad, normal, rate, gain))
            left.append(
                pltpu.make_async_copy(
                    input_grad_ref.at[rows, :], input_grad_hbm.at[rows, :], tile_sems.at[rows.start // 256]
                )
            )
            left[-1].start()
        small = [gain_grad, shift_grad] + [before_ref[i : i + 1, :] for i in range(2, 5)]
        sums_ref[:, :128] = collect(small, devices, share)
        sums_ref[:, 128:] = collect([before_ref[i : i + 1, :] for i in range(5, 9)], devices, share)
        leaving = []
        if parts_out > 1:
            z, chips = lax.axis_index("head"), outs[0].shape[0]
            for chip in range(chips):
                for core, out in enumerate((outs[0].at[chip], outs[1 + chip])):
                    n = len(leaving)
                    rows = [
                        sums_ref[pl.ds(own_device(core, chip, steps) + lax.rem(z + steps - a, steps), 1), :]
                        for a in range(steps)
                    ]
                    block = jnp.concatenate(rows + [jnp.zeros((16 - steps, 256), F32)], axis=0)
                    vector_blocks[n] = vector_rows(block, made.shape[2])
                    leaving.append(
                        pltpu.make_async_copy(
                            vector_blocks.at[n], out.at[pl.ds(out.shape[0] - 16, 16), :], sems.at[2 + n]
                        )
                    )
        for copy in leaving:
            copy.start()
        for last in (steps - 2, steps - 1):
            for copy in leave_copies(last, made.at[last % 2], outs, out_sems.at[last % 2]):
                copy.wait()
        for copy in leaving + left:
            copy.wait()


def backward(normed, rows, before, tokens, residual_grad, devices, waits, members, grad_shapes):
    length, width = normed.shape
    slots = members[0].shape[0]
    shape = jax.ShapeDtypeStruct
    outs = [pltpu.HBM((length, width), BF16), shape((devices, 256), F32)]
    grads = [shape(s, BF16) for s in grad_shapes]
    large = [normed, tokens, residual_grad]
    return pl.pallas_call(
        functools.partial(back_kernel, len(waits), len(grad_shapes), slots),
        grid=(slots,),
        out_shape=outs + grads + [MARK],
        in_specs=[fixed(o.shape) for o in (rows, before)] + anywhere(large + waits) + by_step(members),
        out_specs=[pl.BlockSpec(memory_space=pltpu.HBM), fixed(outs[1].shape)] + anywhere(grads) + [mark_spec()],
        scratch_shapes=[
            pltpu.VMEM((length, 4 * PAIR), BF16),
            pltpu.VMEM((2, width, 4 * PAIR), BF16),
            pltpu.VMEM((length, width), F32),
            pltpu.VMEM((length, width), BF16),
        ]
        + [pltpu.VMEM((length, width), m.dtype) for m in large]
        + [
            pltpu.VMEM((8, 16, 4 * PAIR), BF16),
            pltpu.SemaphoreType.DMA((10,)),
            pltpu.SemaphoreType.DMA((2, 8)),
            pltpu.SemaphoreType.DMA((length // 256 + 1,)),
        ],
        compiler_params=params(),
        cost_estimate=cost(27),
        name="attend_back",
    )(rows, before, *large, *waits, *members)


def after(value, *others):
    return pl.pallas_call(
        lambda *refs: None,
        out_shape=jax.ShapeDtypeStruct(value.shape, value.dtype),
        in_specs=anywhere((value,) + others),
        out_specs=anywhere([value])[0],
        input_output_aliases={0: 0},
        name="after",
    )(value, *others)


def near_kernel(slots, block_ref, load_ref, *refs):
    came, (near_ref, loads_ref) = refs[: slots - 1], refs[slots - 1 :]
    rows = came[0].shape[0] - 16
    for a, piece in enumerate(came):
        near_ref[a * rows : (a + 1) * rows, :] = piece[:rows, :]
    lines = [block_ref[...].astype(F32)[0:1, :]]
    lines += [piece[rows:, :].astype(F32)[0:1, :] for piece in reversed(came)]
    lines += [jnp.zeros((16 - slots, block_ref.shape[1]), F32)]
    near_ref[(slots - 1) * rows :, :] = low(jnp.concatenate(lines, axis=0))
    for z in range(slots):
        loads_ref[z] = load_ref[...]


def join_near(block, load, came):
    shape = jax.ShapeDtypeStruct
    slots = len(came) + 1
    rows = came[0].shape[0] - 16
    operands = [block, load, *came]
    outs = [
        shape(((slots - 1) * rows + 16, block.shape[1]), BF16),
        shape((slots,) + load.shape, BF16),
    ]
    return pl.pallas_call(
        functools.partial(near_kernel, slots),
        grid=(1,),
        out_shape=outs,
        in_specs=[fixed(o.shape) for o in operands],
        out_specs=[fixed(o.shape) for o in outs],
        compiler_params=params(12),
        cost_estimate=cost(1),
        name="join_near",
    )(*operands)


def vector_values(block):
    return block[:, :256].astype(F32) + block[:, 256:512].astype(F32)


def vector_rows(values, width):
    high = low(values)
    return jnp.concatenate([high, low(values - high.astype(F32))], axis=1)


def halve_kernel(keep_ref, other_ref, keep_output_ref, other_output_ref, out_ref):
    slots, width = keep_ref.shape[1], keep_ref.shape[-1]
    for chip in range(keep_ref.shape[0]):
        out_ref[chip, :, :8] = low(add(keep_ref[chip], other_ref[chip])).reshape(slots, 8, 16, width)
        out_ref[chip, :, 8] = low(add(keep_output_ref[chip], other_output_ref[chip]))


def halves(shape):
    return pl.BlockSpec((shape[0] // 2,) + shape[1:], lambda a: (a,) + (0,) * (len(shape) - 1))


def halve(keep, other, keep_output, other_output):
    operands = [keep, other, keep_output, other_output]
    out = pltpu.HBM(keep.shape[:2] + (9, 16, keep.shape[-1]), BF16)
    return pl.pallas_call(
        halve_kernel,
        grid=(2,),
        out_shape=out,
        in_specs=[halves(o.shape) for o in operands],
        out_specs=halves(keep.shape[:2] + (9, 16, keep.shape[-1])),
        compiler_params=params(44),
        cost_estimate=cost(2),
        name="halve",
    )(*operands)


def join_kernel(chips, slots, ffn_ref, keep_hbm, *refs):
    others, ffn_outs, outs = refs[:chips], refs[chips : chips + slots], refs[chips + slots : -2]
    keep_ref, sems = refs[-2:]
    copies = [pltpu.make_async_copy(keep_hbm.at[c], keep_ref.at[c], sems.at[c]) for c in range(chips)]
    for copy in copies:
        copy.start()
    z = lax.axis_index("head")
    for a, out in enumerate(ffn_outs):
        place = lax.rem(z + a, slots)
        out[...] = low(add(*[ffn_ref[c, pl.ds(place, 1)][0] for c in range(chips)]))
    body = keep_ref.shape[1] - 16
    for chip, out in enumerate(outs):
        copies[chip].wait()
        out[:body, :] = low(add(keep_ref[chip, :body, :], others[chip][:body, :]))
        values = vector_values(keep_ref[chip, body:, :]) + vector_values(others[chip][body:, :])
        out[body:, :] = vector_rows(values, out.shape[1])


def join(ffn, keep, others):
    shape = jax.ShapeDtypeStruct
    chips, slots = ffn.shape[:2]
    operands = [ffn, pltpu.with_memory_space_constraint(keep, pltpu.HBM), *others]
    outs = [shape(ffn.shape[2:], BF16)] * slots + [shape(keep.shape[1:], BF16)] * chips
    made = pl.pallas_call(
        functools.partial(join_kernel, chips, slots),
        grid=(1,),
        out_shape=outs,
        in_specs=[fixed(ffn.shape), pl.BlockSpec(memory_space=pltpu.HBM)] + [fixed(o.shape) for o in others],
        out_specs=[fixed(o.shape) for o in outs],
        scratch_shapes=[pltpu.VMEM(keep.shape, BF16), pltpu.SemaphoreType.DMA((chips,))],
        compiler_params=params(44),
        cost_estimate=cost(3),
        name="join",
    )(*operands)
    return made[:slots], made[slots:]


def sum_plane_kernel(slots, pairs, mine_ref, vector_ref, sends, mark):
    rows = mine_ref.shape[0]
    values = functools.reduce(lambda x, y: x + y, [vector_values(p[slots * rows :, :]) for p in pairs])
    vector_ref[...] = values[:8, :]
    for a in range(slots):
        mine = add(*[p[a * rows : (a + 1) * rows, :] for p in pairs])
        if a == 0:
            mine_ref[...] = mine
        else:
            sends[a - 1][:rows, :] = low(mine)
            sends[a - 1][rows:, :] = vector_rows(jnp.broadcast_to(values[a : a + 1, :], (16, 256)), mine.shape[1])
    mark[0] = 1.0


def sum_plane(pairs, slots, waits):
    shape = jax.ShapeDtypeStruct
    rows, columns = (pairs[0].shape[0] - 16) // slots, pairs[0].shape[1]
    outs = [shape((rows, columns), F32), shape((8, 256), F32)]
    outs += [shape((rows + 16, columns), BF16)] * (slots - 1)

    def kernel(*refs):
        made = refs[len(pairs) + len(waits) :]
        sum_plane_kernel(slots, refs[: len(pairs)], made[0], made[1], made[2:-1], made[-1])

    return pl.pallas_call(
        kernel,
        grid=(1,),
        out_shape=outs + [MARK],
        in_specs=[fixed(p.shape) for p in pairs] + anywhere(waits),
        out_specs=[fixed(o.shape) for o in outs] + [mark_spec()],
        compiler_params=params(12),
        cost_estimate=cost(2),
        name="sum_plane",
    )(*pairs, *waits)


def settle_kernel(ffn, expand_ref, shrink_ref, output_ref):
    blocks, (_, share, width) = 4, ffn[0].shape
    total = add(*[f[...] for f in ffn])
    for i in range(width // PAIR):
        output_ref[i * share : (i + 1) * share, :] = total[8, :, i * PAIR : (i + 1) * PAIR]
    total = total[:8].reshape(blocks, 2, share, width)
    expand_ref[...] = total[:, 0].reshape(blocks * share, width).T
    for i in range(blocks):
        shrink_ref[:, i] = total[i, 1].T.reshape(width // share, share, share)


def settle(ffn, wait):
    shape = jax.ShapeDtypeStruct
    slots = len(ffn)
    blocks, (_, share, width) = 4, ffn[0].shape
    outs = [shape((width, blocks * share), F32), shape((width // share, blocks, share, share), F32)]
    outs += [shape((share * width // PAIR, PAIR), F32)]

    def kernel(*refs):
        settle_kernel(refs[:slots], *refs[slots + 1 :])

    return pl.pallas_call(
        kernel,
        grid=(1,),
        out_shape=outs,
        in_specs=[fixed(f.shape) for f in ffn] + anywhere([wait]),
        out_specs=[fixed(o.shape) for o in outs],
        compiler_params=params(12),
        cost_estimate=cost(3),
        name="settle",
    )(*ffn, wait)


def finish_kernel(share, hidden_share, mine_ref, sums_ref, *refs):
    came, parts, vectors = refs[:3], refs[3:7], refs[7:]
    rows = mine_ref.shape[0]
    total = add(mine_ref[...], *[c[:rows, :] for c in came])
    for i, part in enumerate(parts):
        part[...] = total[:, i * PAIR : (i + 1) * PAIR]
    values = add(sums_ref[0:1, :], *[vector_values(c[rows:, :])[0:1, :] for c in came])
    for i, vector in enumerate(vectors[:-1]):
        vector[...] = values[0, i * share : (i + 1) * share]
    vectors[-1][...] = values[0, 128 : 128 + hidden_share]


def finish(mine, sums, came, share, hidden_share):
    shape = jax.ShapeDtypeStruct
    operands = [mine, sums, *came]
    outs = [shape((mine.shape[0], PAIR), F32)] * 4 + [shape((share,), F32)] * 5 + [shape((hidden_share,), F32)]
    made = pl.pallas_call(
        functools.partial(finish_kernel, share, hidden_share),
        grid=(1,),
        out_shape=outs,
        in_specs=[fixed(o.shape) for o in operands],
        out_specs=[fixed(o.shape) for o in outs],
        compiler_params=params(12),
        cost_estimate=cost(1),
        name="finish",
    )(*operands)
    return made[:4], made[4:]


def flip(count, bit):
    return [(i, i ^ bit) for i in range(count)]


def turn(count, by):
    return [(i, (i + by) % count) for i in range(count)]


def add(*members):
    return functools.reduce(lambda a, b: a + b, [m.astype(F32) for m in members])


def to_mate(shares, seqs):
    return lax.ppermute(shares, "seq", flip(seqs, 1))


def over_chips(shares, chips, seqs):
    return [shares] + [lax.ppermute(shares, "seq", flip(seqs, 2 * r)) for r in range(1, chips)]


def over_cores(held, seqs):
    return [member for h in held for member in (h, to_mate(h, seqs))]


def to_chips(shares, seqs):
    plane = [list(range(core, seqs, 2)) for core in range(2)]
    return lax.all_to_all(shares, "seq", 0, 0, axis_index_groups=plane, tiled=True)


def from_chips(sends, seqs):
    return [lax.ppermute(m, "seq", flip(seqs, 2 * r + 2)) for r, m in enumerate(sends)]


def body(
    inputs,
    attn_gain,
    attn_shift,
    query_weight,
    key_weight,
    value_weight,
    control_weight,
    output_weight,
    ffn_gain,
    ffn_shift,
    expand_weight,
    expand_bias,
    shrink_weight,
    shrink_bias,
    cotangent,
):
    seqs, slots = lax.axis_size("seq"), lax.axis_size("head")
    devices = seqs * slots
    chips = seqs // 2
    width = inputs.shape[1]
    share = width // devices
    hidden_share = expand_weight.shape[1]
    z = lax.axis_index("head")
    direct = seqs == 8 and slots == 4 and share == 16 and hidden_share == 4 * share

    own = jnp.concatenate(
        [
            jnp.concatenate([query_weight, key_weight, value_weight, control_weight], axis=1),
            output_weight,
        ],
        axis=0,
    )
    places = [(attn_gain, 0), (attn_shift, 1), (ffn_gain, 2), (ffn_shift, 3), (shrink_bias, 4)]
    row = functools.reduce(
        lambda a, b: a + b,
        [jnp.pad(m, (i * share, width - (i + 1) * share)) for m, i in places]
        + [jnp.pad(expand_bias, (128, width - 128 - hidden_share))],
    )
    block = jnp.pad(row[None, :], ((0, 15), (0, 0)))
    expand_t = expand_weight.T.reshape(4, share, width)
    shrink_t = shrink_weight.reshape(devices, 4, share, share).transpose(1, 3, 0, 2).reshape(4, share, width)
    load = jnp.stack([expand_t, shrink_t], axis=1)
    if direct:
        rows = own.shape[0] // seqs
        piece = lax.dynamic_slice_in_dim(own, lax.axis_index("seq") * rows, rows, axis=0)
        piece = jnp.concatenate([piece, block], axis=0)
        came = [lax.ppermute(piece, "head", turn(slots, a)) for a in range(1, slots)]
        near, loads = join_near(block, load.reshape(8, share, width), came[::-1])
        pieces, vectors = over_cores(over_chips(near, chips, seqs), seqs), []
        load = lax.all_to_all(loads, "head", 0, 0, tiled=True)
        held = over_chips(load, chips, seqs)
        tall = (slots * width // seqs + 16, 4 * PAIR)
        output_shapes = [(chips, slots, 16, width)] * 2
        pair_shapes = [(chips,) + tall] + [tall] * chips
        ffn_shapes = [(chips, slots, 4, 2, 16, width)] * 2
    else:
        every = lax.all_gather(own, "head", axis=0, tiled=False)
        pieces = [jnp.concatenate([every[(z + slots - a) % slots] for a in range(1, slots)], axis=0)]
        block = jnp.concatenate([block[:1, :128], block[:1, 128:256], block[2:, :128]], axis=0)
        vectors = [lax.all_gather(block, ("seq", "head"), axis=0, tiled=False)]
        both = lax.all_gather(load, ("seq", "head"), axis=2, tiled=True)
        ffn_pieces = [both.reshape(4, 2, width // 16, 16, width).transpose(0, 2, 1, 3, 4)]
        pair_shapes = [(slots, width, 4 * PAIR)]
        output_shapes = [(width, slots * PAIR)]
        ffn_shapes = [ffn_pieces[0].shape]

    (normed, rows, residual, second, mark), (heads, weights, *members) = forward(
        inputs, own, pieces, vectors, devices, slots
    )
    if direct:
        ffn_pieces = over_cores(held[:-1] + [low(held[-1].astype(F32) * mark[0])], seqs)
    total, back, sums, *ffn_grads = feed_forward(second, rows, cotangent, ffn_pieces, ffn_shapes)
    result, branch, sums, heads_grad, *output_grads = heads_back(
        total, back, residual, rows, cotangent, sums, weights, heads, output_shapes
    )
    members = [weights, heads_grad, *members]
    waits = []
    if direct:
        ffn_mine = halve(ffn_grads[0], to_mate(ffn_grads[1], seqs), output_grads[0], to_mate(output_grads[1], seqs))
        waits = [ffn_mine]
    input_grad, sums, *pair_grads, _ = backward(
        normed, rows, sums, inputs, branch, devices, waits, members, pair_shapes
    )

    if direct:
        keep, *sends = pair_grads
        ffn, pairs = join(to_chips(ffn_mine, seqs), keep, [to_mate(m, seqs) for m in sends])
        ffn = [ffn[0]] + [lax.ppermute(ffn[a], "head", turn(slots, a)) for a in range(1, slots)]
        pairs = [pairs[0]] + from_chips(pairs[1:], seqs)
        mine, sums, *sends, wait = sum_plane(pairs, slots, ffn[1:])
        expand_grad, shrink_grad, output_part = settle(ffn, wait)
        came = [lax.ppermute(m, "head", turn(slots, slots - 1 - a)) for a, m in enumerate(sends)]
        parts, vector = finish(mine, sums, came[::-1], share, hidden_share)
        parts = [*parts, output_part]
    else:
        ffn_sum = lax.psum_scatter(
            ffn_grads[0].astype(F32).transpose(0, 2, 1, 3, 4).reshape(4, 2, width, width), ("seq", "head"), scatter_dimension=2, tiled=True
        )
        outputs = output_grads[0].reshape(width, slots, PAIR).transpose(1, 0, 2)
        every = jnp.concatenate([pair_grads[0], outputs], axis=2).astype(F32)
        every = jnp.stack([every[(z + slots - p) % slots] for p in range(slots)])
        pair_sum = lax.psum_scatter(every, "head", scatter_dimension=0, tiled=False)
        pair_sum = lax.psum_scatter(pair_sum, "seq", scatter_dimension=0, tiled=True)

        sums = jnp.sum(
            lax.all_to_all(sums.reshape(devices, 1, 256), ("seq", "head"), 0, 0, tiled=True), axis=(0, 1)
        )
        expand_grad = ffn_sum[:, 0].reshape(hidden_share, width).T
        shrink_grad = ffn_sum[:, 1].reshape(4, share, devices, share).transpose(2, 0, 3, 1)

        parts = [pair_sum[:, i * PAIR : (i + 1) * PAIR] for i in range(5)]
        vector = [sums[i * share : (i + 1) * share] for i in range(5)] + [sums[128 : 128 + hidden_share]]

    return (
        result,
        input_grad,
        vector[0],
        vector[1],
        *parts[:4],
        parts[4].T,
        vector[2],
        vector[3],
        expand_grad,
        vector[5],
        shrink_grad.reshape(devices * hidden_share, share),
        vector[4],
    )


def solution(mesh):
    placed = (
        P(("seq", "head"), None),
        P(("seq", "head")),
        P(("seq", "head")),
        P(None, "head"),
        P(None, "head"),
        P(None, "head"),
        P(None, "head"),
        P("head", None),
        P(("seq", "head")),
        P(("seq", "head")),
        P(None, ("seq", "head")),
        P(("seq", "head")),
        P(None, ("seq", "head")),
        P(("seq", "head")),
        P(("seq", "head"), None),
    )
    return jax.shard_map(
        body,
        mesh=mesh,
        in_specs=placed,
        out_specs=(
            P(("seq", "head"), None),
            P(("seq", "head"), None),
            P(("seq", "head")),
            P(("seq", "head")),
            P("seq", "head"),
            P("seq", "head"),
            P("seq", "head"),
            P("seq", "head"),
            P("head", "seq"),
            P(("seq", "head")),
            P(("seq", "head")),
            P(None, ("seq", "head")),
            P(("seq", "head")),
            P(None, ("seq", "head")),
            P(("seq", "head")),
        ),
        check_vma=False,
    )
```
